256 devices in a mesh: layer: 16 (over z, y_lo), dp: 16 (over x, y_hi, core).
Axes of the slice: x: 4, y: 4 (y_hi: 2, y_lo: 2; y = y_hi * 2 + y_lo), z: 8, core: 2. Of those that a mesh axis runs over, the one named last changes fastest.
Arguments:
- residual: bfloat16 [2, 2048, 3584], P(None, 'dp'), may hold values from -6 to 6
- cotangent: bfloat16 [2, 2048, 3584], P(None, 'dp'), may hold values from -6 to 6
- decoder_first: bfloat16 [8192, 2, 3584], P('layer', None, 'dp'), may hold values from -0.09375 to 0.09375
- decoder_second: bfloat16 [8192, 3584], P('layer', 'dp'), may hold values from -0.09375 to 0.09375
- latent_index: int32 [2, 2048, 64], P(None, 'dp'), may hold values from 0 to 8191, all different within a row
- latent_value: bfloat16 [2, 2048, 64], P(None, 'dp'), may hold values from 0.25 to 3
- active_count: int32 [2, 2048], P(None, 'dp'), may hold values from 8 to 64
Outputs:
- decoder_first_grad: bfloat16 [8192, 2, 3584], P('layer', None, 'dp')
- decoder_second_grad: bfloat16 [8192, 3584], P('layer', 'dp')
- encoder_grad: bfloat16 [3584, 2, 8192], P('dp', None, 'layer')
- latent_grad: float32 [2, 2048, 64], P(None, 'dp')
The draws below stay inside these ranges and needn't reach their ends.
Inputs may be any that keep to these rules, and one draw needn't show every extreme that they name: `latent_index`: the 64 slots of a token and layer name distinct latents of that layer; slots at or past active_count are padding.
All inputs are finite; a program needn't handle non-finite values.
Results may differ from the reference program's by a relative error of at most 0.02.
Values may be sent and summed in bfloat16 or wider, within the bound.
No kernel may reach another device: no remote copies, remote signals or barrier semaphores. Data moves between devices by JAX's collectives and lax.ppermute only.
A program may use at most 128 MiB of HBM per device.

```python
import math
import jax
import jax.numpy as jnp
from jax import lax

D = 3584
LAYERS = 2
K = 64
TOK_DEV = 128
F = 8192
TOKENS = 2048
N_DP = 16


def set_ends(array, own_key, least, largest):
    spot = [jax.random.randint(jax.random.fold_in(own_key, axis), (), 0, length) for axis, length in enumerate(array.shape)]
    longest = array.shape.index(max(array.shape))
    neighbour = spot[:longest] + [(spot[longest] + 1) % array.shape[longest]] + spot[longest + 1:]
    return array.at[tuple(spot)].set(least).at[tuple(neighbour)].set(largest)


def raised(values, own_key, source, target, blocks, factor):
    owner, partner = [(jnp.arange(values.shape[dim]) // (values.shape[dim] // blocks)).reshape([-1 if axis == dim else 1 for axis in range(values.ndim)]) for dim in (source, target)]
    chosen = jax.random.permutation(own_key, blocks)[partner]
    strong = (owner == chosen) | (owner == (partner + blocks // 2) % blocks)
    return jnp.where(strong, factor * values, values)


def shard_levels(own_key, shape, shards, smallest, high):
    gain = 1.0
    for axis_at, parts in shards:
        heights = jax.random.uniform(jax.random.fold_in(jax.random.fold_in(own_key, 6), axis_at), (parts,), jnp.float32, smallest / len(shards), high / len(shards))
        gain = gain * jnp.repeat(jnp.exp(heights), shape[axis_at] // parts).reshape((-1,) + (1,) * (len(shape) - 1 - axis_at))
    return gain


def choose_distinct(rng, rows, count, top, lift):
    order = jax.random.permutation(jax.random.fold_in(rng, 1), count)
    favour = order
    for power in range(3):
        favour = favour * favour // count
    favour = favour * lift // count
    chance = jax.random.randint(jax.random.fold_in(rng, 2), (rows, count), 0, 4096) + favour
    holders = jax.random.permutation(jax.random.fold_in(rng, 3), rows)[jnp.arange(count) % rows]
    chance = jnp.where(jnp.arange(rows)[:, None] == holders[None, :], 1 << 14, chance)
    score = chance * count + jnp.arange(count)
    return lax.top_k(score.astype(jnp.int32), top)[1].astype(jnp.int32)


def bell_draw(stream_key, dims, spread, reach, pieces=(), dtype=jnp.bfloat16):
    result = jax.random.normal(stream_key, dims, jnp.float32) * spread
    if len(pieces) > 0:
        result = shard_levels(stream_key, dims, pieces, -0.22, 0.18) * result
    return jnp.clip(result, min=-reach, max=reach).astype(dtype)


def noise_with(stream_key, dims, spread, reach, shards, heavy, dtype=jnp.bfloat16):
    result = spread * jax.random.normal(stream_key, dims, jnp.float32)
    if shards:
        result = result * shard_levels(stream_key, dims, shards, -0.22, 0.18)
    return jnp.clip(raised(result, jax.random.fold_in(stream_key, 3), *heavy), -reach, reach).astype(dtype)


def setup_inputs(seed: int = 0) -> dict:
    key_list = jax.random.split(jax.random.key(seed), 8)
    residual = noise_with(key_list[0], (LAYERS, TOKENS, D), 1.0, 6.0, ((1, 16),), (1, 2, 16, 2.0))
    cotangent = noise_with(key_list[1], (LAYERS, TOKENS, D), 1.0, 6.0, ((1, 16),), (1, 2, 16, 2.0))
    decoder_first = bell_draw(key_list[2], (F, LAYERS, D), D ** -0.5, 0.09375, ((0, 16), (2, 16)))
    decoder_second = bell_draw(key_list[3], (F, D), D ** -0.5, 0.09375, ((0, 16), (1, 16)))
    latent_index = choose_distinct(key_list[4], LAYERS * TOKENS, F, K, 64).reshape((LAYERS, TOKENS, K))
    latent_value = jnp.clip(jnp.exp(math.log(3.0) - 2.4849066 * jax.random.uniform(key_list[5], (LAYERS, TOKENS, K), jnp.float32) ** shard_levels(key_list[5], (LAYERS, TOKENS, K), ((1, 16),), -0.2, 0.2)), 0.25, 3.0).astype(jnp.bfloat16)
    active_count = set_ends(jax.random.randint(key_list[6], (LAYERS, TOKENS), K // 8, K + 1), jax.random.fold_in(key_list[6], 1), K // 8, K).astype(jnp.int32)
    return dict(residual=residual, cotangent=cotangent, decoder_first=decoder_first, decoder_second=decoder_second, latent_index=latent_index, latent_value=latent_value, active_count=active_count)


def dense_codes(latent_ids, latent_vals, live_count, lat_width):
    row_count = latent_ids.shape[0]
    slot_count = latent_ids.shape[1]
    is_live = jnp.arange(slot_count)[None, :] < live_count[:, None]
    live_values = jnp.where(is_live, latent_vals.astype(jnp.float32), jnp.float32(0.0))
    holder = jnp.zeros((row_count, lat_width), jnp.float32)
    filled = holder.at[jnp.arange(row_count)[:, None], latent_ids].add(live_values)
    return filled.astype(jnp.bfloat16)


def rounded(partial_value):
    return lax.optimization_barrier(partial_value.astype(jnp.bfloat16)).astype(jnp.float32)


def contract_last(left_side, right_side):
    return lax.dot_general(left_side, right_side, (((1,), (1,)), ((), ())), preferred_element_type=jnp.float32)


def reference(residual, cotangent, decoder_first, decoder_second, latent_index, latent_value, active_count):
    lat_width = decoder_first.shape[0]
    model_width = residual.shape[2]
    slot_count = latent_index.shape[2]
    first_grads = contract_last(cotangent[0], decoder_first[:, 0, :]) + contract_last(cotangent[1], decoder_first[:, 1, :])
    second_grads = contract_last(cotangent[1], decoder_second)
    is_live = jnp.arange(slot_count)[None, None, :] < active_count[:, :, None]
    chosen_first = jnp.take_along_axis(first_grads, latent_index[0], axis=1)
    chosen_second = jnp.take_along_axis(second_grads, latent_index[1], axis=1)
    latent_grad = jnp.where(is_live, jnp.stack([chosen_first, chosen_second]), jnp.float32(0.0))
    grad_codes = latent_grad.astype(jnp.bfloat16)
    dec_first = jnp.zeros((lat_width, 2, model_width), jnp.float32)
    dec_second = jnp.zeros((lat_width, model_width), jnp.float32)
    encoder_sum = jnp.zeros((model_width, 2, lat_width), jnp.float32)
    for shard_num in range(N_DP):
        row_low = shard_num * TOK_DEV
        row_high = row_low + TOK_DEV
        ids_block = latent_index[:, row_low:row_high]
        vals_block = latent_value[:, row_low:row_high]
        live_block = active_count[:, row_low:row_high]
        codes_first = dense_codes(ids_block[0], vals_block[0], live_block[0], lat_width).astype(jnp.float32)
        codes_second = dense_codes(ids_block[1], vals_block[1], live_block[1], lat_width).astype(jnp.float32)
        cot_block = cotangent[:, row_low:row_high].astype(jnp.float32)
        dec_first = dec_first + rounded(jnp.einsum("tr,atd->rad", codes_first, cot_block))
        dec_second = dec_second + rounded(jnp.einsum("tr,td->rd", codes_second, cot_block[1]))
        back_first = dense_codes(ids_block[0], grad_codes[0, row_low:row_high], live_block[0], lat_width).astype(jnp.float32)
        back_second = dense_codes(ids_block[1], grad_codes[1, row_low:row_high], live_block[1], lat_width).astype(jnp.float32)
        res_block = residual[:, row_low:row_high].astype(jnp.float32)
        encoder_sum = encoder_sum + rounded(jnp.einsum("atd,atr->dar", res_block, jnp.stack([back_first, back_second])))
    return dec_first.astype(jnp.bfloat16), dec_second.astype(jnp.bfloat16), encoder_sum.astype(jnp.bfloat16), latent_grad
```

```python
import functools
import jax
import jax.numpy as jnp
from jax import lax
from jax.experimental import pallas as pl
from jax.experimental.pallas import tpu as pltpu
from jax.sharding import PartitionSpec as P

BF16 = jnp.bfloat16
F32 = jnp.float32
LANES = 128
SHIFT = 256
EMPTY = 512


def grant(mib):
    return pltpu.CompilerParams(vmem_limit_bytes=mib << 20)


def cost(flops, moved):
    return pl.CostEstimate(flops=flops, bytes_accessed=moved, transcendentals=0)


def lane_pick(table, where):
    return jnp.take_along_axis(table, where, axis=1, mode="promise_in_bounds")


def pack_kernel(lat_width, start_ref, cot_ref, res_ref, idx_ref, val_ref, live_ref, out_ref, rank_ref, slot_ref):
    slots, tokens = idx_ref.shape[1:]
    dests = out_ref.shape[0]
    cols = cot_ref.shape[2] // dests

    @pl.when(pl.program_id(0) == 0)
    def _():
        start = start_ref[0]
        place = lax.broadcasted_iota(jnp.int32, (slots, tokens), 0)
        found, values = [], []
        for layer in range(2):
            local = idx_ref[layer] - start
            inside = (place < live_ref[layer : layer + 1, :]) & (local >= 0) & (local < lat_width)
            key = jnp.where(inside, local, 1 << 20)
            rank = jnp.zeros((slots, tokens), jnp.int32)
            for slot in range(slots):
                rank = rank + jnp.where(key[slot : slot + 1, :] < key, 1, 0)
            rank = jnp.where(inside, rank, slots)
            rank_ref[layer] = rank
            key = local - SHIFT
            value = val_ref[layer].astype(F32)
            held = jnp.full((slots, tokens), EMPTY, jnp.int32)
            code = jnp.zeros((slots, tokens), F32)
            for slot in range(slots):
                here = rank[slot : slot + 1, :] == place
                held = jnp.where(here, key[slot : slot + 1, :], held)
                code = jnp.where(here, value[slot : slot + 1, :], code)
            found.append(held.astype(F32))
            values.append(code)
        slot_ref[0:tokens, :] = jnp.concatenate(found, axis=0).T.astype(BF16)
        slot_ref[tokens : 2 * tokens, :] = jnp.concatenate(values, axis=0).T.astype(BF16)

    half = 2 * cols + tokens
    for source, base in ((cot_ref, 0), (res_ref, half + tokens)):
        for layer in range(2):
            turned = source[layer].T
            for dest in range(dests):
                out_ref[dest, base + layer * cols : base + (layer + 1) * cols, :] = turned[
                    dest * cols : (dest + 1) * cols
                ]
    for dest in range(dests):
        out_ref[dest, 2 * cols : half + tokens, :] = slot_ref[...]


def pack(start, cotangent, residual, index, value, live, lat_width, parts):
    _, tokens, width = cotangent.shape
    slots = index.shape[1]
    steps = 4
    cols = width // parts
    rows = 4 * cols + 2 * tokens
    return pl.pallas_call(
        functools.partial(pack_kernel, lat_width),
        grid=(steps,),
        in_specs=[
            pl.BlockSpec(memory_space=pltpu.SMEM),
            pl.BlockSpec((2, tokens, width // steps), lambda i: (0, 0, i)),
            pl.BlockSpec((2, tokens, width // steps), lambda i: (0, 0, i)),
            pl.BlockSpec((2, slots, tokens), lambda i: (0, 0, 0)),
            pl.BlockSpec((2, slots, tokens), lambda i: (0, 0, 0)),
            pl.BlockSpec((2, tokens), lambda i: (0, 0)),
        ],
        out_specs=[
            pl.BlockSpec((parts // steps, rows, tokens), lambda i: (i, 0, 0)),
            pl.BlockSpec((2, slots, tokens), lambda i: (0, 0, 0)),
        ],
        out_shape=[
            jax.ShapeDtypeStruct((parts, rows, tokens), BF16),
            jax.ShapeDtypeStruct((2, slots, tokens), jnp.int32),
        ],
        scratch_shapes=[pltpu.VMEM((2 * tokens, LANES), BF16)],
        compiler_params=grant(40),
        cost_estimate=cost(0, 10 << 20),
    )(start, cotangent, residual, index, value, live)


def terms_kernel(wf_ref, ws_ref, got_ref, out_ref, weight_ref):
    shards, _, tokens = got_ref.shape
    cols, lat_width = ws_ref.shape

    @pl.when(pl.program_id(0) == 0)
    def _():
        weight_ref[0:cols, 0:lat_width] = wf_ref[0]
        weight_ref[cols : 2 * cols, 0:lat_width] = wf_ref[1]
        weight_ref[0:cols, lat_width:] = jnp.zeros((cols, lat_width), BF16)
        weight_ref[cols : 2 * cols, lat_width:] = ws_ref[...]

    for shard in range(shards):
        dense = lax.dot_general(
            got_ref[shard, 0 : 2 * cols, :].T,
            weight_ref[...],
            (((1,), (0,)), ((), ())),
            preferred_element_type=F32,
        )
        held = got_ref[shard, 2 * cols : 2 * cols + tokens, :].astype(F32).astype(jnp.int32) + SHIFT
        lane = lax.broadcasted_iota(jnp.int32, held.shape, 1)
        chunks = lat_width // LANES
        chunk = jnp.where(
            held < lat_width, (held >> 7) + jnp.where(lane >= LANES // 2, chunks, 0), 2 * chunks
        )
        within = held & (LANES - 1)
        picked = jnp.zeros(held.shape, F32)
        for part in range(2 * chunks):
            table = dense[:, part * LANES : (part + 1) * LANES]
            picked = jnp.where(chunk == part, lane_pick(table, within), picked)
        out_ref[shard] = picked.astype(BF16)


def slot_terms(first, second, got):
    parts, rows, tokens = got.shape
    cols, lat_width = second.shape
    shards = 2
    return pl.pallas_call(
        terms_kernel,
        grid=(parts // shards,),
        in_specs=[
            pl.BlockSpec((2, cols, lat_width), lambda i: (0, 0, 0)),
            pl.BlockSpec((cols, lat_width), lambda i: (0, 0)),
            pl.BlockSpec((shards, rows // 2, tokens), lambda i: (i, 0, 0)),
        ],
        out_specs=pl.BlockSpec((shards, tokens, LANES), lambda i: (i, 0, 0)),
        out_shape=jax.ShapeDtypeStruct((parts, tokens, LANES), BF16),
        scratch_shapes=[pltpu.VMEM((2 * cols, 2 * lat_width), BF16)],
        compiler_params=grant(40),
        cost_estimate=cost(2 * parts * tokens * cols * 3 * lat_width, 6 << 20),
    )(first, second, got)


def total_kernel(got_ref, rank_ref, grad_ref, part_ref):
    total = jnp.sum(got_ref[...].astype(F32), axis=0)
    for dest in range(grad_ref.shape[0]):
        grad_ref[dest] = total.astype(BF16)
    turned = total.T
    slots = rank_ref.shape[1]
    for layer in range(2):
        rank = rank_ref[layer]
        part = jnp.zeros(rank.shape, F32)
        for slot in range(slots):
            row = layer * slots + slot
            part = jnp.where(rank == slot, turned[row : row + 1, :], part)
        part_ref[layer] = part.astype(BF16)


def slot_totals(got, rank):
    parts, tokens, _ = got.shape
    return pl.pallas_call(
        total_kernel,
        out_shape=[
            jax.ShapeDtypeStruct(got.shape, BF16),
            jax.ShapeDtypeStruct(rank.shape, BF16),
        ],
        compiler_params=grant(40),
        cost_estimate=cost(0, 1 << 20),
    )(got, rank)


def weights_kernel(low_ref, high_ref, grad_ref, first_ref, second_ref, enc_ref, code_ref, back_ref, sum_ref):
    shards, half, tokens = low_ref.shape
    cols, lat_width = second_ref.shape
    step = pl.program_id(0)
    block = 16
    steps = (32, 16, 8, 4, 2, 1)

    def spread(at, carry):
        shard = at // (tokens // block)
        low = pl.multiple_of((at % (tokens // block)) * block, block)
        held = low_ref[shard, pl.ds(2 * cols + low, block), :].astype(F32)
        value = high_ref[shard, pl.ds(low, block), :].astype(F32)
        grad = grad_ref[shard, pl.ds(low, block), :].astype(F32)
        row = pl.multiple_of(at * block, block)
        for layer in range(2):
            base = layer * (LANES // 2)
            for chunk in range(lat_width // LANES):
                column = (
                    lax.broadcasted_iota(jnp.int32, (block, LANES), 1) + (chunk * LANES - SHIFT)
                ).astype(F32)
                spot = jnp.full((block, LANES), base, jnp.int32)
                key = lane_pick(held, spot)
                for jump in steps:
                    next_spot = spot + jump
                    next_key = lane_pick(held, next_spot)
                    before = next_key <= column
                    spot = jnp.where(before, next_spot, spot)
                    key = jnp.where(before, next_key, key)
                hit = key == column
                at_col = layer * lat_width + chunk * LANES
                code_ref[pl.ds(row, block), at_col : at_col + LANES] = jnp.where(
                    hit, lane_pick(value, spot), 0.0
                ).astype(BF16)
                back_ref[pl.ds(row, block), at_col : at_col + LANES] = jnp.where(
                    hit, lane_pick(grad, spot), 0.0
                ).astype(BF16)
        return carry

    lax.fori_loop(0, shards * tokens // block, spread, 0)

    @pl.when(step == 0)
    def _():
        sum_ref[...] = jnp.zeros_like(sum_ref)

    cot = jnp.concatenate([low_ref[shard, 0 : 2 * cols, :] for shard in range(shards)], axis=1)
    res = jnp.concatenate([high_ref[shard, tokens : tokens + 2 * cols, :] for shard in range(shards)], axis=1)
    dot = functools.partial(jnp.dot, preferred_element_type=F32)
    sum_ref[0 : 2 * cols, :] += dot(cot, code_ref[:, 0:lat_width])
    sum_ref[2 * cols : 3 * cols, :] += dot(cot[cols:], code_ref[:, lat_width:])
    sum_ref[3 * cols : 4 * cols, :] += dot(res[0:cols], back_ref[:, 0:lat_width])
    sum_ref[4 * cols : 5 * cols, :] += dot(res[cols:], back_ref[:, lat_width:])

    @pl.when(step == pl.num_programs(0) - 1)
    def _():
        first_ref[0] = sum_ref[0:cols, :].astype(BF16)
        first_ref[1] = sum_ref[cols : 2 * cols, :].astype(BF16)
        second_ref[...] = sum_ref[2 * cols : 3 * cols, :].astype(BF16)
        enc_ref[0] = sum_ref[3 * cols : 4 * cols, :].astype(BF16)
        enc_ref[1] = sum_ref[4 * cols : 5 * cols, :].astype(BF16)


def weight_grads(got, grads, cols, lat_width):
    parts, rows, tokens = got.shape
    shards = 4
    return pl.pallas_call(
        weights_kernel,
        grid=(parts // shards,),
        in_specs=[
            pl.BlockSpec((shards, rows // 2, tokens), lambda i: (i, 0, 0)),
            pl.BlockSpec((shards, rows // 2, tokens), lambda i: (i, 1, 0)),
            pl.BlockSpec((shards, tokens, LANES), lambda i: (i, 0, 0)),
        ],
        out_specs=[
            pl.BlockSpec((2, cols, lat_width), lambda i: (0, 0, 0)),
            pl.BlockSpec((cols, lat_width), lambda i: (0, 0)),
            pl.BlockSpec((2, cols, lat_width), lambda i: (0, 0, 0)),
        ],
        out_shape=[
            jax.ShapeDtypeStruct((2, cols, lat_width), BF16),
            jax.ShapeDtypeStruct((cols, lat_width), BF16),
            jax.ShapeDtypeStruct((2, cols, lat_width), BF16),
        ],
        scratch_shapes=[
            pltpu.VMEM((shards * tokens, 2 * lat_width), BF16),
            pltpu.VMEM((shards * tokens, 2 * lat_width), BF16),
            pltpu.VMEM((5 * cols, lat_width), F32),
        ],
        compiler_params=grant(40),
        cost_estimate=cost(2 * parts * tokens * cols * 5 * lat_width, 8 << 20),
    )(got, got, grads)


def exchange(array, axis):
    return lax.all_to_all(array, axis, 0, 0, tiled=True)


def union(part, axis, size):
    reach = 1
    while reach < size:
        others = [
            lax.ppermute(part, axis, [(at, at ^ (reach * hop)) for at in range(size)])
            for hop in (1, 2, 3)
            if reach * hop < size
        ]
        for other in others:
            part = part + other
        reach *= 4
    return part


def shards(layers, parts, residual, cotangent, decoder_first, decoder_second, latent_index, latent_value, active_count):
    lat_width = decoder_first.shape[0]
    cols = decoder_second.shape[1]
    start = (lax.axis_index("layer") * lat_width).astype(jnp.int32).reshape(1)
    packed, rank = pack(
        start,
        cotangent,
        residual,
        latent_index.transpose(0, 2, 1),
        latent_value.transpose(0, 2, 1),
        active_count,
        lat_width,
        parts,
    )
    got = exchange(packed, "dp")
    terms = slot_terms(decoder_first.transpose(1, 2, 0), decoder_second.T, got)
    grads, part = slot_totals(exchange(terms, "dp"), rank)
    all_grads = exchange(grads, "dp")
    first_grad, second_grad, encoder_grad = weight_grads(got, all_grads, cols, lat_width)
    latent_grad = union(part, "layer", layers)
    return (
        first_grad.transpose(2, 0, 1),
        second_grad.T,
        encoder_grad.transpose(1, 0, 2),
        latent_grad.astype(F32).transpose(0, 2, 1),
    )


def solution(mesh):
    return jax.shard_map(
        functools.partial(shards, mesh.shape["layer"], mesh.shape["dp"]),
        mesh=mesh,
        in_specs=(
            P(None, "dp", None),
            P(None, "dp", None),
            P("layer", None, "dp"),
            P("layer", "dp"),
            P(None, "dp", None),
            P(None, "dp", None),
            P(None, "dp"),
        ),
        out_specs=(
            P("layer", None, "dp"),
            P("layer", "dp"),
            P("dp", None, "layer"),
            P(None, "dp", None),
        ),
        check_vma=False,
    )
```

```python
import functools
import jax
import jax.numpy as jnp
from jax import lax
from jax.experimental import pallas as pl
from jax.experimental.pallas import tpu as pltpu
from jax.sharding import PartitionSpec as P

BF16 = jnp.bfloat16
F32 = jnp.float32
LANES = 128
SHIFT = 256
EMPTY = 512
PACK_MIB = 60


def grant(mib):
    return pltpu.CompilerParams(vmem_limit_bytes=mib << 20)


def cost(flops, moved):
    return pl.CostEstimate(flops=flops, bytes_accessed=moved, transcendentals=0)


def lane_pick(table, where):
    return jnp.take_along_axis(table, where, axis=1, mode="promise_in_bounds")


def turn(source_ref, out_ref, layer, base):
    dests = out_ref.shape[0]
    cols = source_ref.shape[2] // dests
    turned = source_ref[layer].T
    for dest in range(dests):
        out_ref[dest, base + layer * cols : base + (layer + 1) * cols, :] = turned[dest * cols : (dest + 1) * cols]


def kept_slots(start_ref, idx_ref, live_ref, layer, lat_width):
    slots, tokens = idx_ref.shape[1:]
    place = lax.broadcasted_iota(jnp.int32, (slots, tokens), 0)
    local = idx_ref[layer] - start_ref[0]
    inside = (place < live_ref[layer : layer + 1, :]) & (local >= 0) & (local < lat_width)
    return place, local, inside


def pack_first_kernel(lat_width, start_ref, cot_ref, idx_ref, live_ref, out_ref, rank_ref, slot_ref):
    slots, tokens = idx_ref.shape[1:]
    dests = out_ref.shape[0]
    cols = cot_ref.shape[2] // dests

    @pl.when(pl.program_id(0) == 0)
    def _():
        found = []
        for layer in range(2):
            place, local, inside = kept_slots(start_ref, idx_ref, live_ref, layer, lat_width)
            key = jnp.where(inside, local, 1 << 20)
            rank = jnp.zeros((slots, tokens), jnp.int32)
            for slot in range(slots):
                rank = rank + jnp.where(key[slot : slot + 1, :] < key, 1, 0)
            rank = jnp.where(inside, rank, slots)
            rank_ref[layer] = rank
            key = local - SHIFT
            held = jnp.full((slots, tokens), EMPTY, jnp.int32)
            for slot in range(slots):
                held = jnp.where(rank[slot : slot + 1, :] == place, key[slot : slot + 1, :], held)
            found.append(held.astype(F32))
        slot_ref[...] = jnp.concatenate(found, axis=0).T.astype(BF16)

    for layer in range(2):
        turn(cot_ref, out_ref, layer, 0)
    for dest in range(dests):
        out_ref[dest, 2 * cols :, :] = slot_ref[...]


def pack_second_kernel(lat_width, start_ref, res_ref, idx_ref, val_ref, live_ref, rank_ref, out_ref, slot_ref):
    slots, tokens = idx_ref.shape[1:]
    dests = out_ref.shape[0]

    @pl.when(pl.program_id(0) == 0)
    def _():
        codes, runs = [], []
        for layer in range(2):
            place, local, inside = kept_slots(start_ref, idx_ref, live_ref, layer, lat_width)
            rank = rank_ref[layer]
            value = val_ref[layer].astype(F32)
            run = jnp.where(inside, local >> 3, lat_width)
            bit = jnp.left_shift(1, local & 7)
            code = jnp.zeros((slots, tokens), F32)
            bits = jnp.zeros((slots, tokens), jnp.int32)
            for slot in range(slots):
                code = jnp.where(rank[slot : slot + 1, :] == place, value[slot : slot + 1, :], code)
                bits = bits + jnp.where(run[slot : slot + 1, :] == place, bit[slot : slot + 1, :], 0)
            codes.append(code)
            runs.append(bits.astype(F32))
        slot_ref[0:tokens, :] = jnp.concatenate(codes, axis=0).T.astype(BF16)
        slot_ref[tokens:, :] = jnp.concatenate(runs, axis=0).T.astype(BF16)

    for layer in range(2):
        turn(res_ref, out_ref, layer, 2 * tokens)
    for dest in range(dests):
        out_ref[dest, 0 : 2 * tokens, :] = slot_ref[...]


def pack(kernel, lat_width, parts, more, start, wide, *small):
    _, tokens, width = wide.shape
    steps = 4
    rows = 2 * (width // parts) + more * tokens
    out_specs = [pl.BlockSpec((parts // steps, rows, tokens), lambda i: (i, 0, 0))]
    out_shape = [jax.ShapeDtypeStruct((parts, rows, tokens), BF16)]
    if more == 1:
        out_specs.append(pl.BlockSpec(small[0].shape, lambda i: (0, 0, 0)))
        out_shape.append(jax.ShapeDtypeStruct(small[0].shape, jnp.int32))
    return pl.pallas_call(
        functools.partial(kernel, lat_width),
        grid=(steps,),
        in_specs=[
            pl.BlockSpec(memory_space=pltpu.SMEM),
            pl.BlockSpec((2, tokens, width // steps), lambda i: (0, 0, i)),
        ]
        + [pl.BlockSpec(array.shape, lambda i, rank=array.ndim: (0,) * rank) for array in small],
        out_specs=out_specs,
        out_shape=out_shape,
        scratch_shapes=[pltpu.VMEM((more * tokens, LANES), BF16)],
        compiler_params=grant(PACK_MIB),
        cost_estimate=cost(0, 5 << 20),
    )(start, wide, *small)


def terms_kernel(wf_ref, ws_ref, got_ref, out_ref, weight_ref):
    shards, _, tokens = got_ref.shape
    cols, lat_width = ws_ref.shape

    @pl.when(pl.program_id(0) == 0)
    def _():
        weight_ref[0:cols, 0:lat_width] = wf_ref[0]
        weight_ref[cols : 2 * cols, 0:lat_width] = wf_ref[1]
        weight_ref[0:cols, lat_width:] = jnp.zeros((cols, lat_width), BF16)
        weight_ref[cols : 2 * cols, lat_width:] = ws_ref[...]

    for shard in range(shards):
        dense = lax.dot_general(
            got_ref[shard, 0 : 2 * cols, :].T,
            weight_ref[...],
            (((1,), (0,)), ((), ())),
            preferred_element_type=F32,
        )
        held = got_ref[shard, 2 * cols : 2 * cols + tokens, :].astype(F32).astype(jnp.int32) + SHIFT
        lane = lax.broadcasted_iota(jnp.int32, held.shape, 1)
        chunks = lat_width // LANES
        chunk = jnp.where(
            held < lat_width, (held >> 7) + jnp.where(lane >= LANES // 2, chunks, 0), 2 * chunks
        )
        within = held & (LANES - 1)
        picked = jnp.zeros(held.shape, F32)
        for part in range(2 * chunks):
            table = dense[:, part * LANES : (part + 1) * LANES]
            picked = jnp.where(chunk == part, lane_pick(table, within), picked)
        out_ref[shard] = picked.astype(BF16)


def slot_terms(first, second, got):
    parts, rows, tokens = got.shape
    cols, lat_width = second.shape
    shards = 2
    return pl.pallas_call(
        terms_kernel,
        grid=(parts // shards,),
        in_specs=[
            pl.BlockSpec((2, cols, lat_width), lambda i: (0, 0, 0)),
            pl.BlockSpec((cols, lat_width), lambda i: (0, 0)),
            pl.BlockSpec((shards, rows, tokens), lambda i: (i, 0, 0)),
        ],
        out_specs=pl.BlockSpec((shards, tokens, LANES), lambda i: (i, 0, 0)),
        out_shape=jax.ShapeDtypeStruct((parts, tokens, LANES), BF16),
        scratch_shapes=[pltpu.VMEM((2 * cols, 2 * lat_width), BF16)],
        compiler_params=grant(40),
        cost_estimate=cost(2 * parts * tokens * cols * 3 * lat_width, 6 << 20),
    )(first, second, got)


def total_kernel(got_ref, rank_ref, grad_ref, part_ref):
    total = jnp.sum(got_ref[...].astype(F32), axis=0)
    for dest in range(grad_ref.shape[0]):
        grad_ref[dest] = total.astype(BF16)
    turned = total.T
    slots = rank_ref.shape[1]
    for layer in range(2):
        rank = rank_ref[layer]
        part = jnp.zeros(rank.shape, F32)
        for slot in range(slots):
            row = layer * slots + slot
            part = jnp.where(rank == slot, turned[row : row + 1, :], part)
        part_ref[layer] = part.astype(BF16)


def slot_totals(got, rank):
    parts, tokens, _ = got.shape
    return pl.pallas_call(
        total_kernel,
        out_shape=[
            jax.ShapeDtypeStruct(got.shape, BF16),
            jax.ShapeDtypeStruct(rank.shape, BF16),
        ],
        compiler_params=grant(40),
        cost_estimate=cost(0, 1 << 20),
    )(got, rank)


def codes_kernel(low_ref, high_ref, first_ref, second_ref, spot_ref, code_ref, map_ref, sum_ref):
    shards, _, tokens = low_ref.shape
    cols, lat_width = second_ref.shape
    step = pl.program_id(0)
    runs = lat_width // 8
    block = 32

    @pl.when(step == 0)
    def _():
        sum_ref[...] = jnp.zeros_like(sum_ref)
        row = lax.broadcasted_iota(jnp.int32, map_ref.shape, 0)
        col = lax.broadcasted_iota(jnp.int32, map_ref.shape, 1)
        same = ((row // runs) % 2) == (col // lat_width)
        own, mine = row % runs, (col % lat_width) // 8
        weight = jnp.where(row < 2 * runs, jnp.where(own == mine, LANES, 0), jnp.where(own < mine, 1, 0))
        map_ref[...] = jnp.where(same, weight, 0).astype(F32).astype(BF16)

    for shard in range(shards):
        bits = high_ref[shard, tokens : 2 * tokens, :].astype(F32).astype(jnp.int32)
        held = lax.population_count(bits).astype(F32)
        both = jnp.concatenate([bits.astype(F32).astype(BF16), held.astype(BF16)], axis=1)
        spot_ref[shard] = jnp.dot(both, map_ref[...], preferred_element_type=F32).astype(jnp.int32)

    lane = lax.broadcasted_iota(jnp.int32, (block, LANES), 1)
    self_bit = jnp.left_shift(1, lane & 7)

    def spread(at, carry):
        shard = at // (tokens // block)
        low = pl.multiple_of((at % (tokens // block)) * block, block)
        row = pl.multiple_of(at * block, block)
        value = high_ref[shard, pl.ds(low, block), :].astype(F32)
        for chunk in range(2 * lat_width // LANES):
            base = (chunk * LANES // lat_width) * (LANES // 2)
            packed = spot_ref[shard, pl.ds(low, block), chunk * LANES : (chunk + 1) * LANES]
            bits = packed >> 7
            spot = (packed & (LANES - 1)) + lax.population_count(bits & (self_bit - 1)) + base
            spot = jnp.where((bits & self_bit) != 0, spot, LANES)
            spot_ref[shard, pl.ds(low, block), chunk * LANES : (chunk + 1) * LANES] = spot
            code = jnp.where(spot < LANES, lane_pick(value, spot & (LANES - 1)), 0.0)
            code_ref[pl.ds(row, block), chunk * LANES : (chunk + 1) * LANES] = code.astype(BF16)
        return carry

    lax.fori_loop(0, shards * tokens // block, spread, 0)

    cot = jnp.concatenate([low_ref[shard, 0 : 2 * cols, :] for shard in range(shards)], axis=1)
    dot = functools.partial(jnp.dot, preferred_element_type=F32)
    sum_ref[0 : 2 * cols, :] += dot(cot, code_ref[:, 0:lat_width])
    sum_ref[2 * cols : 3 * cols, :] += dot(cot[cols:], code_ref[:, lat_width:])

    @pl.when(step == pl.num_programs(0) - 1)
    def _():
        first_ref[0] = sum_ref[0:cols, :].astype(BF16)
        first_ref[1] = sum_ref[cols : 2 * cols, :].astype(BF16)
        second_ref[...] = sum_ref[2 * cols : 3 * cols, :].astype(BF16)


def decoder_grads(low, high, cols, lat_width):
    parts, _, tokens = low.shape
    shards = 4
    return pl.pallas_call(
        codes_kernel,
        grid=(parts // shards,),
        in_specs=[
            pl.BlockSpec((shards,) + low.shape[1:], lambda i: (i, 0, 0)),
            pl.BlockSpec((shards, 2 * tokens, tokens), lambda i: (i, 0, 0)),
        ],
        out_specs=[
            pl.BlockSpec((2, cols, lat_width), lambda i: (0, 0, 0)),
            pl.BlockSpec((cols, lat_width), lambda i: (0, 0)),
            pl.BlockSpec((shards, tokens, 2 * lat_width), lambda i: (i, 0, 0)),
        ],
        out_shape=[
            jax.ShapeDtypeStruct((2, cols, lat_width), BF16),
            jax.ShapeDtypeStruct((cols, lat_width), BF16),
            jax.ShapeDtypeStruct((parts, tokens, 2 * lat_width), jnp.int32),
        ],
        scratch_shapes=[
            pltpu.VMEM((shards * tokens, 2 * lat_width), BF16),
            pltpu.VMEM((4 * lat_width // 8, 2 * lat_width), BF16),
            pltpu.VMEM((3 * cols, lat_width), F32),
        ],
        compiler_params=grant(40),
        cost_estimate=cost(2 * parts * tokens * cols * 3 * lat_width, 16 << 20),
    )(low, high)


def back_kernel(high_ref, spot_ref, grad_ref, enc_ref, back_ref, sum_ref):
    shards, _, tokens = high_ref.shape
    _, cols, lat_width = enc_ref.shape
    step = pl.program_id(0)
    block = 32

    def spread(at, carry):
        shard = at // (tokens // block)
        low = pl.multiple_of((at % (tokens // block)) * block, block)
        row = pl.multiple_of(at * block, block)
        grad = grad_ref[shard, pl.ds(low, block), :].astype(F32)
        for chunk in range(2 * lat_width // LANES):
            spot = spot_ref[shard, pl.ds(low, block), chunk * LANES : (chunk + 1) * LANES]
            back = jnp.where(spot < LANES, lane_pick(grad, spot & (LANES - 1)), 0.0)
            back_ref[pl.ds(row, block), chunk * LANES : (chunk + 1) * LANES] = back.astype(BF16)
        return carry

    lax.fori_loop(0, shards * tokens // block, spread, 0)

    @pl.when(step == 0)
    def _():
        sum_ref[...] = jnp.zeros_like(sum_ref)

    res = jnp.concatenate([high_ref[shard, 2 * tokens :, :] for shard in range(shards)], axis=1)
    dot = functools.partial(jnp.dot, preferred_element_type=F32)
    sum_ref[0:cols, :] += dot(res[0:cols], back_ref[:, 0:lat_width])
    sum_ref[cols:, :] += dot(res[cols:], back_ref[:, lat_width:])

    @pl.when(step == pl.num_programs(0) - 1)
    def _():
        enc_ref[0] = sum_ref[0:cols, :].astype(BF16)
        enc_ref[1] = sum_ref[cols:, :].astype(BF16)


def encoder_grads(high, spots, grads, cols, lat_width):
    parts, rows, tokens = high.shape
    shards = 4
    return pl.pallas_call(
        back_kernel,
        grid=(parts // shards,),
        in_specs=[
            pl.BlockSpec((shards, rows, tokens), lambda i: (i, 0, 0)),
            pl.BlockSpec((shards,) + spots.shape[1:], lambda i: (i, 0, 0)),
            pl.BlockSpec((shards, tokens, LANES), lambda i: (i, 0, 0)),
        ],
        out_specs=pl.BlockSpec((2, cols, lat_width), lambda i: (0, 0, 0)),
        out_shape=jax.ShapeDtypeStruct((2, cols, lat_width), BF16),
        scratch_shapes=[
            pltpu.VMEM((shards * tokens, 2 * lat_width), BF16),
            pltpu.VMEM((2 * cols, lat_width), F32),
        ],
        compiler_params=grant(40),
        cost_estimate=cost(2 * parts * tokens * cols * 2 * lat_width, 16 << 20),
    )(high, spots, grads)


def exchange(array, axis):
    return lax.all_to_all(array, axis, 0, 0, tiled=True)


def union(part, axis, size):
    reach = 1
    while reach < size:
        others = [
            lax.ppermute(part, axis, [(at, at ^ (reach * hop)) for at in range(size)])
            for hop in (1, 2, 3)
            if reach * hop < size
        ]
        for other in others:
            part = part + other
        reach *= 4
    return part


def shards(layers, parts, residual, cotangent, decoder_first, decoder_second, latent_index, latent_value, active_count):
    lat_width = decoder_first.shape[0]
    cols = decoder_second.shape[1]
    start = (lax.axis_index("layer") * lat_width).astype(jnp.int32).reshape(1)
    index, value = latent_index.transpose(0, 2, 1), latent_value.transpose(0, 2, 1)
    packed, rank = pack(pack_first_kernel, lat_width, parts, 1, start, cotangent, index, active_count)
    (later,) = pack(pack_second_kernel, lat_width, parts, 2, start, residual, index, value, active_count, rank)
    got = exchange(packed, "dp")
    later, got = lax.optimization_barrier((later, got))
    got_later = exchange(later, "dp")
    terms = slot_terms(decoder_first.transpose(1, 2, 0), decoder_second.T, got)
    grads, part = slot_totals(exchange(terms, "dp"), rank)
    all_grads = exchange(grads, "dp")
    first_grad, second_grad, spots = decoder_grads(got, got_later, cols, lat_width)
    encoder_grad = encoder_grads(got_later, spots, all_grads, cols, lat_width)
    latent_grad = union(part, "layer", layers)
    return (
        first_grad.transpose(2, 0, 1),
        second_grad.T,
        encoder_grad.transpose(1, 0, 2),
        latent_grad.astype(F32).transpose(0, 2, 1),
    )


def solution(mesh):
    return jax.shard_map(
        functools.partial(shards, mesh.shape["layer"], mesh.shape["dp"]),
        mesh=mesh,
        in_specs=(
            P(None, "dp", None),
            P(None, "dp", None),
            P("layer", None, "dp"),
            P("layer", "dp"),
            P(None, "dp", None),
            P(None, "dp", None),
            P(None, "dp"),
        ),
        out_specs=(
            P("layer", None, "dp"),
            P("layer", "dp"),
            P("dp", None, "layer"),
            P(None, "dp", None),
        ),
        check_vma=False,
    )
```

```python
import functools
import jax
import jax.numpy as jnp
from jax import lax
from jax.experimental import pallas as pl
from jax.experimental.pallas import tpu as pltpu
from jax.sharding import PartitionSpec as P

BF16 = jnp.bfloat16
F32 = jnp.float32
LANES = 128
SHIFT = 256
EMPTY = 512
PACK_MIB = 60


def grant(mib):
    return pltpu.CompilerParams(vmem_limit_bytes=mib << 20)


def cost(flops, moved):
    return pl.CostEstimate(flops=flops, bytes_accessed=moved, transcendentals=0)


def lane_pick(table, where):
    return jnp.take_along_axis(table, where, axis=1, mode="promise_in_bounds")


def turn(source_ref, out_ref, layer, base):
    dests = out_ref.shape[0]
    cols = source_ref.shape[2] // dests
    turned = source_ref[layer].T
    for dest in range(dests):
        out_ref[dest, base + layer * cols : base + (layer + 1) * cols, :] = turned[dest * cols : (dest + 1) * cols]


def kept_slots(start_ref, idx_ref, live_ref, layer, lat_width):
    slots, tokens = idx_ref.shape[1:]
    place = lax.broadcasted_iota(jnp.int32, (slots, tokens), 0)
    local = idx_ref[layer] - start_ref[0]
    inside = (place < live_ref[layer : layer + 1, :]) & (local >= 0) & (local < lat_width)
    return place, local, inside


def pack_kernel(lat_width, start_ref, cot_ref, res_ref, idx_ref, live_ref, out_ref, rank_ref, slot_ref):
    slots, tokens = idx_ref.shape[1:]
    dests = out_ref.shape[0]
    cols = cot_ref.shape[2] // dests
    rows = res_ref.shape[1]

    @pl.when(pl.program_id(0) == 0)
    def _():
        found = []
        for layer in range(2):
            place, local, inside = kept_slots(start_ref, idx_ref, live_ref, layer, lat_width)
            key = jnp.where(inside, local, 1 << 20)
            rank = jnp.zeros((slots, tokens), jnp.int32)
            for slot in range(slots):
                rank = rank + jnp.where(key[slot : slot + 1, :] < key, 1, 0)
            rank = jnp.where(inside, rank, slots)
            rank_ref[layer] = rank
            key = local - SHIFT
            held = jnp.full((slots, tokens), EMPTY, jnp.int32)
            for slot in range(slots):
                held = jnp.where(rank[slot : slot + 1, :] == place, key[slot : slot + 1, :], held)
            found.append(held.astype(F32))
        slot_ref[...] = jnp.concatenate(found, axis=0).T.astype(BF16)

    for layer in range(2):
        turn(cot_ref, out_ref, layer, 0)
    base = 2 * cols + tokens
    for dest in range(dests):
        out_ref[dest, 2 * cols : base, :] = slot_ref[...]
        piece = res_ref[0, :, dest * cols : (dest + 1) * cols]
        out_ref[dest, base : base + rows, :] = piece[:, 0:LANES]
        rest = jnp.concatenate([piece[:, LANES:], jnp.zeros((rows, 2 * LANES - cols), BF16)], axis=1)
        out_ref[dest, base + rows : base + 2 * rows, :] = rest


def pack(lat_width, parts, start, cotangent, residual, index, live):
    _, tokens, width = cotangent.shape
    slots = index.shape[1]
    steps = 4
    share = residual.shape[1]
    rows = 2 * (width // parts) + tokens + 2 * share
    return pl.pallas_call(
        functools.partial(pack_kernel, lat_width),
        grid=(steps,),
        in_specs=[
            pl.BlockSpec(memory_space=pltpu.SMEM),
            pl.BlockSpec((2, tokens, width // steps), lambda i: (0, 0, i)),
            pl.BlockSpec((1, share, width // steps), lambda i: (0, 0, i)),
            pl.BlockSpec((2, slots, tokens), lambda i: (0, 0, 0)),
            pl.BlockSpec((2, tokens), lambda i: (0, 0)),
        ],
        out_specs=[
            pl.BlockSpec((parts // steps, rows, tokens), lambda i: (i, 0, 0)),
            pl.BlockSpec((2, slots, tokens), lambda i: (0, 0, 0)),
        ],
        out_shape=[
            jax.ShapeDtypeStruct((parts, rows, tokens), BF16),
            jax.ShapeDtypeStruct((2, slots, tokens), jnp.int32),
        ],
        scratch_shapes=[pltpu.VMEM((tokens, LANES), BF16)],
        compiler_params=grant(PACK_MIB),
        cost_estimate=cost(0, 5 << 20),
    )(start, cotangent, residual, index, live)


def values_kernel(rank_ref, val_ref, out_ref):
    slots, tokens = val_ref.shape[1:]
    place = lax.broadcasted_iota(jnp.int32, (slots, tokens), 0)
    codes = []
    for layer in range(2):
        rank = rank_ref[layer]
        value = val_ref[layer].astype(F32)
        code = jnp.zeros((slots, tokens), F32)
        for slot in range(slots):
            code = jnp.where(rank[slot : slot + 1, :] == place, value[slot : slot + 1, :], code)
        codes.append(code)
    out_ref[...] = jnp.concatenate(codes, axis=0).T.astype(BF16)


def slot_values(rank, value):
    return pl.pallas_call(
        values_kernel,
        out_shape=jax.ShapeDtypeStruct((value.shape[2], LANES), BF16),
        compiler_params=grant(40),
        cost_estimate=cost(0, 1 << 20),
    )(rank, value)


def terms_kernel(wf_ref, ws_ref, val_ref, got_ref, out_ref, weight_ref):
    shards, _, tokens = got_ref.shape
    cols, lat_width = ws_ref.shape

    @pl.when(pl.program_id(0) == 0)
    def _():
        weight_ref[0:cols, 0:lat_width] = wf_ref[0]
        weight_ref[cols : 2 * cols, 0:lat_width] = wf_ref[1]
        weight_ref[0:cols, lat_width:] = jnp.zeros((cols, lat_width), BF16)
        weight_ref[cols : 2 * cols, lat_width:] = ws_ref[...]

    for shard in range(shards):
        dense = lax.dot_general(
            got_ref[shard, 0 : 2 * cols, :].T,
            weight_ref[...],
            (((1,), (0,)), ((), ())),
            preferred_element_type=F32,
        )
        held = got_ref[shard, 2 * cols : 2 * cols + tokens, :].astype(F32).astype(jnp.int32) + SHIFT
        lane = lax.broadcasted_iota(jnp.int32, held.shape, 1)
        chunks = lat_width // LANES
        chunk = jnp.where(
            held < lat_width, (held >> 7) + jnp.where(lane >= LANES // 2, chunks, 0), 2 * chunks
        )
        within = held & (LANES - 1)
        picked = jnp.zeros(held.shape, F32)
        for part in range(2 * chunks):
            table = dense[:, part * LANES : (part + 1) * LANES]
            picked = jnp.where(chunk == part, lane_pick(table, within), picked)
        out_ref[shard, 0:tokens, :] = picked.astype(BF16)
        out_ref[shard, tokens:, :] = val_ref[...]


def slot_terms(first, second, values, got):
    parts, rows, tokens = got.shape
    cols, lat_width = second.shape
    shards = 2
    return pl.pallas_call(
        terms_kernel,
        grid=(parts // shards,),
        in_specs=[
            pl.BlockSpec((2, cols, lat_width), lambda i: (0, 0, 0)),
            pl.BlockSpec((cols, lat_width), lambda i: (0, 0)),
            pl.BlockSpec((tokens, LANES), lambda i: (0, 0)),
            pl.BlockSpec((shards, rows, tokens), lambda i: (i, 0, 0)),
        ],
        out_specs=pl.BlockSpec((shards, 2 * tokens, LANES), lambda i: (i, 0, 0)),
        out_shape=jax.ShapeDtypeStruct((parts, 2 * tokens, LANES), BF16),
        scratch_shapes=[pltpu.VMEM((2 * cols, 2 * lat_width), BF16)],
        compiler_params=grant(40),
        cost_estimate=cost(2 * parts * tokens * cols * 3 * lat_width, 6 << 20),
    )(first, second, values, got)


def total_kernel(got_ref, rank_ref, grad_ref, part_ref):
    tokens = grad_ref.shape[1]
    total = jnp.sum(got_ref[:, 0:tokens, :].astype(F32), axis=0)
    for dest in range(grad_ref.shape[0]):
        grad_ref[dest] = total.astype(BF16)
    turned = total.T
    slots = rank_ref.shape[1]
    for layer in range(2):
        rank = rank_ref[layer]
        part = jnp.zeros(rank.shape, F32)
        for slot in range(slots):
            row = layer * slots + slot
            part = jnp.where(rank == slot, turned[row : row + 1, :], part)
        part_ref[layer] = part.astype(BF16)


def slot_totals(got, rank):
    parts, rows, _ = got.shape
    return pl.pallas_call(
        total_kernel,
        out_shape=[
            jax.ShapeDtypeStruct((parts, rows // 2, LANES), BF16),
            jax.ShapeDtypeStruct(rank.shape, BF16),
        ],
        compiler_params=grant(40),
        cost_estimate=cost(0, 1 << 20),
    )(got, rank)


def spots_kernel(cols, got_ref, spot_ref, map_ref):
    shards, _, tokens = got_ref.shape
    lat_width = spot_ref.shape[2] // 2
    runs = lat_width // 8

    @pl.when(pl.program_id(0) == 0)
    def _():
        row = lax.broadcasted_iota(jnp.int32, map_ref.shape, 0)
        col = lax.broadcasted_iota(jnp.int32, map_ref.shape, 1)
        same = (row % (2 * runs)) == (col // 8)
        map_ref[...] = jnp.where(same, jnp.where(row < 2 * runs, LANES, 1), 0).astype(F32).astype(BF16)

    lane = lax.broadcasted_iota(jnp.int32, (tokens, LANES), 1)
    half = LANES // 2
    base = lane & half
    start = 8 * (lane & (half - 1)) - SHIFT
    self_bit = jnp.left_shift(1, lane & 7)
    for shard in range(shards):
        held = got_ref[shard, 2 * cols : 2 * cols + tokens, :].astype(F32).astype(jnp.int32)
        below = base
        for jump in (32, 16, 8, 4, 2, 1):
            further = below + jump
            below = jnp.where(lane_pick(held, further - 1) < start, further, below)
        last = base + (half - 1)
        bits = jnp.zeros((tokens, LANES), jnp.int32)
        for hop in range(8):
            spot = below if hop == 0 else jnp.minimum(below + hop, last)
            ahead = lane_pick(held, spot) - start
            bits = bits | jnp.where((ahead & -8) == 0, jnp.left_shift(1, ahead & 7), 0)
        both = jnp.concatenate([bits.astype(F32).astype(BF16), below.astype(F32).astype(BF16)], axis=1)
        spread = jnp.dot(both, map_ref[...], preferred_element_type=F32).astype(jnp.int32)
        for chunk in range(2 * lat_width // LANES):
            packed = spread[:, chunk * LANES : (chunk + 1) * LANES]
            bits = packed >> 7
            spot = (packed & (LANES - 1)) + lax.population_count(bits & (self_bit - 1))
            spot = jnp.where((bits & self_bit) != 0, spot, LANES)
            spot_ref[shard, :, chunk * LANES : (chunk + 1) * LANES] = spot.astype(F32).astype(BF16)


def slot_spots(got, cols, lat_width):
    parts, rows, tokens = got.shape
    shards = 2
    return pl.pallas_call(
        functools.partial(spots_kernel, cols),
        grid=(parts // shards,),
        in_specs=[pl.BlockSpec((shards, rows, tokens), lambda i: (i, 0, 0))],
        out_specs=pl.BlockSpec((shards, tokens, 2 * lat_width), lambda i: (i, 0, 0)),
        out_shape=jax.ShapeDtypeStruct((parts, tokens, 2 * lat_width), BF16),
        scratch_shapes=[pltpu.VMEM((2 * LANES, 2 * lat_width), BF16)],
        compiler_params=grant(40),
        cost_estimate=cost(2 * parts * tokens * 2 * LANES * 2 * lat_width, 8 << 20),
    )(got)


def dense(table_ref, first_row, spot_ref, out_ref):
    shards, tokens, width = spot_ref.shape
    for shard in range(shards):
        table = table_ref[shard, first_row : first_row + tokens, :].astype(F32)
        for chunk in range(width // LANES):
            at = slice(chunk * LANES, (chunk + 1) * LANES)
            spot = spot_ref[shard, :, at].astype(F32).astype(jnp.int32)
            found = jnp.where(spot < LANES, lane_pick(table, spot & (LANES - 1)), 0.0)
            out_ref[shard * tokens : (shard + 1) * tokens, at] = found.astype(BF16)


def codes_kernel(got_ref, val_ref, spot_ref, first_ref, second_ref, code_ref, sum_ref):
    shards, tokens, _ = spot_ref.shape
    cols, lat_width = second_ref.shape
    step = pl.program_id(0)

    @pl.when(step == 0)
    def _():
        sum_ref[...] = jnp.zeros_like(sum_ref)

    dense(val_ref, tokens, spot_ref, code_ref)
    cot = jnp.concatenate([got_ref[shard, 0 : 2 * cols, :] for shard in range(shards)], axis=1)
    dot = functools.partial(jnp.dot, preferred_element_type=F32)
    sum_ref[0 : 2 * cols, :] += dot(cot, code_ref[:, 0:lat_width])
    sum_ref[2 * cols : 3 * cols, :] += dot(cot[cols:], code_ref[:, lat_width:])

    @pl.when(step == pl.num_programs(0) - 1)
    def _():
        first_ref[0] = sum_ref[0:cols, :].astype(BF16)
        first_ref[1] = sum_ref[cols : 2 * cols, :].astype(BF16)
        second_ref[...] = sum_ref[2 * cols : 3 * cols, :].astype(BF16)


def decoder_grads(got, slots, spots, cols, lat_width):
    parts, rows, tokens = got.shape
    shards = 4
    return pl.pallas_call(
        codes_kernel,
        grid=(parts // shards,),
        in_specs=[
            pl.BlockSpec((shards, rows, tokens), lambda i: (i, 0, 0)),
            pl.BlockSpec((shards, 2 * tokens, LANES), lambda i: (i, 0, 0)),
            pl.BlockSpec((shards, tokens, 2 * lat_width), lambda i: (i, 0, 0)),
        ],
        out_specs=[
            pl.BlockSpec((2, cols, lat_width), lambda i: (0, 0, 0)),
            pl.BlockSpec((cols, lat_width), lambda i: (0, 0)),
        ],
        out_shape=[
            jax.ShapeDtypeStruct((2, cols, lat_width), BF16),
            jax.ShapeDtypeStruct((cols, lat_width), BF16),
        ],
        scratch_shapes=[
            pltpu.VMEM((shards * tokens, 2 * lat_width), BF16),
            pltpu.VMEM((3 * cols, lat_width), F32),
        ],
        compiler_params=grant(40),
        cost_estimate=cost(2 * parts * tokens * cols * 3 * lat_width, 8 << 20),
    )(got, slots, spots)


def back_kernel(res_ref, spot_ref, grad_ref, enc_ref, back_ref, sum_ref):
    shards, tokens, _ = spot_ref.shape
    _, cols, lat_width = enc_ref.shape
    owners = res_ref.shape[0] // 2
    rows = res_ref.shape[2] // 2
    step = pl.program_id(0)
    dense(grad_ref, 0, spot_ref, back_ref)

    @pl.when(step == 0)
    def _():
        sum_ref[...] = jnp.zeros_like(sum_ref)

    for layer in range(2):
        sides = []
        for side in range(2):
            pieces = [
                res_ref[layer * owners + owner, shard, side * rows : (side + 1) * rows, :]
                for shard in range(shards)
                for owner in range(owners)
            ]
            sides.append(jnp.concatenate(pieces, axis=0).T)
        left = jnp.concatenate(sides, axis=0)[0:cols]
        sum_ref[layer * cols : (layer + 1) * cols, :] += jnp.dot(
            left, back_ref[:, layer * lat_width : (layer + 1) * lat_width], preferred_element_type=F32
        )

    @pl.when(step == pl.num_programs(0) - 1)
    def _():
        enc_ref[0] = sum_ref[0:cols, :].astype(BF16)
        enc_ref[1] = sum_ref[cols:, :].astype(BF16)


def encoder_grads(res, spots, grads, cols, lat_width):
    owners, parts, rows, _ = res.shape
    tokens = spots.shape[1]
    shards = 4
    return pl.pallas_call(
        back_kernel,
        grid=(parts // shards,),
        in_specs=[
            pl.BlockSpec((owners, shards, rows, LANES), lambda i: (0, i, 0, 0)),
            pl.BlockSpec((shards,) + spots.shape[1:], lambda i: (i, 0, 0)),
            pl.BlockSpec((shards, tokens, LANES), lambda i: (i, 0, 0)),
        ],
        out_specs=pl.BlockSpec((2, cols, lat_width), lambda i: (0, 0, 0)),
        out_shape=jax.ShapeDtypeStruct((2, cols, lat_width), BF16),
        scratch_shapes=[
            pltpu.VMEM((shards * tokens, 2 * lat_width), BF16),
            pltpu.VMEM((2 * cols, lat_width), F32),
        ],
        compiler_params=grant(40),
        cost_estimate=cost(2 * parts * tokens * cols * 2 * lat_width, 8 << 20),
    )(res, spots, grads)


def exchange(array, axis):
    return lax.all_to_all(array, axis, 0, 0, tiled=True)


def union(part, axis, size):
    reach = 1
    while reach < size:
        others = [
            lax.ppermute(part, axis, [(at, at ^ (reach * hop)) for at in range(size)])
            for hop in (1, 2, 3)
            if reach * hop < size
        ]
        for other in others:
            part = part + other
        reach *= 4
    return part


def shards(layers, parts, residual, cotangent, decoder_first, decoder_second, latent_index, latent_value, active_count):
    lat_width = decoder_first.shape[0]
    cols = decoder_second.shape[1]
    start = (lax.axis_index("layer") * lat_width).astype(jnp.int32).reshape(1)
    index, value = latent_index.transpose(0, 2, 1), latent_value.transpose(0, 2, 1)
    tokens = residual.shape[1]
    place = lax.axis_index("layer")
    share = 2 * tokens // layers
    own = lax.dynamic_slice(
        residual,
        (place * 2 // layers, place % (layers // 2) * share, 0),
        (1, share, residual.shape[2]),
    )
    packed, rank = pack(lat_width, parts, start, cotangent, own, index, active_count)
    values = slot_values(rank, value)
    got = exchange(packed, "dp")
    res = lax.all_gather(got[:, 2 * cols + tokens :, :], "layer", axis=0)
    terms = slot_terms(decoder_first.transpose(1, 2, 0), decoder_second.T, values, got)
    slots = exchange(terms, "dp")
    spots = slot_spots(got, cols, lat_width)
    grads, part = slot_totals(slots, rank)
    all_grads = exchange(grads, "dp")
    first_grad, second_grad = decoder_grads(got, slots, spots, cols, lat_width)
    encoder_grad = encoder_grads(res, spots, all_grads, cols, lat_width)
    latent_grad = union(part, "layer", layers)
    return (
        first_grad.transpose(2, 0, 1),
        second_grad.T,
        encoder_grad.transpose(1, 0, 2),
        latent_grad.astype(F32).transpose(0, 2, 1),
    )


def solution(mesh):
    return jax.shard_map(
        functools.partial(shards, mesh.shape["layer"], mesh.shape["dp"]),
        mesh=mesh,
        in_specs=(
            P(None, "dp", None),
            P(None, "dp", None),
            P("layer", None, "dp"),
            P("layer", "dp"),
            P(None, "dp", None),
            P(None, "dp", None),
            P(None, "dp"),
        ),
        out_specs=(
            P("layer", None, "dp"),
            P("layer", "dp"),
            P("dp", None, "layer"),
            P(None, "dp", None),
        ),
        check_vma=False,
    )
```

```python
import functools
import jax
import jax.numpy as jnp
from jax import lax
from jax.experimental import pallas as pl
from jax.experimental.pallas import tpu as pltpu
from jax.sharding import PartitionSpec as P

BF16 = jnp.bfloat16
F32 = jnp.float32
LANES = 128
SHIFT = 256
EMPTY = 512
STREAM_MIB = 60
KERNEL_MIB = 16


def grant(mib=KERNEL_MIB):
    return pltpu.CompilerParams(vmem_limit_bytes=mib << 20)


def cost(flops, moved):
    return pl.CostEstimate(flops=flops, bytes_accessed=moved, transcendentals=0)


def lane_pick(table, where):
    return jnp.take_along_axis(table, where, axis=1, mode="promise_in_bounds")


def turn(source_ref, out_ref, layer, base):
    dests = out_ref.shape[0]
    cols = source_ref.shape[2] // dests
    turned = source_ref[layer].T
    for dest in range(dests):
        out_ref[dest, base + layer * cols : base + (layer + 1) * cols, :] = turned[dest * cols : (dest + 1) * cols]


def kept_slots(start_ref, idx_ref, live_ref, layer, lat_width):
    slots, tokens = idx_ref.shape[1:]
    place = lax.broadcasted_iota(jnp.int32, (slots, tokens), 0)
    local = idx_ref[layer] - start_ref[0]
    inside = (place < live_ref[layer : layer + 1, :]) & (local >= 0) & (local < lat_width)
    return place, local, inside


def pack_kernel(lat_width, start_ref, cot_ref, res_ref, idx_ref, live_ref, out_ref, rank_ref, slot_ref):
    slots, tokens = idx_ref.shape[1:]
    dests = out_ref.shape[0]
    cols = cot_ref.shape[2] // dests
    rows = res_ref.shape[1]

    @pl.when(pl.program_id(0) == 0)
    def _():
        found = []
        for layer in range(2):
            place, local, inside = kept_slots(start_ref, idx_ref, live_ref, layer, lat_width)
            key = jnp.where(inside, local, 1 << 20)
            rank = jnp.zeros((slots, tokens), jnp.int32)
            for slot in range(slots):
                rank = rank + jnp.where(key[slot : slot + 1, :] < key, 1, 0)
            rank = jnp.where(inside, rank, slots)
            rank_ref[layer] = rank
            key = local - SHIFT
            held = jnp.full((slots, tokens), EMPTY, jnp.int32)
            for slot in range(slots):
                held = jnp.where(rank[slot : slot + 1, :] == place, key[slot : slot + 1, :], held)
            found.append(held.astype(F32))
        slot_ref[...] = jnp.concatenate(found, axis=0).T.astype(BF16)

    more = 4 * rows
    for layer in range(2):
        turn(cot_ref, out_ref, layer, more)
    for dest in range(dests):
        out_ref[dest, more + 2 * cols :, :] = slot_ref[...]
        for layer in range(2):
            piece = res_ref[layer, :, dest * cols : (dest + 1) * cols]
            out_ref[dest, 2 * layer * rows : (2 * layer + 1) * rows, :] = piece[:, 0:LANES]
            rest = jnp.concatenate([piece[:, LANES:], jnp.zeros((rows, 2 * LANES - cols), BF16)], axis=1)
            out_ref[dest, (2 * layer + 1) * rows : (2 * layer + 2) * rows, :] = rest


def pack(lat_width, parts, members, start, cotangent, residual, index, live):
    _, tokens, width = cotangent.shape
    slots = index.shape[1]
    steps = 4
    share = tokens // members
    rows = 2 * (width // parts) + tokens + 4 * share
    return pl.pallas_call(
        functools.partial(pack_kernel, lat_width),
        grid_spec=pltpu.PrefetchScalarGridSpec(
            num_scalar_prefetch=1,
            grid=(steps,),
            in_specs=[
                pl.BlockSpec((2, tokens, width // steps), lambda i, own: (0, 0, i)),
                pl.BlockSpec((2, share, width // steps), lambda i, own: (0, own[1], i)),
                pl.BlockSpec((2, slots, tokens), lambda i, own: (0, 0, 0)),
                pl.BlockSpec((2, tokens), lambda i, own: (0, 0)),
            ],
            out_specs=[
                pl.BlockSpec((parts // steps, rows, tokens), lambda i, own: (i, 0, 0)),
                pl.BlockSpec((2, slots, tokens), lambda i, own: (0, 0, 0)),
            ],
            scratch_shapes=[pltpu.VMEM((tokens, LANES), BF16)],
        ),
        out_shape=[
            jax.ShapeDtypeStruct((parts, rows, tokens), BF16),
            jax.ShapeDtypeStruct((2, slots, tokens), jnp.int32),
        ],
        compiler_params=grant(STREAM_MIB),
        cost_estimate=cost(0, 5 << 20),
    )(start, cotangent, residual, index, live)


def values_kernel(rank_ref, val_ref, out_ref):
    slots, tokens = val_ref.shape[1:]
    place = lax.broadcasted_iota(jnp.int32, (slots, tokens), 0)
    codes = []
    for layer in range(2):
        rank = rank_ref[layer]
        value = val_ref[layer].astype(F32)
        code = jnp.zeros((slots, tokens), F32)
        for slot in range(slots):
            code = jnp.where(rank[slot : slot + 1, :] == place, value[slot : slot + 1, :], code)
        codes.append(code)
    out_ref[...] = jnp.concatenate(codes, axis=0).T.astype(BF16)


def slot_values(rank, value):
    return pl.pallas_call(
        values_kernel,
        out_shape=jax.ShapeDtypeStruct((value.shape[2], LANES), BF16),
        compiler_params=grant(),
        cost_estimate=cost(0, 1 << 20),
    )(rank, value)


def terms_kernel(more, wf_ref, ws_ref, val_ref, got_ref, out_ref, weight_ref):
    shards, _, tokens = got_ref.shape
    cols, lat_width = ws_ref.shape

    @pl.when(pl.program_id(0) == 0)
    def _():
        weight_ref[0:cols, 0:lat_width] = wf_ref[0]
        weight_ref[cols : 2 * cols, 0:lat_width] = wf_ref[1]
        weight_ref[0:cols, lat_width:] = jnp.zeros((cols, lat_width), BF16)
        weight_ref[cols : 2 * cols, lat_width:] = ws_ref[...]

    for shard in range(shards):
        dense = lax.dot_general(
            got_ref[shard, more : more + 2 * cols, :].T,
            weight_ref[...],
            (((1,), (0,)), ((), ())),
            preferred_element_type=F32,
        )
        held = got_ref[shard, more + 2 * cols :, :].astype(F32).astype(jnp.int32) + SHIFT
        lane = lax.broadcasted_iota(jnp.int32, held.shape, 1)
        chunks = lat_width // LANES
        chunk = jnp.where(
            held < lat_width, (held >> 7) + jnp.where(lane >= LANES // 2, chunks, 0), 2 * chunks
        )
        within = held & (LANES - 1)
        picked = jnp.zeros(held.shape, F32)
        for part in range(2 * chunks):
            table = dense[:, part * LANES : (part + 1) * LANES]
            picked = jnp.where(chunk == part, lane_pick(table, within), picked)
        out_ref[shard, 0:tokens, :] = picked.astype(BF16)
        out_ref[shard, tokens:, :] = val_ref[...]


def slot_terms(first, second, values, got):
    parts, rows, tokens = got.shape
    cols, lat_width = second.shape
    shards = 2
    return pl.pallas_call(
        functools.partial(terms_kernel, rows - tokens - 2 * cols),
        grid=(parts // shards,),
        in_specs=[
            pl.BlockSpec((2, cols, lat_width), lambda i: (0, 0, 0)),
            pl.BlockSpec((cols, lat_width), lambda i: (0, 0)),
            pl.BlockSpec((tokens, LANES), lambda i: (0, 0)),
            pl.BlockSpec((shards, rows, tokens), lambda i: (i, 0, 0)),
        ],
        out_specs=pl.BlockSpec((shards, 2 * tokens, LANES), lambda i: (i, 0, 0)),
        out_shape=jax.ShapeDtypeStruct((parts, 2 * tokens, LANES), BF16),
        scratch_shapes=[pltpu.VMEM((2 * cols, 2 * lat_width), BF16)],
        compiler_params=grant(),
        cost_estimate=cost(2 * parts * tokens * cols * 3 * lat_width, 6 << 20),
    )(first, second, values, got)


def total_kernel(got_ref, rank_ref, grad_ref, part_ref):
    tokens = grad_ref.shape[1]
    total = jnp.sum(got_ref[:, 0:tokens, :].astype(F32), axis=0)
    for dest in range(grad_ref.shape[0]):
        grad_ref[dest] = total.astype(BF16)
    turned = total.T
    slots = rank_ref.shape[1]
    for layer in range(2):
        rank = rank_ref[layer]
        part = jnp.zeros(rank.shape, F32)
        for slot in range(slots):
            row = layer * slots + slot
            part = jnp.where(rank == slot, turned[row : row + 1, :], part)
        part_ref[layer] = part.astype(BF16)


def slot_totals(got, rank):
    parts, rows, _ = got.shape
    return pl.pallas_call(
        total_kernel,
        out_shape=[
            jax.ShapeDtypeStruct((parts, rows // 2, LANES), BF16),
            jax.ShapeDtypeStruct(rank.shape, BF16),
        ],
        compiler_params=grant(),
        cost_estimate=cost(0, 1 << 20),
    )(got, rank)


def spots_kernel(got_ref, spot_ref, map_ref):
    shards, _, tokens = got_ref.shape
    lat_width = spot_ref.shape[2] // 2
    runs = lat_width // 8

    @pl.when(pl.program_id(0) == 0)
    def _():
        row = lax.broadcasted_iota(jnp.int32, map_ref.shape, 0)
        col = lax.broadcasted_iota(jnp.int32, map_ref.shape, 1)
        same = (row % (2 * runs)) == (col // 8)
        map_ref[...] = jnp.where(same, jnp.where(row < 2 * runs, LANES, 1), 0).astype(F32).astype(BF16)

    lane = lax.broadcasted_iota(jnp.int32, (tokens, LANES), 1)
    half = LANES // 2
    base = lane & half
    start = 8 * (lane & (half - 1)) - SHIFT
    self_bit = jnp.left_shift(1, lane & 7)
    for shard in range(shards):
        held = got_ref[shard, got_ref.shape[1] - tokens :, :].astype(F32).astype(jnp.int32)
        below = base
        for jump in (32, 16, 8, 4, 2, 1):
            further = below + jump
            below = jnp.where(lane_pick(held, further - 1) < start, further, below)
        last = base + (half - 1)
        bits = jnp.zeros((tokens, LANES), jnp.int32)
        for hop in range(8):
            spot = below if hop == 0 else jnp.minimum(below + hop, last)
            ahead = lane_pick(held, spot) - start
            bits = bits | jnp.where((ahead & -8) == 0, jnp.left_shift(1, ahead & 7), 0)
        both = jnp.concatenate([bits.astype(F32).astype(BF16), below.astype(F32).astype(BF16)], axis=1)
        spread = jnp.dot(both, map_ref[...], preferred_element_type=F32).astype(jnp.int32)
        for chunk in range(2 * lat_width // LANES):
            packed = spread[:, chunk * LANES : (chunk + 1) * LANES]
            bits = packed >> 7
            spot = (packed & (LANES - 1)) + lax.population_count(bits & (self_bit - 1))
            spot = jnp.where((bits & self_bit) != 0, spot, LANES)
            spot_ref[shard, :, chunk * LANES : (chunk + 1) * LANES] = spot.astype(F32).astype(BF16)


def slot_spots(got, lat_width):
    parts, rows, tokens = got.shape
    shards = 2
    return pl.pallas_call(
        spots_kernel,
        grid=(parts // shards,),
        in_specs=[pl.BlockSpec((shards, rows, tokens), lambda i: (i, 0, 0))],
        out_specs=pl.BlockSpec((shards, tokens, 2 * lat_width), lambda i: (i, 0, 0)),
        out_shape=jax.ShapeDtypeStruct((parts, tokens, 2 * lat_width), BF16),
        scratch_shapes=[pltpu.VMEM((2 * LANES, 2 * lat_width), BF16)],
        compiler_params=grant(),
        cost_estimate=cost(2 * parts * tokens * 2 * LANES * 2 * lat_width, 8 << 20),
    )(got)


def dense(table_ref, first_row, spot_ref, out_ref):
    shards, tokens, width = spot_ref.shape
    for shard in range(shards):
        table = table_ref[shard, first_row : first_row + tokens, :].astype(F32)
        for chunk in range(width // LANES):
            at = slice(chunk * LANES, (chunk + 1) * LANES)
            spot = spot_ref[shard, :, at].astype(F32).astype(jnp.int32)
            found = jnp.where(spot < LANES, lane_pick(table, spot & (LANES - 1)), 0.0)
            out_ref[shard * tokens : (shard + 1) * tokens, at] = found.astype(BF16)


def codes_kernel(got_ref, val_ref, spot_ref, first_ref, second_ref, code_ref, sum_ref):
    shards, tokens, _ = spot_ref.shape
    cols, lat_width = second_ref.shape
    step = pl.program_id(0)

    @pl.when(step == 0)
    def _():
        sum_ref[...] = jnp.zeros_like(sum_ref)

    dense(val_ref, tokens, spot_ref, code_ref)
    more = got_ref.shape[1] - tokens - 2 * cols
    cot = jnp.concatenate([got_ref[shard, more : more + 2 * cols, :] for shard in range(shards)], axis=1)
    dot = functools.partial(jnp.dot, preferred_element_type=F32)
    sum_ref[0 : 2 * cols, :] += dot(cot, code_ref[:, 0:lat_width])
    sum_ref[2 * cols : 3 * cols, :] += dot(cot[cols:], code_ref[:, lat_width:])

    @pl.when(step == pl.num_programs(0) - 1)
    def _():
        first_ref[0] = sum_ref[0:cols, :].astype(BF16)
        first_ref[1] = sum_ref[cols : 2 * cols, :].astype(BF16)
        second_ref[...] = sum_ref[2 * cols : 3 * cols, :].astype(BF16)


def decoder_grads(got, slots, spots, cols, lat_width):
    parts, rows, tokens = got.shape
    shards = 4
    return pl.pallas_call(
        codes_kernel,
        grid=(parts // shards,),
        in_specs=[
            pl.BlockSpec((shards, rows, tokens), lambda i: (i, 0, 0)),
            pl.BlockSpec((shards, 2 * tokens, LANES), lambda i: (i, 0, 0)),
            pl.BlockSpec((shards, tokens, 2 * lat_width), lambda i: (i, 0, 0)),
        ],
        out_specs=[
            pl.BlockSpec((2, cols, lat_width), lambda i: (0, 0, 0)),
            pl.BlockSpec((cols, lat_width), lambda i: (0, 0)),
        ],
        out_shape=[
            jax.ShapeDtypeStruct((2, cols, lat_width), BF16),
            jax.ShapeDtypeStruct((cols, lat_width), BF16),
        ],
        scratch_shapes=[
            pltpu.VMEM((shards * tokens, 2 * lat_width), BF16),
            pltpu.VMEM((3 * cols, lat_width), F32),
        ],
        compiler_params=grant(STREAM_MIB),
        cost_estimate=cost(2 * parts * tokens * cols * 3 * lat_width, 8 << 20),
    )(got, slots, spots)


def back_kernel(own_ref, *refs):
    res_refs, (spot_ref, grad_ref, enc_ref, back_ref, sum_ref) = refs[:-5], refs[-5:]
    members = len(res_refs)
    shards, tokens, width = spot_ref.shape
    _, cols, lat_width = enc_ref.shape
    rows = tokens // members
    step = pl.program_id(0)
    for shard in range(shards):
        for member in range(members):
            low = pl.multiple_of((own_ref[1] ^ member) * rows, rows)
            table = grad_ref[shard, pl.ds(low, rows), :].astype(F32)
            to = shard * tokens + member * rows
            for chunk in range(width // LANES):
                at = slice(chunk * LANES, (chunk + 1) * LANES)
                spot = spot_ref[shard, pl.ds(low, rows), at].astype(F32).astype(jnp.int32)
                found = jnp.where(spot < LANES, lane_pick(table, spot & (LANES - 1)), 0.0)
                back_ref[to : to + rows, at] = found.astype(BF16)

    @pl.when(step == 0)
    def _():
        sum_ref[...] = jnp.zeros_like(sum_ref)

    for layer in range(2):
        sides = []
        for side in range(2):
            low = (2 * layer + side) * rows
            pieces = [res_ref[shard, low : low + rows, :] for shard in range(shards) for res_ref in res_refs]
            sides.append(jnp.concatenate(pieces, axis=0).T)
        left = jnp.concatenate(sides, axis=0)[0:cols]
        sum_ref[layer * cols : (layer + 1) * cols, :] += jnp.dot(
            left, back_ref[:, layer * lat_width : (layer + 1) * lat_width], preferred_element_type=F32
        )

    @pl.when(step == pl.num_programs(0) - 1)
    def _():
        enc_ref[0] = sum_ref[0:cols, :].astype(BF16)
        enc_ref[1] = sum_ref[cols:, :].astype(BF16)


def encoder_grads(own, res, spots, grads, cols, lat_width):
    parts, tokens, _ = spots.shape
    rows = 4 * tokens // len(res)
    shards = 4
    return pl.pallas_call(
        back_kernel,
        grid=(parts // shards,),
        in_specs=[pl.BlockSpec(memory_space=pltpu.SMEM)]
        + [pl.BlockSpec((shards, rows, LANES), lambda i: (i, 0, 0)) for _ in res]
        + [
            pl.BlockSpec((shards,) + spots.shape[1:], lambda i: (i, 0, 0)),
            pl.BlockSpec((shards, tokens, LANES), lambda i: (i, 0, 0)),
        ],
        out_specs=pl.BlockSpec((2, cols, lat_width), lambda i: (0, 0, 0)),
        out_shape=jax.ShapeDtypeStruct((2, cols, lat_width), BF16),
        scratch_shapes=[
            pltpu.VMEM((shards * tokens, 2 * lat_width), BF16),
            pltpu.VMEM((2 * cols, lat_width), F32),
        ],
        compiler_params=grant(STREAM_MIB),
        cost_estimate=cost(2 * parts * tokens * cols * 2 * lat_width, 8 << 20),
    )(own, *res, spots, grads)


def exchange(array, axis):
    return lax.all_to_all(array, axis, 0, 0, tiled=True)


def from_hops(array, axis, size, hops):
    return [lax.ppermute(array, axis, [(at, at ^ hop) for at in range(size)]) for hop in hops]


def union(part, axis, size):
    reach = 1
    while reach < size:
        for other in from_hops(part, axis, size, [reach * hop for hop in (1, 2, 3) if reach * hop < size]):
            part = part + other
        reach *= 4
    return part


def shards(layers, parts, residual, cotangent, decoder_first, decoder_second, latent_index, latent_value, active_count):
    lat_width = decoder_first.shape[0]
    cols = decoder_second.shape[1]
    tokens = residual.shape[1]
    members = 4
    place = lax.axis_index("layer")
    own = jnp.stack([place * lat_width, place % members]).astype(jnp.int32)
    index, value = latent_index.transpose(0, 2, 1), latent_value.transpose(0, 2, 1)
    packed, rank = pack(lat_width, parts, members, own, cotangent, residual, index, active_count)
    values = slot_values(rank, value)
    got = exchange(packed, "dp")
    share = got[:, : 4 * tokens // members, :]
    res = [got] + from_hops(share, "layer", layers, range(1, members))
    terms = slot_terms(decoder_first.transpose(1, 2, 0), decoder_second.T, values, got)
    slots = exchange(terms, "dp")
    spots = slot_spots(got, lat_width)
    slots, spots, *res[1:3] = lax.optimization_barrier((slots, spots, *res[1:3]))
    grads, part = slot_totals(slots, rank)
    all_grads = exchange(grads, "dp")
    first_grad, second_grad = decoder_grads(got, slots, spots, cols, lat_width)
    all_grads, first_grad = lax.optimization_barrier((all_grads, first_grad))
    encoder_grad = encoder_grads(own, res, spots, all_grads, cols, lat_width)
    latent_grad = union(part, "layer", layers)
    return (
        first_grad.transpose(2, 0, 1),
        second_grad.T,
        encoder_grad.transpose(1, 0, 2),
        latent_grad.astype(F32).transpose(0, 2, 1),
    )


def solution(mesh):
    return jax.shard_map(
        functools.partial(shards, mesh.shape["layer"], mesh.shape["dp"]),
        mesh=mesh,
        in_specs=(
            P(None, "dp", None),
            P(None, "dp", None),
            P("layer", None, "dp"),
            P("layer", "dp"),
            P(None, "dp", None),
            P(None, "dp", None),
            P(None, "dp"),
        ),
        out_specs=(
            P("layer", None, "dp"),
            P("layer", "dp"),
            P("dp", None, "layer"),
            P(None, "dp", None),
        ),
        check_vma=False,
    )
```

```python
import functools
import jax
import jax.numpy as jnp
from jax import lax
from jax.experimental import pallas as pl
from jax.experimental.pallas import tpu as pltpu
from jax.sharding import PartitionSpec as P

BF16 = jnp.bfloat16
F32 = jnp.float32
LANES = 128
SHIFT = 256
EMPTY = 512
STREAM_MIB = 60
KERNEL_MIB = 16


def grant(mib=KERNEL_MIB):
    return pltpu.CompilerParams(vmem_limit_bytes=mib << 20)


def cost(flops, moved):
    return pl.CostEstimate(flops=flops, bytes_accessed=moved, transcendentals=0)


def lane_pick(table, where):
    return jnp.take_along_axis(table, where, axis=1, mode="promise_in_bounds")


def turn(source_ref, out_ref, layer, base):
    dests = out_ref.shape[0]
    cols = source_ref.shape[2] // dests
    turned = source_ref[layer].T
    for dest in range(dests):
        out_ref[dest, base + layer * cols : base + (layer + 1) * cols, :] = turned[dest * cols : (dest + 1) * cols]


def kept_slots(start_ref, idx_ref, live_ref, layer, lat_width):
    slots, tokens = idx_ref.shape[1:]
    place = lax.broadcasted_iota(jnp.int32, (slots, tokens), 0)
    local = idx_ref[layer] - start_ref[0]
    inside = (place < live_ref[layer : layer + 1, :]) & (local >= 0) & (local < lat_width)
    return place, local, inside


def pack_kernel(lat_width, start_ref, cot_ref, res_ref, idx_ref, live_ref, out_ref, rank_ref, slot_ref):
    slots, tokens = idx_ref.shape[1:]
    dests = out_ref.shape[0]
    cols = cot_ref.shape[2] // dests
    rows = res_ref.shape[1]

    @pl.when(pl.program_id(0) == 0)
    def _():
        found = []
        for layer in range(2):
            place, local, inside = kept_slots(start_ref, idx_ref, live_ref, layer, lat_width)
            key = jnp.where(inside, local, 1 << 20)
            rank = jnp.zeros((slots, tokens), jnp.int32)
            for slot in range(slots):
                rank = rank + jnp.where(key[slot : slot + 1, :] < key, 1, 0)
            rank = jnp.where(inside, rank, slots)
            rank_ref[layer] = rank
            key = local - SHIFT
            held = jnp.full((slots, tokens), EMPTY, jnp.int32)
            for slot in range(slots):
                held = jnp.where(rank[slot : slot + 1, :] == place, key[slot : slot + 1, :], held)
            found.append(held.astype(F32))
        slot_ref[...] = jnp.concatenate(found, axis=0).T.astype(BF16)

    more = 4 * rows
    for layer in range(2):
        turn(cot_ref, out_ref, layer, more)
    for dest in range(dests):
        out_ref[dest, more + 2 * cols :, :] = slot_ref[...]
        for layer in range(2):
            piece = res_ref[layer, :, dest * cols : (dest + 1) * cols]
            out_ref[dest, 2 * layer * rows : (2 * layer + 1) * rows, :] = piece[:, 0:LANES]
            rest = jnp.concatenate([piece[:, LANES:], jnp.zeros((rows, 2 * LANES - cols), BF16)], axis=1)
            out_ref[dest, (2 * layer + 1) * rows : (2 * layer + 2) * rows, :] = rest


def pack(lat_width, parts, members, start, cotangent, residual, index, live):
    _, tokens, width = cotangent.shape
    slots = index.shape[1]
    steps = 4
    share = tokens // members
    rows = 2 * (width // parts) + tokens + 4 * share
    return pl.pallas_call(
        functools.partial(pack_kernel, lat_width),
        grid_spec=pltpu.PrefetchScalarGridSpec(
            num_scalar_prefetch=1,
            grid=(steps,),
            in_specs=[
                pl.BlockSpec((2, tokens, width // steps), lambda i, own: (0, 0, i)),
                pl.BlockSpec((2, share, width // steps), lambda i, own: (0, own[1], i)),
                pl.BlockSpec((2, slots, tokens), lambda i, own: (0, 0, 0)),
                pl.BlockSpec((2, tokens), lambda i, own: (0, 0)),
            ],
            out_specs=[
                pl.BlockSpec((parts // steps, rows, tokens), lambda i, own: (i, 0, 0)),
                pl.BlockSpec((2, slots, tokens), lambda i, own: (0, 0, 0)),
            ],
            scratch_shapes=[pltpu.VMEM((tokens, LANES), BF16)],
        ),
        out_shape=[
            jax.ShapeDtypeStruct((parts, rows, tokens), BF16),
            jax.ShapeDtypeStruct((2, slots, tokens), jnp.int32),
        ],
        compiler_params=grant(STREAM_MIB),
        cost_estimate=cost(0, 5 << 20),
    )(start, cotangent, residual, index, live)


def values_kernel(rank_ref, val_ref, out_ref):
    slots, tokens = val_ref.shape[1:]
    place = lax.broadcasted_iota(jnp.int32, (slots, tokens), 0)
    codes = []
    for layer in range(2):
        rank = rank_ref[layer]
        value = val_ref[layer].astype(F32)
        code = jnp.zeros((slots, tokens), F32)
        for slot in range(slots):
            code = jnp.where(rank[slot : slot + 1, :] == place, value[slot : slot + 1, :], code)
        codes.append(code)
    out_ref[...] = jnp.concatenate(codes, axis=0).T.astype(BF16)


def slot_values(rank, value):
    return pl.pallas_call(
        values_kernel,
        out_shape=jax.ShapeDtypeStruct((value.shape[2], LANES), BF16),
        compiler_params=grant(),
        cost_estimate=cost(0, 1 << 20),
    )(rank, value)


def terms_kernel(more, wf_ref, ws_ref, val_ref, got_ref, out_ref, weight_ref):
    shards, _, tokens = got_ref.shape
    cols, lat_width = ws_ref.shape

    @pl.when(pl.program_id(0) == 0)
    def _():
        weight_ref[0:cols, 0:lat_width] = wf_ref[0]
        weight_ref[cols : 2 * cols, 0:lat_width] = wf_ref[1]
        weight_ref[0:cols, lat_width:] = jnp.zeros((cols, lat_width), BF16)
        weight_ref[cols : 2 * cols, lat_width:] = ws_ref[...]

    for shard in range(shards):
        dense = lax.dot_general(
            got_ref[shard, more : more + 2 * cols, :].T,
            weight_ref[...],
            (((1,), (0,)), ((), ())),
            preferred_element_type=F32,
        )
        held = got_ref[shard, more + 2 * cols :, :].astype(F32).astype(jnp.int32) + SHIFT
        lane = lax.broadcasted_iota(jnp.int32, held.shape, 1)
        chunks = lat_width // LANES
        chunk = jnp.where(
            held < lat_width, (held >> 7) + jnp.where(lane >= LANES // 2, chunks, 0), 2 * chunks
        )
        within = held & (LANES - 1)
        picked = jnp.zeros(held.shape, F32)
        for part in range(2 * chunks):
            table = dense[:, part * LANES : (part + 1) * LANES]
            picked = jnp.where(chunk == part, lane_pick(table, within), picked)
        out_ref[shard, 0:tokens, :] = picked.astype(BF16)
        out_ref[shard, tokens:, :] = val_ref[...]


def slot_terms(first, second, values, got):
    parts, rows, tokens = got.shape
    cols, lat_width = second.shape
    shards = 2
    return pl.pallas_call(
        functools.partial(terms_kernel, rows - tokens - 2 * cols),
        grid=(parts // shards,),
        in_specs=[
            pl.BlockSpec((2, cols, lat_width), lambda i: (0, 0, 0)),
            pl.BlockSpec((cols, lat_width), lambda i: (0, 0)),
            pl.BlockSpec((tokens, LANES), lambda i: (0, 0)),
            pl.BlockSpec((shards, rows, tokens), lambda i: (i, 0, 0)),
        ],
        out_specs=pl.BlockSpec((shards, 2 * tokens, LANES), lambda i: (i, 0, 0)),
        out_shape=jax.ShapeDtypeStruct((parts, 2 * tokens, LANES), BF16),
        scratch_shapes=[pltpu.VMEM((2 * cols, 2 * lat_width), BF16)],
        compiler_params=grant(50),
        cost_estimate=cost(2 * parts * tokens * cols * 3 * lat_width, 6 << 20),
    )(first, second, values, got)


def total_kernel(got_ref, rank_ref, grad_ref, part_ref):
    tokens = grad_ref.shape[1]
    total = jnp.sum(got_ref[:, 0:tokens, :].astype(F32), axis=0)
    for dest in range(grad_ref.shape[0]):
        grad_ref[dest] = total.astype(BF16)
    turned = total.T
    slots = rank_ref.shape[1]
    for layer in range(2):
        rank = rank_ref[layer]
        part = jnp.zeros(rank.shape, F32)
        for slot in range(slots):
            row = layer * slots + slot
            part = jnp.where(rank == slot, turned[row : row + 1, :], part)
        part_ref[layer] = part.astype(BF16)


def slot_totals(got, rank):
    parts, rows, _ = got.shape
    return pl.pallas_call(
        total_kernel,
        out_shape=[
            jax.ShapeDtypeStruct((parts, rows // 2, LANES), BF16),
            jax.ShapeDtypeStruct(rank.shape, BF16),
        ],
        compiler_params=grant(),
        cost_estimate=cost(0, 1 << 20),
    )(got, rank)


def spots_kernel(got_ref, spot_ref, map_ref):
    shards, _, tokens = got_ref.shape
    lat_width = spot_ref.shape[2] // 2
    runs = lat_width // 8

    @pl.when(pl.program_id(0) == 0)
    def _():
        row = lax.broadcasted_iota(jnp.int32, map_ref.shape, 0)
        col = lax.broadcasted_iota(jnp.int32, map_ref.shape, 1)
        same = (row % (2 * runs)) == (col // 8)
        map_ref[...] = jnp.where(same, jnp.where(row < 2 * runs, LANES, 1), 0).astype(F32).astype(BF16)

    lane = lax.broadcasted_iota(jnp.int32, (tokens, LANES), 1)
    half = LANES // 2
    base = lane & half
    start = 8 * (lane & (half - 1)) - SHIFT
    self_bit = jnp.left_shift(1, lane & 7)
    for shard in range(shards):
        held = got_ref[shard, got_ref.shape[1] - tokens :, :].astype(F32).astype(jnp.int32)
        below = base
        for jump in (32, 16, 8, 4, 2, 1):
            further = below + jump
            below = jnp.where(lane_pick(held, further - 1) < start, further, below)
        last = base + (half - 1)
        bits = jnp.zeros((tokens, LANES), jnp.int32)
        for hop in range(8):
            spot = below if hop == 0 else jnp.minimum(below + hop, last)
            ahead = lane_pick(held, spot) - start
            bits = bits | jnp.where((ahead & -8) == 0, jnp.left_shift(1, ahead & 7), 0)
        both = jnp.concatenate([bits.astype(F32).astype(BF16), below.astype(F32).astype(BF16)], axis=1)
        spread = jnp.dot(both, map_ref[...], preferred_element_type=F32).astype(jnp.int32)
        for chunk in range(2 * lat_width // LANES):
            packed = spread[:, chunk * LANES : (chunk + 1) * LANES]
            bits = packed >> 7
            spot = (packed & (LANES - 1)) + lax.population_count(bits & (self_bit - 1))
            spot = jnp.where((bits & self_bit) != 0, spot, LANES)
            spot_ref[shard, :, chunk * LANES : (chunk + 1) * LANES] = spot.astype(F32).astype(BF16)


def slot_spots(got, lat_width):
    parts, rows, tokens = got.shape
    shards = 2
    return pl.pallas_call(
        spots_kernel,
        grid=(parts // shards,),
        in_specs=[pl.BlockSpec((shards, rows, tokens), lambda i: (i, 0, 0))],
        out_specs=pl.BlockSpec((shards, tokens, 2 * lat_width), lambda i: (i, 0, 0)),
        out_shape=jax.ShapeDtypeStruct((parts, tokens, 2 * lat_width), BF16),
        scratch_shapes=[pltpu.VMEM((2 * LANES, 2 * lat_width), BF16)],
        compiler_params=grant(56),
        cost_estimate=cost(2 * parts * tokens * 2 * LANES * 2 * lat_width, 8 << 20),
    )(got)


def dense(table_ref, first_row, spot_ref, out_ref):
    shards, tokens, width = spot_ref.shape
    for shard in range(shards):
        table = table_ref[shard, first_row : first_row + tokens, :].astype(F32)
        for chunk in range(width // LANES):
            at = slice(chunk * LANES, (chunk + 1) * LANES)
            spot = spot_ref[shard, :, at].astype(F32).astype(jnp.int32)
            found = jnp.where(spot < LANES, lane_pick(table, spot & (LANES - 1)), 0.0)
            out_ref[shard * tokens : (shard + 1) * tokens, at] = found.astype(BF16)


def codes_kernel(got_ref, val_ref, spot_ref, first_ref, second_ref, code_ref, sum_ref):
    shards, tokens, _ = spot_ref.shape
    cols, lat_width = second_ref.shape
    step = pl.program_id(0)

    @pl.when(step == 0)
    def _():
        sum_ref[...] = jnp.zeros_like(sum_ref)

    dense(val_ref, tokens, spot_ref, code_ref)
    more = got_ref.shape[1] - tokens - 2 * cols
    cot = jnp.concatenate([got_ref[shard, more : more + 2 * cols, :] for shard in range(shards)], axis=1)
    dot = functools.partial(jnp.dot, preferred_element_type=F32)
    sum_ref[0 : 2 * cols, :] += dot(cot, code_ref[:, 0:lat_width])
    sum_ref[2 * cols : 3 * cols, :] += dot(cot[cols:], code_ref[:, lat_width:])

    @pl.when(step == pl.num_programs(0) - 1)
    def _():
        first_ref[0] = sum_ref[0:cols, :].astype(BF16)
        first_ref[1] = sum_ref[cols : 2 * cols, :].astype(BF16)
        second_ref[...] = sum_ref[2 * cols : 3 * cols, :].astype(BF16)


def decoder_grads(got, slots, spots, cols, lat_width):
    parts, rows, tokens = got.shape
    shards = 4
    return pl.pallas_call(
        codes_kernel,
        grid=(parts // shards,),
        in_specs=[
            pl.BlockSpec((shards, rows, tokens), lambda i: (i, 0, 0)),
            pl.BlockSpec((shards, 2 * tokens, LANES), lambda i: (i, 0, 0)),
            pl.BlockSpec((shards, tokens, 2 * lat_width), lambda i: (i, 0, 0)),
        ],
        out_specs=[
            pl.BlockSpec((2, cols, lat_width), lambda i: (0, 0, 0)),
            pl.BlockSpec((cols, lat_width), lambda i: (0, 0)),
        ],
        out_shape=[
            jax.ShapeDtypeStruct((2, cols, lat_width), BF16),
            jax.ShapeDtypeStruct((cols, lat_width), BF16),
        ],
        scratch_shapes=[
            pltpu.VMEM((shards * tokens, 2 * lat_width), BF16),
            pltpu.VMEM((3 * cols, lat_width), F32),
        ],
        compiler_params=grant(52),
        cost_estimate=cost(2 * parts * tokens * cols * 3 * lat_width, 8 << 20),
    )(got, slots, spots)


def back_kernel(own_ref, *refs):
    res_refs, (spot_ref, grad_ref, enc_ref, back_ref, sum_ref) = refs[:-5], refs[-5:]
    members = len(res_refs)
    shards, tokens, width = spot_ref.shape
    cols, _, lat_width = enc_ref.shape
    rows = tokens // members
    step = pl.program_id(0)
    for shard in range(shards):
        for member in range(members):
            low = pl.multiple_of((own_ref[1] ^ member) * rows, rows)
            table = grad_ref[shard, pl.ds(low, rows), :].astype(F32)
            to = shard * tokens + member * rows
            for chunk in range(width // LANES):
                at = slice(chunk * LANES, (chunk + 1) * LANES)
                spot = spot_ref[shard, pl.ds(low, rows), at].astype(F32).astype(jnp.int32)
                found = jnp.where(spot < LANES, lane_pick(table, spot & (LANES - 1)), 0.0)
                back_ref[to : to + rows, at] = found.astype(BF16)

    @pl.when(step == 0)
    def _():
        sum_ref[...] = jnp.zeros_like(sum_ref)

    for layer in range(2):
        sides = []
        for side in range(2):
            low = (2 * layer + side) * rows
            pieces = [res_ref[shard, low : low + rows, :] for shard in range(shards) for res_ref in res_refs]
            sides.append(jnp.concatenate(pieces, axis=0).T)
        left = jnp.concatenate(sides, axis=0)[0:cols]
        sum_ref[layer * cols : (layer + 1) * cols, :] += jnp.dot(
            left, back_ref[:, layer * lat_width : (layer + 1) * lat_width], preferred_element_type=F32
        )

    @pl.when(step == pl.num_programs(0) - 1)
    def _():
        enc_ref[:, 0, :] = sum_ref[0:cols, :].astype(BF16)
        enc_ref[:, 1, :] = sum_ref[cols:, :].astype(BF16)


def encoder_grads(own, res, spots, grads, cols, lat_width):
    parts, tokens, _ = spots.shape
    rows = 4 * tokens // len(res)
    shards = 4
    return pl.pallas_call(
        back_kernel,
        grid=(parts // shards,),
        in_specs=[pl.BlockSpec(memory_space=pltpu.SMEM)]
        + [pl.BlockSpec((shards, rows, LANES), lambda i: (i, 0, 0)) for _ in res]
        + [
            pl.BlockSpec((shards,) + spots.shape[1:], lambda i: (i, 0, 0)),
            pl.BlockSpec((shards, tokens, LANES), lambda i: (i, 0, 0)),
        ],
        out_specs=pl.BlockSpec((cols, 2, lat_width), lambda i: (0, 0, 0)),
        out_shape=jax.ShapeDtypeStruct((cols, 2, lat_width), BF16),
        scratch_shapes=[
            pltpu.VMEM((shards * tokens, 2 * lat_width), BF16),
            pltpu.VMEM((2 * cols, lat_width), F32),
        ],
        compiler_params=grant(50),
        cost_estimate=cost(2 * parts * tokens * cols * 2 * lat_width, 8 << 20),
    )(own, *res, spots, grads)


def exchange(array, axis):
    return lax.all_to_all(array, axis, 0, 0, tiled=True)


def from_hops(array, axis, size, hops):
    return [lax.ppermute(array, axis, [(at, at ^ hop) for at in range(size)]) for hop in hops]


def shards(layers, parts, residual, cotangent, decoder_first, decoder_second, latent_index, latent_value, active_count):
    lat_width = decoder_first.shape[0]
    cols = decoder_second.shape[1]
    tokens = residual.shape[1]
    members = 4
    place = lax.axis_index("layer")
    own = jnp.stack([place * lat_width, place % members]).astype(jnp.int32)
    index, value = latent_index.transpose(0, 2, 1), latent_value.transpose(0, 2, 1)
    packed, rank = pack(lat_width, parts, members, own, cotangent, residual, index, active_count)
    values = slot_values(rank, value)
    got = exchange(packed, "dp")
    share = got[:, : 4 * tokens // members, :]
    res_near, res_next = from_hops(share, "layer", layers, (1, 2))
    terms = slot_terms(decoder_first.transpose(1, 2, 0), decoder_second.T, values, got)
    slots = exchange(terms, "dp")
    spots = slot_spots(got, lat_width)
    slots, spots, res_next = lax.optimization_barrier((slots, spots, res_next))
    grads, part = slot_totals(slots, rank)
    grads, res_near = lax.optimization_barrier((grads, res_near))
    (res_last,) = from_hops(res_near, "layer", layers, (2,))
    all_grads = exchange(grads, "dp")
    first_grad, second_grad = decoder_grads(got, slots, spots, cols, lat_width)
    part = functools.reduce(jnp.add, from_hops(part, "layer", layers, (1, 2, 3)), part)
    all_grads, first_grad, part = lax.optimization_barrier((all_grads, first_grad, part))
    res = [got, res_near, res_next, res_last]
    encoder_grad = encoder_grads(own, res, spots, all_grads, cols, lat_width)
    far = from_hops(part, "layer", layers, (4, 8, 12))
    *far, encoder_grad = lax.optimization_barrier((*far, encoder_grad))
    latent_grad = functools.reduce(jnp.add, far, part)
    return (
        first_grad.transpose(2, 0, 1),
        second_grad.T,
        encoder_grad,
        latent_grad.astype(F32).transpose(0, 2, 1),
    )


def solution(mesh):
    return jax.shard_map(
        functools.partial(shards, mesh.shape["layer"], mesh.shape["dp"]),
        mesh=mesh,
        in_specs=(
            P(None, "dp", None),
            P(None, "dp", None),
            P("layer", None, "dp"),
            P("layer", "dp"),
            P(None, "dp", None),
            P(None, "dp", None),
            P(None, "dp"),
        ),
        out_specs=(
            P("layer", None, "dp"),
            P("layer", "dp"),
            P("dp", None, "layer"),
            P(None, "dp", None),
        ),
        check_vma=False,
    )
```

```python
import functools
import jax
import jax.numpy as jnp
from jax import lax
from jax.experimental import pallas as pl
from jax.experimental.pallas import tpu as pltpu
from jax.sharding import PartitionSpec as P

BF16 = jnp.bfloat16
F32 = jnp.float32
LANES = 128
RUNS = LANES // 2
SHIFT = 256
EMPTY = 512
STREAM_MIB = 60
KERNEL_MIB = 16
SPOTS_FLOPS = 1 << 32


def grant(mib=KERNEL_MIB):
    return pltpu.CompilerParams(vmem_limit_bytes=mib << 20)


def cost(flops, moved):
    return pl.CostEstimate(flops=flops, bytes_accessed=moved, transcendentals=0)


def lane_pick(table, where):
    return jnp.take_along_axis(table, where, axis=1, mode="promise_in_bounds")


def turn(source_ref, out_ref, layer, base):
    dests = out_ref.shape[0]
    cols = source_ref.shape[2] // dests
    turned = source_ref[layer].T
    for dest in range(dests):
        out_ref[dest, base + layer * cols : base + (layer + 1) * cols, :] = turned[dest * cols : (dest + 1) * cols]


def kept_slots(start_ref, idx_ref, live_ref, layer, lat_width):
    slots, tokens = idx_ref.shape[1:]
    place = lax.broadcasted_iota(jnp.int32, (slots, tokens), 0)
    local = idx_ref[layer] - start_ref[0]
    inside = (place < live_ref[layer : layer + 1, :]) & (local >= 0) & (local < lat_width)
    return place, local, inside


def pack_kernel(lat_width, start_ref, cot_ref, res_ref, idx_ref, live_ref, out_ref, rank_ref, slot_ref):
    slots, tokens = idx_ref.shape[1:]
    dests = out_ref.shape[0]
    cols = cot_ref.shape[2] // dests
    rows = res_ref.shape[1]

    @pl.when(pl.program_id(0) == 0)
    def _():
        found = []
        for layer in range(2):
            place, local, inside = kept_slots(start_ref, idx_ref, live_ref, layer, lat_width)
            key = (local & (RUNS - 1)) * 8 + (local >> 6)
            held_key = key - SHIFT
            key = jnp.where(inside, key, 1 << 20)
            rank = jnp.zeros((slots, tokens), jnp.int32)
            for slot in range(slots):
                rank = rank + jnp.where(key[slot : slot + 1, :] < key, 1, 0)
            rank = jnp.where(inside, rank, slots)
            rank_ref[layer] = rank
            held = jnp.full((slots, tokens), EMPTY, jnp.int32)
            for slot in range(slots):
                held = jnp.where(rank[slot : slot + 1, :] == place, held_key[slot : slot + 1, :], held)
            found.append(held.astype(F32))
        slot_ref[...] = jnp.concatenate(found, axis=0).T.astype(BF16)

    more = 4 * rows
    for layer in range(2):
        turn(cot_ref, out_ref, layer, more)
    for dest in range(dests):
        out_ref[dest, more + 2 * cols :, :] = slot_ref[...]
        for layer in range(2):
            piece = res_ref[layer, :, dest * cols : (dest + 1) * cols]
            out_ref[dest, 2 * layer * rows : (2 * layer + 1) * rows, :] = piece[:, 0:LANES]
            rest = jnp.concatenate([piece[:, LANES:], jnp.zeros((rows, 2 * LANES - cols), BF16)], axis=1)
            out_ref[dest, (2 * layer + 1) * rows : (2 * layer + 2) * rows, :] = rest


def pack(lat_width, parts, members, start, cotangent, residual, index, live):
    _, tokens, width = cotangent.shape
    slots = index.shape[1]
    steps = 4
    share = tokens // members
    rows = 2 * (width // parts) + tokens + 4 * share
    return pl.pallas_call(
        functools.partial(pack_kernel, lat_width),
        grid_spec=pltpu.PrefetchScalarGridSpec(
            num_scalar_prefetch=1,
            grid=(steps,),
            in_specs=[
                pl.BlockSpec((2, tokens, width // steps), lambda i, own: (0, 0, i)),
                pl.BlockSpec((2, share, width // steps), lambda i, own: (0, own[1], i)),
                pl.BlockSpec((2, slots, tokens), lambda i, own: (0, 0, 0)),
                pl.BlockSpec((2, tokens), lambda i, own: (0, 0)),
            ],
            out_specs=[
                pl.BlockSpec((parts // steps, rows, tokens), lambda i, own: (i, 0, 0)),
                pl.BlockSpec((2, slots, tokens), lambda i, own: (0, 0, 0)),
            ],
            scratch_shapes=[pltpu.VMEM((tokens, LANES), BF16)],
        ),
        out_shape=[
            jax.ShapeDtypeStruct((parts, rows, tokens), BF16),
            jax.ShapeDtypeStruct((2, slots, tokens), jnp.int32),
        ],
        compiler_params=grant(STREAM_MIB),
        cost_estimate=cost(0, 5 << 20),
    )(start, cotangent, residual, index, live)


def values_kernel(rank_ref, val_ref, out_ref):
    slots, tokens = val_ref.shape[1:]
    place = lax.broadcasted_iota(jnp.int32, (slots, tokens), 0)
    codes = []
    for layer in range(2):
        rank = rank_ref[layer]
        value = val_ref[layer].astype(F32)
        code = jnp.zeros((slots, tokens), F32)
        for slot in range(slots):
            code = jnp.where(rank[slot : slot + 1, :] == place, value[slot : slot + 1, :], code)
        codes.append(code)
    out_ref[...] = jnp.concatenate(codes, axis=0).T.astype(BF16)


def slot_values(rank, value):
    return pl.pallas_call(
        values_kernel,
        out_shape=jax.ShapeDtypeStruct((value.shape[2], LANES), BF16),
        compiler_params=grant(),
        cost_estimate=cost(0, 1 << 20),
    )(rank, value)


def terms_kernel(more, wf_ref, ws_ref, val_ref, got_ref, out_ref, share_ref, weight_ref):
    shards, _, tokens = got_ref.shape
    cols, lat_width = ws_ref.shape

    @pl.when(pl.program_id(0) == 0)
    def _():
        weight_ref[0:cols, 0:lat_width] = wf_ref[0]
        weight_ref[cols : 2 * cols, 0:lat_width] = wf_ref[1]
        weight_ref[0:cols, lat_width:] = jnp.zeros((cols, lat_width), BF16)
        weight_ref[cols : 2 * cols, lat_width:] = ws_ref[...]

    share_ref[...] = got_ref[:, 0:more, :]
    pair = 2
    for first in range(0, shards, pair):
        some = range(first, first + pair)
        cot = jnp.concatenate([got_ref[shard, more : more + 2 * cols, :] for shard in some], axis=1)
        dense = jnp.dot(cot.T, weight_ref[...], preferred_element_type=F32)
        held = jnp.concatenate([got_ref[shard, more + 2 * cols :, :] for shard in some], axis=0)
        held = held.astype(F32).astype(jnp.int32) + SHIFT
        lane = lax.broadcasted_iota(jnp.int32, held.shape, 1)
        chunks = lat_width // LANES
        chunk = ((held & 7) >> 1) + jnp.where(lane >= RUNS, chunks, 0)
        chunk = jnp.where(held < lat_width, chunk, 2 * chunks)
        within = jnp.where((held & 1) == 1, RUNS, 0) + (held >> 3)
        picked = jnp.zeros(held.shape, F32)
        for part in range(2 * chunks):
            table = dense[:, part * LANES : (part + 1) * LANES]
            picked = jnp.where(chunk == part, lane_pick(table, within), picked)
        for shard in some:
            out_ref[shard, 0:tokens, :] = picked[(shard - first) * tokens : (shard - first + 1) * tokens].astype(BF16)
            out_ref[shard, tokens:, :] = val_ref[...]


def slot_terms(first, second, values, got):
    parts, rows, tokens = got.shape
    cols, lat_width = second.shape
    more = rows - tokens - 2 * cols
    shards = 4
    return pl.pallas_call(
        functools.partial(terms_kernel, more),
        grid=(parts // shards,),
        in_specs=[
            pl.BlockSpec((2, cols, lat_width), lambda i: (0, 0, 0)),
            pl.BlockSpec((cols, lat_width), lambda i: (0, 0)),
            pl.BlockSpec((tokens, LANES), lambda i: (0, 0)),
            pl.BlockSpec((shards, rows, tokens), lambda i: (i, 0, 0)),
        ],
        out_specs=[
            pl.BlockSpec((shards, 2 * tokens, LANES), lambda i: (i, 0, 0)),
            pl.BlockSpec((shards, more, tokens), lambda i: (i, 0, 0)),
        ],
        out_shape=[
            jax.ShapeDtypeStruct((parts, 2 * tokens, LANES), BF16),
            jax.ShapeDtypeStruct((parts, more, tokens), BF16),
        ],
        scratch_shapes=[pltpu.VMEM((2 * cols, 2 * lat_width), BF16)],
        compiler_params=grant(50),
        cost_estimate=cost(2 * parts * tokens * cols * 3 * lat_width, 6 << 20),
    )(first, second, values, got)


def total_kernel(got_ref, rank_ref, grad_ref, part_ref):
    tokens = grad_ref.shape[1]
    total = jnp.sum(got_ref[:, 0:tokens, :].astype(F32), axis=0)
    for dest in range(grad_ref.shape[0]):
        grad_ref[dest] = total.astype(BF16)
    turned = total.T
    slots = rank_ref.shape[1]
    for layer in range(2):
        rank = rank_ref[layer]
        part = jnp.zeros(rank.shape, F32)
        for slot in range(slots):
            row = layer * slots + slot
            part = jnp.where(rank == slot, turned[row : row + 1, :], part)
        part_ref[layer] = part.astype(BF16)


def slot_totals(got, rank):
    parts, rows, _ = got.shape
    return pl.pallas_call(
        total_kernel,
        out_shape=[
            jax.ShapeDtypeStruct((parts, rows // 2, LANES), BF16),
            jax.ShapeDtypeStruct(rank.shape, BF16),
        ],
        compiler_params=grant(),
        cost_estimate=cost(0, 1 << 20),
    )(got, rank)


FEW = ((8, 4, 2, 1), 3)
ALL = ((32, 16, 8, 4, 2, 1), 8)


def spots_kernel(got_ref, spot_ref):
    shards, _, tokens = got_ref.shape
    top = got_ref.shape[1] - tokens
    lane = lax.broadcasted_iota(jnp.int32, (tokens, LANES), 1)
    place = lane & (RUNS - 1)
    base = lane & RUNS
    last = base + (RUNS - 1)
    start = 8 * place - SHIFT

    def fill(jumps, hops):
        for shard in range(shards):
            held = got_ref[shard, top:, :].astype(F32).astype(jnp.int32)
            below = base
            for jump in jumps:
                further = below + jump
                below = jnp.where(lane_pick(held, further - 1) < start, further, below)
            codes = jnp.zeros((tokens, LANES), jnp.int32)
            for hop in range(hops):
                spot = below if hop == 0 else jnp.minimum(below + hop, last)
                ahead = lane_pick(held, spot) - start
                code = jnp.where((ahead & -8) == 0, ahead + 1, 0)
                if hop > 0:
                    code = jnp.where(below + hop <= last, code, 0)
                codes = codes | jnp.left_shift(code, 4 * hop)
            spot_ref[shard, 0:tokens, :] = below
            spot_ref[shard, tokens:, :] = codes

    deep = jnp.zeros((tokens, LANES), jnp.int32)
    for shard in range(shards):
        held = got_ref[shard, top:, :].astype(F32).astype(jnp.int32)
        ahead = pltpu.roll(held, LANES - FEW[1], 1)
        crowd = ((held >> 3) == (ahead >> 3)) & (place < RUNS - FEW[1])
        many = place == sum(FEW[0])
        deep = jnp.where((held < EMPTY) & (crowd | many), 1, deep)
    deep = jnp.max(deep)

    @pl.when(deep == 0)
    def _():
        fill(*FEW)

    @pl.when(deep != 0)
    def _():
        fill(*ALL)


def slot_spots(got):
    parts, rows, tokens = got.shape
    shards = 2
    return pl.pallas_call(
        spots_kernel,
        grid=(parts // shards,),
        in_specs=[pl.BlockSpec((shards, rows, tokens), lambda i: (i, 0, 0))],
        out_specs=pl.BlockSpec((shards, 2 * tokens, LANES), lambda i: (i, 0, 0)),
        out_shape=jax.ShapeDtypeStruct((parts, 2 * tokens, LANES), jnp.int32),
        compiler_params=grant(56),
        cost_estimate=cost(SPOTS_FLOPS, 8 << 20),
    )(got)


def dense(table, below, codes, hops):
    rows = below.shape[0]
    lane = lax.broadcasted_iota(jnp.int32, (rows, LANES), 1)
    near = lane < RUNS
    far_codes = pltpu.roll(codes, RUNS, 1)
    out = [jnp.zeros((rows, LANES), F32) for _ in range(8)]
    for hop in range(hops):
        spot = below if hop == 0 else jnp.minimum(below + hop, LANES - 1)
        value = lane_pick(table, spot)
        far_value = pltpu.roll(value, RUNS, 1)
        code = (codes >> (4 * hop)) & 15
        far_code = (far_codes >> (4 * hop)) & 15
        for layer, (kept, moved, one, two) in enumerate(
            ((value, far_value, code, far_code - 1), (far_value, value, far_code, code - 1))
        ):
            kept = jnp.where(near, kept, moved)
            which = jnp.where(near, one, two)
            for chunk in range(4):
                at = 4 * layer + chunk
                out[at] = jnp.where(which == 2 * chunk + 1, kept, out[at])
    return out


def fill_dense(table_ref, spot_ref, out_ref, row_of):
    shards, tokens = spot_ref.shape[0], spot_ref.shape[1] // 2
    block = 16
    crowd = jnp.zeros((tokens, LANES), jnp.int32)
    for shard in range(shards):
        crowd = jnp.where((spot_ref[shard, tokens:, :] >> (4 * FEW[1])) != 0, 1, crowd)
    crowd = jnp.max(crowd)

    def fill(hops, shard, part):
        low = row_of(part * block)
        table = table_ref[shard, pl.ds(low, block), :].astype(F32)
        below = spot_ref[shard, pl.ds(low, block), :]
        codes = spot_ref[shard, pl.ds(low + tokens, block), :]
        to = pl.multiple_of(shard * tokens + part * block, block)
        for chunk, found in enumerate(dense(table, below, codes, hops)):
            out_ref[pl.ds(to, block), chunk * LANES : (chunk + 1) * LANES] = found.astype(BF16)

    @pl.when(crowd == 0)
    def _():
        for shard in range(shards):
            for part in range(tokens // block):
                fill(FEW[1], shard, part)

    @pl.when(crowd != 0)
    def _():
        def one(at, carry):
            fill(ALL[1], at // (tokens // block), at % (tokens // block))
            return carry

        lax.fori_loop(0, shards * tokens // block, one, 0)


def codes_kernel(got_ref, val_ref, spot_ref, first_ref, second_ref, code_ref, sum_ref):
    shards, tokens = spot_ref.shape[0], spot_ref.shape[1] // 2
    cols, lat_width = second_ref.shape
    step = pl.program_id(0)

    @pl.when(step == 0)
    def _():
        sum_ref[...] = jnp.zeros_like(sum_ref)

    fill_dense(val_ref, spot_ref, code_ref, lambda row: row)
    more = got_ref.shape[1] - tokens - 2 * cols
    cot = jnp.concatenate([got_ref[shard, more : more + 2 * cols, :] for shard in range(shards)], axis=1)
    dot = functools.partial(jnp.dot, preferred_element_type=F32)
    sum_ref[0 : 2 * cols, :] += dot(cot, code_ref[:, 0:lat_width])
    sum_ref[2 * cols : 3 * cols, :] += dot(cot[cols:], code_ref[:, lat_width:])

    @pl.when(step == pl.num_programs(0) - 1)
    def _():
        first_ref[0] = sum_ref[0:cols, :].astype(BF16)
        first_ref[1] = sum_ref[cols : 2 * cols, :].astype(BF16)
        second_ref[...] = sum_ref[2 * cols : 3 * cols, :].astype(BF16)


def decoder_grads(got, slots, spots, cols, lat_width):
    parts, rows, tokens = got.shape
    shards = 4
    return pl.pallas_call(
        codes_kernel,
        grid=(parts // shards,),
        in_specs=[
            pl.BlockSpec((shards, rows, tokens), lambda i: (i, 0, 0)),
            pl.BlockSpec((shards, tokens, LANES), lambda i: (i, 1, 0)),
            pl.BlockSpec((shards, 2 * tokens, LANES), lambda i: (i, 0, 0)),
        ],
        out_specs=[
            pl.BlockSpec((2, cols, lat_width), lambda i: (0, 0, 0)),
            pl.BlockSpec((cols, lat_width), lambda i: (0, 0)),
        ],
        out_shape=[
            jax.ShapeDtypeStruct((2, cols, lat_width), BF16),
            jax.ShapeDtypeStruct((cols, lat_width), BF16),
        ],
        scratch_shapes=[
            pltpu.VMEM((shards * tokens, 2 * lat_width), BF16),
            pltpu.VMEM((3 * cols, lat_width), F32),
        ],
        compiler_params=grant(52),
        cost_estimate=cost(2 * parts * tokens * cols * 3 * lat_width, 8 << 20),
    )(got, slots, spots)


def back_kernel(own_ref, *refs):
    res_refs, (spot_ref, grad_ref, enc_ref, back_ref, sum_ref) = refs[:-5], refs[-5:]
    members = len(res_refs)
    shards, tokens = spot_ref.shape[0], spot_ref.shape[1] // 2
    cols, _, lat_width = enc_ref.shape
    rows = tokens // members
    step = pl.program_id(0)

    def row_of(row):
        return pl.multiple_of((own_ref[1] ^ (row // rows)) * rows + row % rows, 16)

    fill_dense(grad_ref, spot_ref, back_ref, row_of)

    @pl.when(step == 0)
    def _():
        sum_ref[...] = jnp.zeros_like(sum_ref)

    for layer in range(2):
        sides = []
        for side in range(2):
            low = (2 * layer + side) * rows
            pieces = [res_ref[shard, low : low + rows, :] for shard in range(shards) for res_ref in res_refs]
            sides.append(jnp.concatenate(pieces, axis=0).T)
        left = jnp.concatenate(sides, axis=0)[0:cols]
        sum_ref[layer * cols : (layer + 1) * cols, :] += jnp.dot(
            left, back_ref[:, layer * lat_width : (layer + 1) * lat_width], preferred_element_type=F32
        )

    @pl.when(step == pl.num_programs(0) - 1)
    def _():
        enc_ref[:, 0, :] = sum_ref[0:cols, :].astype(BF16)
        enc_ref[:, 1, :] = sum_ref[cols:, :].astype(BF16)


def encoder_grads(own, res, spots, grads, cols, lat_width):
    parts, tokens, _ = grads.shape
    rows = 4 * tokens // len(res)
    shards = 4
    return pl.pallas_call(
        back_kernel,
        grid=(parts // shards,),
        in_specs=[pl.BlockSpec(memory_space=pltpu.SMEM)]
        + [pl.BlockSpec((shards, rows, LANES), lambda i: (i, 0, 0)) for _ in res]
        + [
            pl.BlockSpec((shards,) + spots.shape[1:], lambda i: (i, 0, 0)),
            pl.BlockSpec((shards, tokens, LANES), lambda i: (i, 0, 0)),
        ],
        out_specs=pl.BlockSpec((cols, 2, lat_width), lambda i: (0, 0, 0)),
        out_shape=jax.ShapeDtypeStruct((cols, 2, lat_width), BF16),
        scratch_shapes=[
            pltpu.VMEM((shards * tokens, 2 * lat_width), BF16),
            pltpu.VMEM((2 * cols, lat_width), F32),
        ],
        compiler_params=grant(50),
        cost_estimate=cost(2 * parts * tokens * cols * 2 * lat_width, 8 << 20),
    )(own, *res, spots, grads)


def exchange(array, axis):
    return lax.all_to_all(array, axis, 0, 0, tiled=True)


def from_hops(array, axis, size, hops):
    return [lax.ppermute(array, axis, [(at, at ^ hop) for at in range(size)]) for hop in hops]


def shards(layers, parts, residual, cotangent, decoder_first, decoder_second, latent_index, latent_value, active_count):
    lat_width = decoder_first.shape[0]
    cols = decoder_second.shape[1]
    tokens = residual.shape[1]
    members = 4
    place = lax.axis_index("layer")
    own = jnp.stack([place * lat_width, place % members]).astype(jnp.int32)
    index, value = latent_index.transpose(0, 2, 1), latent_value.transpose(0, 2, 1)
    packed, rank = pack(lat_width, parts, members, own, cotangent, residual, index, active_count)
    values = slot_values(rank, value)
    got = exchange(packed, "dp")
    terms, share = slot_terms(decoder_first.transpose(1, 2, 0), decoder_second.T, values, got)
    res_near, res_next = from_hops(share, "layer", layers, (1, 2))
    slots = exchange(terms, "dp")
    spots = slot_spots(got)
    slots, spots, res_next = lax.optimization_barrier((slots, spots, res_next))
    grads, part = slot_totals(slots, rank)
    grads, res_near = lax.optimization_barrier((grads, res_near))
    (res_last,) = from_hops(res_near, "layer", layers, (2,))
    all_grads = exchange(grads, "dp")
    first_grad, second_grad = decoder_grads(got, slots, spots, cols, lat_width)
    part = functools.reduce(jnp.add, from_hops(part, "layer", layers, (1, 2, 3)), part)
    all_grads, first_grad, part = lax.optimization_barrier((all_grads, first_grad, part))
    res = [share, res_near, res_next, res_last]
    encoder_grad = encoder_grads(own, res, spots, all_grads, cols, lat_width)
    far = from_hops(part, "layer", layers, (4, 8, 12))
    *far, encoder_grad = lax.optimization_barrier((*far, encoder_grad))
    latent_grad = functools.reduce(jnp.add, far, part)
    return (
        first_grad.transpose(2, 0, 1),
        second_grad.T,
        encoder_grad,
        latent_grad.astype(F32).transpose(0, 2, 1),
    )


def solution(mesh):
    return jax.shard_map(
        functools.partial(shards, mesh.shape["layer"], mesh.shape["dp"]),
        mesh=mesh,
        in_specs=(
            P(None, "dp", None),
            P(None, "dp", None),
            P("layer", None, "dp"),
            P("layer", "dp"),
            P(None, "dp", None),
            P(None, "dp", None),
            P(None, "dp"),
        ),
        out_specs=(
            P("layer", None, "dp"),
            P("layer", "dp"),
            P("dp", None, "layer"),
            P(None, "dp", None),
        ),
        check_vma=False,
    )
```

```python
import functools
import jax
import jax.numpy as jnp
from jax import lax
from jax.experimental import pallas as pl
from jax.experimental.pallas import tpu as pltpu
from jax.sharding import PartitionSpec as P

BF16 = jnp.bfloat16
F32 = jnp.float32
LANES = 128
RUNS = LANES // 2
SHIFT = 256
EMPTY = 512
STREAM_MIB = 60
KERNEL_MIB = 16
SPOTS_FLOPS = 1 << 32


def grant(mib=KERNEL_MIB):
    return pltpu.CompilerParams(vmem_limit_bytes=mib << 20)


def cost(flops, moved):
    return pl.CostEstimate(flops=flops, bytes_accessed=moved, transcendentals=0)


def lane_pick(table, where):
    return jnp.take_along_axis(table, where, axis=1, mode="promise_in_bounds")


def turn(source, out_ref, base):
    dests = out_ref.shape[0]
    cols = source.shape[1] // dests
    turned = source.T
    for dest in range(dests):
        out_ref[dest, base : base + cols, :] = turned[dest * cols : (dest + 1) * cols]


def kept_slots(own_ref, idx_ref, live_ref, layer, lat_width):
    slots, tokens = idx_ref.shape[1:]
    place = lax.broadcasted_iota(jnp.int32, (slots, tokens), 0)
    local = idx_ref[layer] - own_ref[0]
    inside = (place < live_ref[layer : layer + 1, :]) & (local >= 0) & (local < lat_width)
    return place, local, inside


def pack_kernel(lat_width, own_ref, cot_ref, res_ref, idx_ref, live_ref, out_ref, rank_ref, slot_ref):
    slots, tokens = idx_ref.shape[1:]
    dests = out_ref.shape[0]
    cols = cot_ref.shape[2] // dests

    @pl.when(pl.program_id(0) == 0)
    def _():
        found = []
        for layer in range(2):
            place, local, inside = kept_slots(own_ref, idx_ref, live_ref, layer, lat_width)
            key = (local & (RUNS - 1)) * 8 + (local >> 6)
            held_key = key - SHIFT
            key = jnp.where(inside, key, 1 << 20)
            rank = jnp.zeros((slots, tokens), jnp.int32)
            for slot in range(slots):
                rank = rank + jnp.where(key[slot : slot + 1, :] < key, 1, 0)
            rank = jnp.where(inside, rank, slots)
            rank_ref[layer] = rank
            held = jnp.full((slots, tokens), EMPTY, jnp.int32)
            for slot in range(slots):
                held = jnp.where(rank[slot : slot + 1, :] == place, held_key[slot : slot + 1, :], held)
            found.append(held.astype(F32))
        slot_ref[...] = jnp.concatenate(found, axis=0).T.astype(BF16)

    for layer in range(2):
        turn(cot_ref[layer], out_ref, (1 + layer) * cols)
    turn(jnp.concatenate([res_ref[own_ref[1]], res_ref[1 - own_ref[1]]], axis=0), out_ref, 0)
    for dest in range(dests):
        out_ref[dest, 3 * cols :, :] = slot_ref[...]


def pack(lat_width, parts, members, start, cotangent, residual, index, live):
    _, tokens, width = cotangent.shape
    slots = index.shape[1]
    steps = 4
    share = tokens // members
    rows = 3 * (width // parts) + tokens
    return pl.pallas_call(
        functools.partial(pack_kernel, lat_width),
        grid_spec=pltpu.PrefetchScalarGridSpec(
            num_scalar_prefetch=1,
            grid=(steps,),
            in_specs=[
                pl.BlockSpec((2, tokens, width // steps), lambda i, own: (0, 0, i)),
                pl.BlockSpec((2, share, width // steps), lambda i, own: (0, own[1], i)),
                pl.BlockSpec((2, slots, tokens), lambda i, own: (0, 0, 0)),
                pl.BlockSpec((2, tokens), lambda i, own: (0, 0)),
            ],
            out_specs=[
                pl.BlockSpec((parts // steps, rows, tokens), lambda i, own: (i, 0, 0)),
                pl.BlockSpec((2, slots, tokens), lambda i, own: (0, 0, 0)),
            ],
            scratch_shapes=[pltpu.VMEM((tokens, LANES), BF16)],
        ),
        out_shape=[
            jax.ShapeDtypeStruct((parts, rows, tokens), BF16),
            jax.ShapeDtypeStruct((2, slots, tokens), jnp.int32),
        ],
        compiler_params=grant(STREAM_MIB),
        cost_estimate=cost(0, 5 << 20),
    )(start, cotangent, residual, index, live)


def values_kernel(rank_ref, val_ref, out_ref):
    slots, tokens = val_ref.shape[1:]
    place = lax.broadcasted_iota(jnp.int32, (slots, tokens), 0)
    codes = []
    for layer in range(2):
        rank = rank_ref[layer]
        value = val_ref[layer].astype(F32)
        code = jnp.zeros((slots, tokens), F32)
        for slot in range(slots):
            code = jnp.where(rank[slot : slot + 1, :] == place, value[slot : slot + 1, :], code)
        codes.append(code)
    out_ref[...] = jnp.concatenate(codes, axis=0).T.astype(BF16)


def slot_values(rank, value):
    return pl.pallas_call(
        values_kernel,
        out_shape=jax.ShapeDtypeStruct((value.shape[2], LANES), BF16),
        compiler_params=grant(),
        cost_estimate=cost(0, 1 << 20),
    )(rank, value)


def terms_kernel(more, wf_ref, ws_ref, val_ref, got_ref, out_ref, share_ref, weight_ref):
    shards, _, tokens = got_ref.shape
    cols, lat_width = ws_ref.shape

    @pl.when(pl.program_id(0) == 0)
    def _():
        weight_ref[0:cols, 0:lat_width] = wf_ref[0]
        weight_ref[cols : 2 * cols, 0:lat_width] = wf_ref[1]
        weight_ref[0:cols, lat_width:] = jnp.zeros((cols, lat_width), BF16)
        weight_ref[cols : 2 * cols, lat_width:] = ws_ref[...]

    share_ref[...] = got_ref[:, 0:more, :]
    pair = 2
    for first in range(0, shards, pair):
        some = range(first, first + pair)
        cot = jnp.concatenate([got_ref[shard, more : more + 2 * cols, :] for shard in some], axis=1)
        dense = jnp.dot(cot.T, weight_ref[...], preferred_element_type=F32)
        held = jnp.concatenate([got_ref[shard, more + 2 * cols :, :] for shard in some], axis=0)
        held = held.astype(F32).astype(jnp.int32) + SHIFT
        lane = lax.broadcasted_iota(jnp.int32, held.shape, 1)
        chunks = lat_width // LANES
        chunk = ((held & 7) >> 1) + jnp.where(lane >= RUNS, chunks, 0)
        chunk = jnp.where(held < lat_width, chunk, 2 * chunks)
        within = jnp.where((held & 1) == 1, RUNS, 0) + (held >> 3)
        picked = jnp.zeros(held.shape, F32)
        for part in range(2 * chunks):
            table = dense[:, part * LANES : (part + 1) * LANES]
            picked = jnp.where(chunk == part, lane_pick(table, within), picked)
        for shard in some:
            out_ref[shard, 0:tokens, :] = picked[(shard - first) * tokens : (shard - first + 1) * tokens].astype(BF16)
            out_ref[shard, tokens:, :] = val_ref[...]


def slot_terms(first, second, values, got):
    parts, rows, tokens = got.shape
    cols, lat_width = second.shape
    more = rows - tokens - 2 * cols
    shards = 4
    return pl.pallas_call(
        functools.partial(terms_kernel, more),
        grid=(parts // shards,),
        in_specs=[
            pl.BlockSpec((2, cols, lat_width), lambda i: (0, 0, 0)),
            pl.BlockSpec((cols, lat_width), lambda i: (0, 0)),
            pl.BlockSpec((tokens, LANES), lambda i: (0, 0)),
            pl.BlockSpec((shards, rows, tokens), lambda i: (i, 0, 0)),
        ],
        out_specs=[
            pl.BlockSpec((shards, 2 * tokens, LANES), lambda i: (i, 0, 0)),
            pl.BlockSpec((shards, more, tokens), lambda i: (i, 0, 0)),
        ],
        out_shape=[
            jax.ShapeDtypeStruct((parts, 2 * tokens, LANES), BF16),
            jax.ShapeDtypeStruct((parts, more, tokens), BF16),
        ],
        scratch_shapes=[pltpu.VMEM((2 * cols, 2 * lat_width), BF16)],
        compiler_params=grant(50),
        cost_estimate=cost(2 * parts * tokens * cols * 3 * lat_width, 6 << 20),
    )(first, second, values, got)


def total_kernel(got_ref, rank_ref, grad_ref, part_ref):
    tokens = grad_ref.shape[1]
    total = jnp.sum(got_ref[:, 0:tokens, :].astype(F32), axis=0)
    for dest in range(grad_ref.shape[0]):
        grad_ref[dest] = total.astype(BF16)
    turned = total.T
    slots = rank_ref.shape[1]
    for layer in range(2):
        rank = rank_ref[layer]
        part = jnp.zeros(rank.shape, F32)
        for slot in range(slots):
            row = layer * slots + slot
            part = jnp.where(rank == slot, turned[row : row + 1, :], part)
        part_ref[layer] = part.astype(BF16)


def slot_totals(got, rank):
    parts, rows, _ = got.shape
    return pl.pallas_call(
        total_kernel,
        out_shape=[
            jax.ShapeDtypeStruct((parts, rows // 2, LANES), BF16),
            jax.ShapeDtypeStruct(rank.shape, BF16),
        ],
        compiler_params=grant(),
        cost_estimate=cost(0, 1 << 20),
    )(got, rank)


FEW = ((8, 4, 2, 1), 3)
ALL = ((32, 16, 8, 4, 2, 1), 8)


def spots_kernel(got_ref, spot_ref):
    shards, _, tokens = got_ref.shape
    top = got_ref.shape[1] - tokens
    lane = lax.broadcasted_iota(jnp.int32, (tokens, LANES), 1)
    place = lane & (RUNS - 1)
    base = lane & RUNS
    last = base + (RUNS - 1)
    start = 8 * place - SHIFT

    def fill(jumps, hops):
        for shard in range(shards):
            held = got_ref[shard, top:, :].astype(F32).astype(jnp.int32)
            below = base
            for jump in jumps:
                further = below + jump
                below = jnp.where(lane_pick(held, further - 1) < start, further, below)
            codes = jnp.zeros((tokens, LANES), jnp.int32)
            for hop in range(hops):
                spot = below if hop == 0 else jnp.minimum(below + hop, last)
                ahead = lane_pick(held, spot) - start
                code = jnp.where((ahead & -8) == 0, ahead + 1, 0)
                if hop > 0:
                    code = jnp.where(below + hop <= last, code, 0)
                codes = codes | jnp.left_shift(code, 4 * hop)
            spot_ref[shard, 0:tokens, :] = below
            spot_ref[shard, tokens:, :] = codes

    deep = jnp.zeros((tokens, LANES), jnp.int32)
    for shard in range(shards):
        held = got_ref[shard, top:, :].astype(F32).astype(jnp.int32)
        ahead = pltpu.roll(held, LANES - FEW[1], 1)
        crowd = ((held >> 3) == (ahead >> 3)) & (place < RUNS - FEW[1])
        many = place == sum(FEW[0])
        deep = jnp.where((held < EMPTY) & (crowd | many), 1, deep)
    deep = jnp.max(deep)

    @pl.when(deep == 0)
    def _():
        fill(*FEW)

    @pl.when(deep != 0)
    def _():
        fill(*ALL)


def slot_spots(got):
    parts, rows, tokens = got.shape
    shards = 2
    return pl.pallas_call(
        spots_kernel,
        grid=(parts // shards,),
        in_specs=[pl.BlockSpec((shards, rows, tokens), lambda i: (i, 0, 0))],
        out_specs=pl.BlockSpec((shards, 2 * tokens, LANES), lambda i: (i, 0, 0)),
        out_shape=jax.ShapeDtypeStruct((parts, 2 * tokens, LANES), jnp.int32),
        compiler_params=grant(56),
        cost_estimate=cost(SPOTS_FLOPS, 8 << 20),
    )(got)


def dense(table, below, codes, hops):
    lane = lax.broadcasted_iota(jnp.int32, below.shape, 1)
    near = lane < RUNS
    far_codes = pltpu.roll(codes, RUNS, 1)
    kept, which = ([], []), ([], [])
    for hop in range(hops):
        spot = below if hop == 0 else jnp.minimum(below + hop, LANES - 1)
        value = lane_pick(table, spot)
        far_value = pltpu.roll(value, RUNS, 1)
        code = (codes >> (4 * hop)) & 15
        far_code = (far_codes >> (4 * hop)) & 15
        kept[0].append(jnp.where(near, value, far_value))
        kept[1].append(jnp.where(near, far_value, value))
        which[0].append(jnp.where(near, code, far_code - 1))
        which[1].append(jnp.where(near, far_code, code - 1))
    for layer in range(2):
        for chunk in range(4):
            found = jnp.zeros(below.shape, F32)
            for hop in range(hops):
                found = jnp.where(which[layer][hop] == 2 * chunk + 1, kept[layer][hop], found)
            yield layer, chunk, found.astype(BF16)


def fill_dense(table_ref, spot_ref, out_ref, halves):
    shards, tokens = spot_ref.shape[0], spot_ref.shape[1] // 2
    crowd = jnp.zeros((tokens, LANES), jnp.int32)
    for shard in range(shards):
        crowd = jnp.where((spot_ref[shard, tokens:, :] >> (4 * FEW[1])) != 0, 1, crowd)
    crowd = jnp.max(crowd)

    def fill(hops, shard):
        table = table_ref[shard].astype(F32)
        low = shard * tokens
        if not isinstance(shard, int):
            low = pl.multiple_of(low, tokens)
        for layer, chunk, found in dense(table, spot_ref[shard, 0:tokens, :], spot_ref[shard, tokens:, :], hops):
            at = slice((4 * layer + chunk) * LANES, (4 * layer + chunk + 1) * LANES)
            if halves and layer == 1:
                half = tokens // 2
                found = jnp.concatenate([found[half:], found[:half]], axis=0)
            out_ref[pl.ds(low, tokens), at] = found

    @pl.when(crowd == 0)
    def _():
        for shard in range(shards):
            fill(FEW[1], shard)

    @pl.when(crowd != 0)
    def _():
        def one(shard, carry):
            fill(ALL[1], shard)
            return carry

        lax.fori_loop(0, shards, one, 0)


def codes_kernel(got_ref, val_ref, spot_ref, first_ref, second_ref, code_ref, sum_ref):
    shards, tokens = spot_ref.shape[0], spot_ref.shape[1] // 2
    cols, lat_width = second_ref.shape
    step = pl.program_id(0)

    @pl.when(step == 0)
    def _():
        sum_ref[...] = jnp.zeros_like(sum_ref)

    fill_dense(val_ref, spot_ref, code_ref, False)
    more = got_ref.shape[1] - tokens - 2 * cols
    cot = jnp.concatenate([got_ref[shard, more : more + 2 * cols, :] for shard in range(shards)], axis=1)
    dot = functools.partial(jnp.dot, preferred_element_type=F32)
    sum_ref[0 : 2 * cols, :] += dot(cot, code_ref[:, 0:lat_width])
    sum_ref[2 * cols : 3 * cols, :] += dot(cot[cols:], code_ref[:, lat_width:])

    @pl.when(step == pl.num_programs(0) - 1)
    def _():
        first_ref[0] = sum_ref[0:cols, :].astype(BF16)
        first_ref[1] = sum_ref[cols : 2 * cols, :].astype(BF16)
        second_ref[...] = sum_ref[2 * cols : 3 * cols, :].astype(BF16)


def decoder_grads(got, slots, spots, cols, lat_width):
    parts, rows, tokens = got.shape
    shards = 4
    return pl.pallas_call(
        codes_kernel,
        grid=(parts // shards,),
        in_specs=[
            pl.BlockSpec((shards, rows, tokens), lambda i: (i, 0, 0)),
            pl.BlockSpec((shards, tokens, LANES), lambda i: (i, 1, 0)),
            pl.BlockSpec((shards, 2 * tokens, LANES), lambda i: (i, 0, 0)),
        ],
        out_specs=[
            pl.BlockSpec((2, cols, lat_width), lambda i: (0, 0, 0)),
            pl.BlockSpec((cols, lat_width), lambda i: (0, 0)),
        ],
        out_shape=[
            jax.ShapeDtypeStruct((2, cols, lat_width), BF16),
            jax.ShapeDtypeStruct((cols, lat_width), BF16),
        ],
        scratch_shapes=[
            pltpu.VMEM((shards * tokens, 2 * lat_width), BF16),
            pltpu.VMEM((3 * cols, lat_width), F32),
        ],
        compiler_params=grant(52),
        cost_estimate=cost(2 * parts * tokens * cols * 3 * lat_width, 8 << 20),
    )(got, slots, spots)


def back_kernel(own_ref, mine_ref, other_ref, spot_ref, grad_ref, enc_ref, back_ref, sum_ref):
    shards, tokens = spot_ref.shape[0], spot_ref.shape[1] // 2
    cols, _, lat_width = enc_ref.shape
    step = pl.program_id(0)
    fill_dense(grad_ref, spot_ref, back_ref, True)

    @pl.when(step == 0)
    def _():
        sum_ref[...] = jnp.zeros_like(sum_ref)

    lane = lax.broadcasted_iota(jnp.int32, (cols, tokens), 1)
    mine = (lane < RUNS) == (own_ref[1] == 0)
    sides = ([], [])
    for shard in range(shards):
        one, two = mine_ref[shard].astype(F32), other_ref[shard].astype(F32)
        sides[0].append(jnp.where(mine, one, two).astype(BF16))
        sides[1].append(jnp.where(mine, two, one).astype(BF16))
    for layer in range(2):
        sum_ref[layer * cols : (layer + 1) * cols, :] += jnp.dot(
            jnp.concatenate(sides[layer], axis=1),
            back_ref[:, layer * lat_width : (layer + 1) * lat_width],
            preferred_element_type=F32,
        )

    @pl.when(step == pl.num_programs(0) - 1)
    def _():
        enc_ref[:, 0, :] = sum_ref[0:cols, :].astype(BF16)
        enc_ref[:, 1, :] = sum_ref[cols:, :].astype(BF16)


def encoder_grads(own, mine, other, spots, grads, cols, lat_width):
    parts, tokens, _ = grads.shape
    shards = 4
    return pl.pallas_call(
        back_kernel,
        grid=(parts // shards,),
        in_specs=[
            pl.BlockSpec(memory_space=pltpu.SMEM),
            pl.BlockSpec((shards, cols, tokens), lambda i: (i, 0, 0)),
            pl.BlockSpec((shards, cols, tokens), lambda i: (i, 0, 0)),
            pl.BlockSpec((shards,) + spots.shape[1:], lambda i: (i, 0, 0)),
            pl.BlockSpec((shards, tokens, LANES), lambda i: (i, 0, 0)),
        ],
        out_specs=pl.BlockSpec((cols, 2, lat_width), lambda i: (0, 0, 0)),
        out_shape=jax.ShapeDtypeStruct((cols, 2, lat_width), BF16),
        scratch_shapes=[
            pltpu.VMEM((shards * tokens, 2 * lat_width), BF16),
            pltpu.VMEM((2 * cols, lat_width), F32),
        ],
        compiler_params=grant(50),
        cost_estimate=cost(2 * parts * tokens * cols * 2 * lat_width, 8 << 20),
    )(own, mine, other, spots, grads)


def exchange(array, axis):
    return lax.all_to_all(array, axis, 0, 0, tiled=True)


def from_hops(array, axis, size, hops):
    return [lax.ppermute(array, axis, [(at, at ^ hop) for at in range(size)]) for hop in hops]


def shards(layers, parts, residual, cotangent, decoder_first, decoder_second, latent_index, latent_value, active_count):
    lat_width = decoder_first.shape[0]
    cols = decoder_second.shape[1]
    tokens = residual.shape[1]
    members = 2
    place = lax.axis_index("layer")
    own = jnp.stack([place * lat_width, place // 2 % members]).astype(jnp.int32)
    index, value = latent_index.transpose(0, 2, 1), latent_value.transpose(0, 2, 1)
    packed, rank = pack(lat_width, parts, members, own, cotangent, residual, index, active_count)
    values = slot_values(rank, value)
    got = exchange(packed, "dp")
    terms, share = slot_terms(decoder_first.transpose(1, 2, 0), decoder_second.T, values, got)
    (other,) = from_hops(share, "layer", layers, (2,))
    slots = exchange(terms, "dp")
    spots = slot_spots(got)
    slots, spots = lax.optimization_barrier((slots, spots))
    grads, part = slot_totals(slots, rank)
    spots, other = lax.optimization_barrier((spots, other))
    all_grads = exchange(grads, "dp")
    first_grad, second_grad = decoder_grads(got, slots, spots, cols, lat_width)
    part = functools.reduce(jnp.add, from_hops(part, "layer", layers, (1, 2, 3)), part)
    all_grads, first_grad, part = lax.optimization_barrier((all_grads, first_grad, part))
    encoder_grad = encoder_grads(own, share, other, spots, all_grads, cols, lat_width)
    far = from_hops(part, "layer", layers, (4, 8, 12))
    *far, encoder_grad = lax.optimization_barrier((*far, encoder_grad))
    latent_grad = functools.reduce(jnp.add, far, part)
    return (
        first_grad.transpose(2, 0, 1),
        second_grad.T,
        encoder_grad,
        latent_grad.astype(F32).transpose(0, 2, 1),
    )


def solution(mesh):
    return jax.shard_map(
        functools.partial(shards, mesh.shape["layer"], mesh.shape["dp"]),
        mesh=mesh,
        in_specs=(
            P(None, "dp", None),
            P(None, "dp", None),
            P("layer", None, "dp"),
            P("layer", "dp"),
            P(None, "dp", None),
            P(None, "dp", None),
            P(None, "dp"),
        ),
        out_specs=(
            P("layer", None, "dp"),
            P("layer", "dp"),
            P("dp", None, "layer"),
            P(None, "dp", None),
        ),
        check_vma=False,
    )
```

```python
import functools
import jax
import jax.numpy as jnp
from jax import lax
from jax.experimental import pallas as pl
from jax.experimental.pallas import tpu as pltpu
from jax.sharding import PartitionSpec as P

BF16 = jnp.bfloat16
F32 = jnp.float32
LANES = 128
RUNS = LANES // 2
SHIFT = 256
EMPTY = 512
STREAM_MIB = 60
KERNEL_MIB = 16
TERMS_MIB = 56
SPOTS_FLOPS = 1 << 32


def grant(mib=KERNEL_MIB):
    return pltpu.CompilerParams(vmem_limit_bytes=mib << 20)


def cost(flops, moved):
    return pl.CostEstimate(flops=flops, bytes_accessed=moved, transcendentals=0)


def lane_pick(table, where):
    return jnp.take_along_axis(table, where, axis=1, mode="promise_in_bounds")


def turn(source, out_ref, base):
    dests = out_ref.shape[0]
    cols = source.shape[1] // dests
    turned = source.T
    for dest in range(dests):
        out_ref[dest, base : base + cols, :] = turned[dest * cols : (dest + 1) * cols]


def kept_slots(own_ref, idx_ref, live_ref, layer, lat_width):
    slots, tokens = idx_ref.shape[1:]
    place = lax.broadcasted_iota(jnp.int32, (slots, tokens), 0)
    local = idx_ref[layer] - own_ref[0]
    inside = (place < live_ref[layer : layer + 1, :]) & (local >= 0) & (local < lat_width)
    return place, local, inside


def pack_kernel(lat_width, own_ref, cot_ref, idx_ref, live_ref, out_ref, rank_ref, slot_ref):
    slots, tokens = idx_ref.shape[1:]
    dests = out_ref.shape[0]
    cols = cot_ref.shape[2] // dests

    @pl.when(pl.program_id(0) == 0)
    def _():
        found = []
        for layer in range(2):
            place, local, inside = kept_slots(own_ref, idx_ref, live_ref, layer, lat_width)
            key = (local & (RUNS - 1)) * 8 + (local >> 6)
            held_key = key - SHIFT
            key = jnp.where(inside, key, 1 << 20)
            rank = jnp.zeros((slots, tokens), jnp.int32)
            for slot in range(slots):
                rank = rank + jnp.where(key[slot : slot + 1, :] < key, 1, 0)
            rank = jnp.where(inside, rank, slots)
            rank_ref[layer] = rank
            held = jnp.full((slots, tokens), EMPTY, jnp.int32)
            for slot in range(slots):
                held = jnp.where(rank[slot : slot + 1, :] == place, held_key[slot : slot + 1, :], held)
            found.append(held.astype(F32))
        slot_ref[...] = jnp.concatenate(found, axis=0).T.astype(BF16)

    for layer in range(2):
        turn(cot_ref[layer], out_ref, layer * cols)
    for dest in range(dests):
        out_ref[dest, 2 * cols :, :] = slot_ref[...]


def pack(lat_width, parts, start, cotangent, index, live):
    _, tokens, width = cotangent.shape
    slots = index.shape[1]
    steps = 4
    rows = 2 * (width // parts) + tokens
    return pl.pallas_call(
        functools.partial(pack_kernel, lat_width),
        grid_spec=pltpu.PrefetchScalarGridSpec(
            num_scalar_prefetch=1,
            grid=(steps,),
            in_specs=[
                pl.BlockSpec((2, tokens, width // steps), lambda i, own: (0, 0, i)),
                pl.BlockSpec((2, slots, tokens), lambda i, own: (0, 0, 0)),
                pl.BlockSpec((2, tokens), lambda i, own: (0, 0)),
            ],
            out_specs=[
                pl.BlockSpec((parts // steps, rows, tokens), lambda i, own: (i, 0, 0)),
                pl.BlockSpec((2, slots, tokens), lambda i, own: (0, 0, 0)),
            ],
            scratch_shapes=[pltpu.VMEM((tokens, LANES), BF16)],
        ),
        out_shape=[
            jax.ShapeDtypeStruct((parts, rows, tokens), BF16),
            jax.ShapeDtypeStruct((2, slots, tokens), jnp.int32),
        ],
        compiler_params=grant(STREAM_MIB),
        cost_estimate=cost(0, 5 << 20),
    )(start, cotangent, index, live)


def half_kernel(own_ref, res_ref, out_ref):
    turn(jnp.concatenate([res_ref[own_ref[1]], res_ref[1 - own_ref[1]]], axis=0), out_ref, 0)


def pack_half(parts, own, residual):
    _, tokens, width = residual.shape
    steps = 4
    share = tokens // 2
    return pl.pallas_call(
        half_kernel,
        grid_spec=pltpu.PrefetchScalarGridSpec(
            num_scalar_prefetch=1,
            grid=(steps,),
            in_specs=[pl.BlockSpec((2, share, width // steps), lambda i, own: (0, own[1], i))],
            out_specs=pl.BlockSpec((parts // steps, width // parts, tokens), lambda i, own: (i, 0, 0)),
        ),
        out_shape=jax.ShapeDtypeStruct((parts, width // parts, tokens), BF16),
        compiler_params=grant(62),
        cost_estimate=cost(0, 2 << 20),
    )(own, residual)


def values_kernel(rank_ref, val_ref, out_ref):
    slots, tokens = val_ref.shape[1:]
    place = lax.broadcasted_iota(jnp.int32, (slots, tokens), 0)
    codes = []
    for layer in range(2):
        rank = rank_ref[layer]
        value = val_ref[layer].astype(F32)
        code = jnp.zeros((slots, tokens), F32)
        for slot in range(slots):
            code = jnp.where(rank[slot : slot + 1, :] == place, value[slot : slot + 1, :], code)
        codes.append(code)
    out_ref[...] = jnp.concatenate(codes, axis=0).T.astype(BF16)


def slot_values(rank, value):
    return pl.pallas_call(
        values_kernel,
        out_shape=jax.ShapeDtypeStruct((value.shape[2], LANES), BF16),
        compiler_params=grant(62),
        cost_estimate=cost(0, 1 << 20),
    )(rank, value)


def terms_kernel(wf_ref, ws_ref, val_ref, half_ref, got_ref, out_ref, weight_ref):
    shards, _, tokens = got_ref.shape
    cols, lat_width = ws_ref.shape

    @pl.when(pl.program_id(0) == 0)
    def _():
        weight_ref[0:cols, 0:lat_width] = wf_ref[0]
        weight_ref[cols : 2 * cols, 0:lat_width] = wf_ref[1]
        weight_ref[0:cols, lat_width:] = jnp.zeros((cols, lat_width), BF16)
        weight_ref[cols : 2 * cols, lat_width:] = ws_ref[...]

    out_ref[:, 2 * tokens :, :] = half_ref[...]
    pair = 2
    for first in range(0, shards, pair):
        some = range(first, first + pair)
        cot = jnp.concatenate([got_ref[shard, 0 : 2 * cols, :] for shard in some], axis=1)
        dense = jnp.dot(cot.T, weight_ref[...], preferred_element_type=F32)
        held = jnp.concatenate([got_ref[shard, 2 * cols :, :] for shard in some], axis=0)
        held = held.astype(F32).astype(jnp.int32) + SHIFT
        lane = lax.broadcasted_iota(jnp.int32, held.shape, 1)
        chunks = lat_width // LANES
        chunk = ((held & 7) >> 1) + jnp.where(lane >= RUNS, chunks, 0)
        chunk = jnp.where(held < lat_width, chunk, 2 * chunks)
        within = jnp.where((held & 1) == 1, RUNS, 0) + (held >> 3)
        picked = jnp.zeros(held.shape, F32)
        for part in range(2 * chunks):
            table = dense[:, part * LANES : (part + 1) * LANES]
            picked = jnp.where(chunk == part, lane_pick(table, within), picked)
        for shard in some:
            out_ref[shard, 0:tokens, :] = picked[(shard - first) * tokens : (shard - first + 1) * tokens].astype(BF16)
            out_ref[shard, tokens : 2 * tokens, :] = val_ref[...]


def slot_terms(first, second, values, half, got):
    parts, rows, tokens = got.shape
    cols, lat_width = second.shape
    shards = 4
    return pl.pallas_call(
        terms_kernel,
        grid=(parts // shards,),
        in_specs=[
            pl.BlockSpec((2, cols, lat_width), lambda i: (0, 0, 0)),
            pl.BlockSpec((cols, lat_width), lambda i: (0, 0)),
            pl.BlockSpec((tokens, LANES), lambda i: (0, 0)),
            pl.BlockSpec((shards, cols, tokens), lambda i: (i, 0, 0)),
            pl.BlockSpec((shards, rows, tokens), lambda i: (i, 0, 0)),
        ],
        out_specs=pl.BlockSpec((shards, 2 * tokens + cols, LANES), lambda i: (i, 0, 0)),
        out_shape=jax.ShapeDtypeStruct((parts, 2 * tokens + cols, LANES), BF16),
        scratch_shapes=[pltpu.VMEM((2 * cols, 2 * lat_width), BF16)],
        compiler_params=grant(TERMS_MIB),
        cost_estimate=cost(2 * parts * tokens * cols * 3 * lat_width, 6 << 20),
    )(first, second, values, half, got)


def total_kernel(got_ref, rank_ref, grad_ref, part_ref):
    total = jnp.sum(got_ref[...].astype(F32), axis=0)
    for dest in range(grad_ref.shape[0]):
        grad_ref[dest] = total.astype(BF16)
    turned = total.T
    slots = rank_ref.shape[1]
    for layer in range(2):
        rank = rank_ref[layer]
        part = jnp.zeros(rank.shape, F32)
        for slot in range(slots):
            row = layer * slots + slot
            part = jnp.where(rank == slot, turned[row : row + 1, :], part)
        part_ref[layer] = part.astype(BF16)


def slot_totals(got, rank):
    parts = got.shape[0]
    tokens = rank.shape[2]
    return pl.pallas_call(
        total_kernel,
        grid=(1,),
        in_specs=[
            pl.BlockSpec((parts, tokens, LANES), lambda i: (0, 0, 0)),
            pl.BlockSpec(rank.shape, lambda i: (0, 0, 0)),
        ],
        out_specs=[
            pl.BlockSpec((parts, tokens, LANES), lambda i: (0, 0, 0)),
            pl.BlockSpec(rank.shape, lambda i: (0, 0, 0)),
        ],
        out_shape=[
            jax.ShapeDtypeStruct((parts, tokens, LANES), BF16),
            jax.ShapeDtypeStruct(rank.shape, BF16),
        ],
        compiler_params=grant(),
        cost_estimate=cost(0, 1 << 20),
    )(got, rank)


FEW = ((8, 4, 2, 1), 3)
ALL = ((32, 16, 8, 4, 2, 1), 8)


def spots_kernel(got_ref, spot_ref):
    shards, _, tokens = got_ref.shape
    top = got_ref.shape[1] - tokens
    lane = lax.broadcasted_iota(jnp.int32, (tokens, LANES), 1)
    place = lane & (RUNS - 1)
    base = lane & RUNS
    last = base + (RUNS - 1)
    start = 8 * place - SHIFT

    def fill(jumps, hops):
        for shard in range(shards):
            held = got_ref[shard, top:, :].astype(F32).astype(jnp.int32)
            below = base
            for jump in jumps:
                further = below + jump
                below = jnp.where(lane_pick(held, further - 1) < start, further, below)
            codes = jnp.zeros((tokens, LANES), jnp.int32)
            for hop in range(hops):
                spot = below if hop == 0 else jnp.minimum(below + hop, last)
                ahead = lane_pick(held, spot) - start
                code = jnp.where((ahead & -8) == 0, ahead + 1, 0)
                if hop > 0:
                    code = jnp.where(below + hop <= last, code, 0)
                codes = codes | jnp.left_shift(code, 4 * hop)
            spot_ref[shard, 0:tokens, :] = below
            spot_ref[shard, tokens:, :] = codes

    deep = jnp.zeros((tokens, LANES), jnp.int32)
    for shard in range(shards):
        held = got_ref[shard, top:, :].astype(F32).astype(jnp.int32)
        ahead = pltpu.roll(held, LANES - FEW[1], 1)
        crowd = ((held >> 3) == (ahead >> 3)) & (place < RUNS - FEW[1])
        many = place == sum(FEW[0])
        deep = jnp.where((held < EMPTY) & (crowd | many), 1, deep)
    deep = jnp.max(deep)

    @pl.when(deep == 0)
    def _():
        fill(*FEW)

    @pl.when(deep != 0)
    def _():
        fill(*ALL)


def slot_spots(got):
    parts, rows, tokens = got.shape
    shards = 2
    return pl.pallas_call(
        spots_kernel,
        grid=(parts // shards,),
        in_specs=[pl.BlockSpec((shards, rows, tokens), lambda i: (i, 0, 0))],
        out_specs=pl.BlockSpec((shards, 2 * tokens, LANES), lambda i: (i, 0, 0)),
        out_shape=jax.ShapeDtypeStruct((parts, 2 * tokens, LANES), jnp.int32),
        compiler_params=grant(56),
        cost_estimate=cost(SPOTS_FLOPS, 8 << 20),
    )(got)


def dense(table, below, codes, hops):
    lane = lax.broadcasted_iota(jnp.int32, below.shape, 1)
    near = lane < RUNS
    far_codes = pltpu.roll(codes, RUNS, 1)
    kept, which = ([], []), ([], [])
    for hop in range(hops):
        spot = below if hop == 0 else jnp.minimum(below + hop, LANES - 1)
        value = lane_pick(table, spot)
        far_value = pltpu.roll(value, RUNS, 1)
        code = (codes >> (4 * hop)) & 15
        far_code = (far_codes >> (4 * hop)) & 15
        kept[0].append(jnp.where(near, value, far_value))
        kept[1].append(jnp.where(near, far_value, value))
        which[0].append(jnp.where(near, code, far_code - 1))
        which[1].append(jnp.where(near, far_code, code - 1))
    for layer in range(2):
        for chunk in range(4):
            found = jnp.zeros(below.shape, F32)
            for hop in range(hops):
                found = jnp.where(which[layer][hop] == 2 * chunk + 1, kept[layer][hop], found)
            yield layer, chunk, found.astype(BF16)


def fill_dense(table_ref, spot_ref, out_ref, halves, product):
    shards, tokens = spot_ref.shape[0], spot_ref.shape[1] // 2
    crowd = jnp.zeros((tokens, LANES), jnp.int32)
    for shard in range(shards):
        crowd = jnp.where((spot_ref[shard, tokens:, :] >> (4 * FEW[1])) != 0, 1, crowd)
    crowd = jnp.max(crowd)

    def fill(hops, shard):
        table = table_ref[shard].astype(F32)
        low = shard * tokens
        if not isinstance(shard, int):
            low = pl.multiple_of(low, tokens)
        for layer, chunk, found in dense(table, spot_ref[shard, 0:tokens, :], spot_ref[shard, tokens:, :], hops):
            at = slice((4 * layer + chunk) * LANES, (4 * layer + chunk + 1) * LANES)
            if halves and layer == 1:
                half = tokens // 2
                found = jnp.concatenate([found[half:], found[:half]], axis=0)
            out_ref[pl.ds(low, tokens), at] = found

    @pl.when(crowd == 0)
    def _():
        for shard in range(shards):
            fill(FEW[1], shard)
            if shard % 2 == 1:
                product(shard - 1)

    @pl.when(crowd != 0)
    def _():
        def one(shard, carry):
            fill(ALL[1], shard)
            return carry

        lax.fori_loop(0, shards, one, 0)
        for shard in range(0, shards, 2):
            product(shard)


def codes_kernel(got_ref, val_ref, spot_ref, first_ref, second_ref, code_ref, sum_ref):
    shards, tokens = spot_ref.shape[0], spot_ref.shape[1] // 2
    cols, lat_width = second_ref.shape
    step = pl.program_id(0)

    @pl.when(step == 0)
    def _():
        sum_ref[...] = jnp.zeros_like(sum_ref)

    def product(first):
        rows = slice(first * tokens, (first + 2) * tokens)
        cot = jnp.concatenate([got_ref[shard, 0 : 2 * cols, :] for shard in (first, first + 1)], axis=1)
        dot = functools.partial(jnp.dot, preferred_element_type=F32)
        sum_ref[0 : 2 * cols, :] += dot(cot, code_ref[rows, 0:lat_width])
        sum_ref[2 * cols : 3 * cols, :] += dot(cot[cols:], code_ref[rows, lat_width:])

    fill_dense(val_ref, spot_ref, code_ref, False, product)

    @pl.when(step == pl.num_programs(0) - 1)
    def _():
        first_ref[0] = sum_ref[0:cols, :].astype(BF16)
        first_ref[1] = sum_ref[cols : 2 * cols, :].astype(BF16)
        second_ref[...] = sum_ref[2 * cols : 3 * cols, :].astype(BF16)


def decoder_grads(got, slots, spots, cols, lat_width):
    parts, rows, tokens = got.shape
    shards = 4
    return pl.pallas_call(
        codes_kernel,
        grid=(parts // shards,),
        in_specs=[
            pl.BlockSpec((shards, rows, tokens), lambda i: (i, 0, 0)),
            pl.BlockSpec((shards, tokens, LANES), lambda i: (i, 1, 0)),
            pl.BlockSpec((shards, 2 * tokens, LANES), lambda i: (i, 0, 0)),
        ],
        out_specs=[
            pl.BlockSpec((2, cols, lat_width), lambda i: (0, 0, 0)),
            pl.BlockSpec((cols, lat_width), lambda i: (0, 0)),
        ],
        out_shape=[
            jax.ShapeDtypeStruct((2, cols, lat_width), BF16),
            jax.ShapeDtypeStruct((cols, lat_width), BF16),
        ],
        scratch_shapes=[
            pltpu.VMEM((shards * tokens, 2 * lat_width), BF16),
            pltpu.VMEM((3 * cols, lat_width), F32),
        ],
        compiler_params=grant(52),
        cost_estimate=cost(2 * parts * tokens * cols * 3 * lat_width, 8 << 20),
    )(got, slots, spots)


def back_kernel(own_ref, mine_ref, other_ref, spot_ref, grad_ref, enc_ref, back_ref, sum_ref):
    shards, tokens = spot_ref.shape[0], spot_ref.shape[1] // 2
    cols, _, lat_width = enc_ref.shape
    step = pl.program_id(0)
    @pl.when(step == 0)
    def _():
        sum_ref[...] = jnp.zeros_like(sum_ref)

    lane = lax.broadcasted_iota(jnp.int32, (cols, tokens), 1)
    mine = (lane < RUNS) == (own_ref[1] == 0)

    def product(first):
        rows = slice(first * tokens, (first + 2) * tokens)
        sides = ([], [])
        for shard in (first, first + 1):
            one, two = mine_ref[shard].astype(F32), other_ref[shard].astype(F32)
            sides[0].append(jnp.where(mine, one, two).astype(BF16))
            sides[1].append(jnp.where(mine, two, one).astype(BF16))
        for layer in range(2):
            sum_ref[layer * cols : (layer + 1) * cols, :] += jnp.dot(
                jnp.concatenate(sides[layer], axis=1),
                back_ref[rows, layer * lat_width : (layer + 1) * lat_width],
                preferred_element_type=F32,
            )

    fill_dense(grad_ref, spot_ref, back_ref, True, product)

    @pl.when(step == pl.num_programs(0) - 1)
    def _():
        enc_ref[:, 0, :] = sum_ref[0:cols, :].astype(BF16)
        enc_ref[:, 1, :] = sum_ref[cols:, :].astype(BF16)


def encoder_grads(own, mine, other, spots, grads, cols, lat_width):
    parts, tokens, _ = grads.shape
    shards = 4
    return pl.pallas_call(
        back_kernel,
        grid=(parts // shards,),
        in_specs=[
            pl.BlockSpec(memory_space=pltpu.SMEM),
            pl.BlockSpec((shards, cols, tokens), lambda i: (i, 0, 0)),
            pl.BlockSpec((shards, cols, tokens), lambda i: (i, 0, 0)),
            pl.BlockSpec((shards,) + spots.shape[1:], lambda i: (i, 0, 0)),
            pl.BlockSpec((shards, tokens, LANES), lambda i: (i, 0, 0)),
        ],
        out_specs=pl.BlockSpec((cols, 2, lat_width), lambda i: (0, 0, 0)),
        out_shape=jax.ShapeDtypeStruct((cols, 2, lat_width), BF16),
        scratch_shapes=[
            pltpu.VMEM((shards * tokens, 2 * lat_width), BF16),
            pltpu.VMEM((2 * cols, lat_width), F32),
        ],
        compiler_params=grant(50),
        cost_estimate=cost(2 * parts * tokens * cols * 2 * lat_width, 8 << 20),
    )(own, mine, other, spots, grads)


def exchange(array, axis):
    return lax.all_to_all(array, axis, 0, 0, tiled=True)


def from_hops(array, axis, size, hops):
    return [lax.ppermute(array, axis, [(at, at ^ hop) for at in range(size)]) for hop in hops]


def shards(layers, parts, residual, cotangent, decoder_first, decoder_second, latent_index, latent_value, active_count):
    lat_width = decoder_first.shape[0]
    cols = decoder_second.shape[1]
    tokens = residual.shape[1]
    members = 2
    place = lax.axis_index("layer")
    own = jnp.stack([place * lat_width, place // 2 % members]).astype(jnp.int32)
    index, value = latent_index.transpose(0, 2, 1), latent_value.transpose(0, 2, 1)
    packed, rank = pack(lat_width, parts, own, cotangent, index, active_count)
    got = exchange(packed, "dp")
    values = slot_values(rank, value)
    half = pack_half(parts, own, residual)
    terms = slot_terms(decoder_first.transpose(1, 2, 0), decoder_second.T, values, half, got)
    slots = exchange(terms, "dp")
    spots = slot_spots(got)
    slots, spots = lax.optimization_barrier((slots, spots))
    grads, part = slot_totals(slots, rank)
    share = slots[:, 2 * tokens :, :]
    (other,) = from_hops(share, "layer", layers, (2,))
    all_grads = exchange(grads, "dp")
    first_grad, second_grad = decoder_grads(got, slots, spots, cols, lat_width)
    part = functools.reduce(jnp.add, from_hops(part, "layer", layers, (1, 2, 3)), part)
    all_grads, first_grad, part = lax.optimization_barrier((all_grads, first_grad, part))
    encoder_grad = encoder_grads(own, share, other, spots, all_grads, cols, lat_width)
    far = from_hops(part, "layer", layers, (4, 8, 12))
    *far, encoder_grad = lax.optimization_barrier((*far, encoder_grad))
    latent_grad = functools.reduce(jnp.add, far, part)
    return (
        first_grad.transpose(2, 0, 1),
        second_grad.T,
        encoder_grad,
        latent_grad.astype(F32).transpose(0, 2, 1),
    )


def solution(mesh):
    return jax.shard_map(
        functools.partial(shards, mesh.shape["layer"], mesh.shape["dp"]),
        mesh=mesh,
        in_specs=(
            P(None, "dp", None),
            P(None, "dp", None),
            P("layer", None, "dp"),
            P("layer", "dp"),
            P(None, "dp", None),
            P(None, "dp", None),
            P(None, "dp"),
        ),
        out_specs=(
            P("layer", None, "dp"),
            P("layer", "dp"),
            P("dp", None, "layer"),
            P(None, "dp", None),
        ),
        check_vma=False,
    )
```

```python
import functools
import jax
import jax.numpy as jnp
from jax import lax
from jax.experimental import pallas as pl
from jax.experimental.pallas import tpu as pltpu
from jax.sharding import PartitionSpec as P

BF16 = jnp.bfloat16
F32 = jnp.float32
LANES = 128
RUNS = LANES // 2
SHIFT = 256
EMPTY = 512
STREAM_MIB = 60
KERNEL_MIB = 16
TERMS_MIB = 56
SPOTS_FLOPS = 1 << 32


def grant(mib=KERNEL_MIB):
    return pltpu.CompilerParams(vmem_limit_bytes=mib << 20)


def cost(flops, moved):
    return pl.CostEstimate(flops=flops, bytes_accessed=moved, transcendentals=0)


def lane_pick(table, where):
    return jnp.take_along_axis(table, where, axis=1, mode="promise_in_bounds")


def turn(source, out_ref, base):
    dests = out_ref.shape[0]
    cols = source.shape[1] // dests
    turned = source.T
    for dest in range(dests):
        out_ref[dest, base : base + cols, :] = turned[dest * cols : (dest + 1) * cols]


def kept_slots(own_ref, idx_ref, live_ref, layer, lat_width):
    slots, tokens = idx_ref.shape[1:]
    place = lax.broadcasted_iota(jnp.int32, (slots, tokens), 0)
    local = idx_ref[layer] - own_ref[0]
    inside = (place < live_ref[layer : layer + 1, :]) & (local >= 0) & (local < lat_width)
    return place, local, inside


def pack_kernel(lat_width, own_ref, cot_ref, idx_ref, val_ref, live_ref, out_ref, rank_ref, slot_ref):
    slots, tokens = idx_ref.shape[1:]
    dests = out_ref.shape[0]
    cols = cot_ref.shape[2] // dests

    @pl.when(pl.program_id(0) == 0)
    def _():
        found, codes = [], []
        for layer in range(2):
            place, local, inside = kept_slots(own_ref, idx_ref, live_ref, layer, lat_width)
            key = (local & (RUNS - 1)) * 8 + (local >> 6)
            held_key = key - SHIFT
            key = jnp.where(inside, key, 1 << 20)
            rank = jnp.zeros((slots, tokens), jnp.int32)
            for slot in range(slots):
                rank = rank + jnp.where(key[slot : slot + 1, :] < key, 1, 0)
            rank = jnp.where(inside, rank, slots)
            rank_ref[layer] = rank
            held = jnp.full((slots, tokens), EMPTY, jnp.int32)
            value = val_ref[layer].astype(F32)
            code = jnp.zeros((slots, tokens), F32)
            for slot in range(slots):
                here = rank[slot : slot + 1, :] == place
                held = jnp.where(here, held_key[slot : slot + 1, :], held)
                code = jnp.where(here, value[slot : slot + 1, :], code)
            found.append(held.astype(F32))
            codes.append(code)
        slot_ref[0:tokens, :] = jnp.concatenate(codes, axis=0).T.astype(BF16)
        slot_ref[tokens:, :] = jnp.concatenate(found, axis=0).T.astype(BF16)

    for layer in range(2):
        turn(cot_ref[layer], out_ref, layer * cols)
    for dest in range(dests):
        out_ref[dest, 2 * cols :, :] = slot_ref[...]


def pack(lat_width, parts, start, cotangent, index, value, live):
    _, tokens, width = cotangent.shape
    slots = index.shape[1]
    steps = 4
    rows = 2 * (width // parts) + 2 * tokens
    return pl.pallas_call(
        functools.partial(pack_kernel, lat_width),
        grid_spec=pltpu.PrefetchScalarGridSpec(
            num_scalar_prefetch=1,
            grid=(steps,),
            in_specs=[
                pl.BlockSpec((2, tokens, width // steps), lambda i, own: (0, 0, i)),
                pl.BlockSpec((2, slots, tokens), lambda i, own: (0, 0, 0)),
                pl.BlockSpec((2, slots, tokens), lambda i, own: (0, 0, 0)),
                pl.BlockSpec((2, tokens), lambda i, own: (0, 0)),
            ],
            out_specs=[
                pl.BlockSpec((parts // steps, rows, tokens), lambda i, own: (i, 0, 0)),
                pl.BlockSpec((2, slots, tokens), lambda i, own: (0, 0, 0)),
            ],
            scratch_shapes=[pltpu.VMEM((2 * tokens, LANES), BF16)],
        ),
        out_shape=[
            jax.ShapeDtypeStruct((parts, rows, tokens), BF16),
            jax.ShapeDtypeStruct((2, slots, tokens), jnp.int32),
        ],
        compiler_params=grant(STREAM_MIB),
        cost_estimate=cost(0, 5 << 20),
    )(start, cotangent, index, value, live)


def half_kernel(own_ref, res_ref, out_ref):
    turn(jnp.concatenate([res_ref[own_ref[1]], res_ref[1 - own_ref[1]]], axis=0), out_ref, 0)


def pack_half(parts, own, residual):
    _, tokens, width = residual.shape
    steps = 4
    share = tokens // 2
    return pl.pallas_call(
        half_kernel,
        grid_spec=pltpu.PrefetchScalarGridSpec(
            num_scalar_prefetch=1,
            grid=(steps,),
            in_specs=[pl.BlockSpec((2, share, width // steps), lambda i, own: (0, own[1], i))],
            out_specs=pl.BlockSpec((parts // steps, width // parts, tokens), lambda i, own: (i, 0, 0)),
        ),
        out_shape=jax.ShapeDtypeStruct((parts, width // parts, tokens), BF16),
        compiler_params=grant(62),
        cost_estimate=cost(0, 2 << 20),
    )(own, residual)


def terms_kernel(wf_ref, ws_ref, half_ref, got_ref, out_ref, weight_ref):
    shards, _, tokens = got_ref.shape
    cols, lat_width = ws_ref.shape

    @pl.when(pl.program_id(0) == 0)
    def _():
        weight_ref[0:cols, 0:lat_width] = wf_ref[0]
        weight_ref[cols : 2 * cols, 0:lat_width] = wf_ref[1]
        weight_ref[0:cols, lat_width:] = jnp.zeros((cols, lat_width), BF16)
        weight_ref[cols : 2 * cols, lat_width:] = ws_ref[...]

    out_ref[:, tokens:, :] = half_ref[...]
    pair = 2
    for first in range(0, shards, pair):
        some = range(first, first + pair)
        cot = jnp.concatenate([got_ref[shard, 0 : 2 * cols, :] for shard in some], axis=1)
        dense = jnp.dot(cot.T, weight_ref[...], preferred_element_type=F32)
        held = jnp.concatenate([got_ref[shard, 2 * cols + tokens :, :] for shard in some], axis=0)
        held = held.astype(F32).astype(jnp.int32) + SHIFT
        lane = lax.broadcasted_iota(jnp.int32, held.shape, 1)
        chunks = lat_width // LANES
        chunk = ((held & 7) >> 1) + jnp.where(lane >= RUNS, chunks, 0)
        chunk = jnp.where(held < lat_width, chunk, 2 * chunks)
        within = jnp.where((held & 1) == 1, RUNS, 0) + (held >> 3)
        picked = jnp.zeros(held.shape, F32)
        for part in range(2 * chunks):
            table = dense[:, part * LANES : (part + 1) * LANES]
            picked = jnp.where(chunk == part, lane_pick(table, within), picked)
        for shard in some:
            out_ref[shard, 0:tokens, :] = picked[(shard - first) * tokens : (shard - first + 1) * tokens].astype(BF16)


def slot_terms(first, second, half, got):
    parts, rows, tokens = got.shape
    cols, lat_width = second.shape
    shards = 4
    return pl.pallas_call(
        terms_kernel,
        grid=(parts // shards,),
        in_specs=[
            pl.BlockSpec((2, cols, lat_width), lambda i: (0, 0, 0)),
            pl.BlockSpec((cols, lat_width), lambda i: (0, 0)),
            pl.BlockSpec((shards, cols, tokens), lambda i: (i, 0, 0)),
            pl.BlockSpec((shards, rows, tokens), lambda i: (i, 0, 0)),
        ],
        out_specs=pl.BlockSpec((shards, tokens + cols, LANES), lambda i: (i, 0, 0)),
        out_shape=jax.ShapeDtypeStruct((parts, tokens + cols, LANES), BF16),
        scratch_shapes=[pltpu.VMEM((2 * cols, 2 * lat_width), BF16)],
        compiler_params=grant(TERMS_MIB),
        cost_estimate=cost(2 * parts * tokens * cols * 3 * lat_width, 6 << 20),
    )(first, second, half, got)


def total_kernel(got_ref, rank_ref, grad_ref, part_ref):
    total = jnp.sum(got_ref[...].astype(F32), axis=0)
    for dest in range(grad_ref.shape[0]):
        grad_ref[dest] = total.astype(BF16)
    turned = total.T
    slots = rank_ref.shape[1]
    for layer in range(2):
        rank = rank_ref[layer]
        part = jnp.zeros(rank.shape, F32)
        for slot in range(slots):
            row = layer * slots + slot
            part = jnp.where(rank == slot, turned[row : row + 1, :], part)
        part_ref[layer] = part.astype(BF16)


def slot_totals(got, rank):
    parts = got.shape[0]
    tokens = rank.shape[2]
    return pl.pallas_call(
        total_kernel,
        grid=(1,),
        in_specs=[
            pl.BlockSpec((parts, tokens, LANES), lambda i: (0, 0, 0)),
            pl.BlockSpec(rank.shape, lambda i: (0, 0, 0)),
        ],
        out_specs=[
            pl.BlockSpec((parts, tokens, LANES), lambda i: (0, 0, 0)),
            pl.BlockSpec(rank.shape, lambda i: (0, 0, 0)),
        ],
        out_shape=[
            jax.ShapeDtypeStruct((parts, tokens, LANES), BF16),
            jax.ShapeDtypeStruct(rank.shape, BF16),
        ],
        compiler_params=grant(),
        cost_estimate=cost(0, 1 << 20),
    )(got, rank)


FEW = ((8, 4, 2, 1), 3)
ALL = ((32, 16, 8, 4, 2, 1), 8)


def spots_kernel(got_ref, spot_ref):
    shards, _, tokens = got_ref.shape
    top = got_ref.shape[1] - tokens
    lane = lax.broadcasted_iota(jnp.int32, (tokens, LANES), 1)
    place = lane & (RUNS - 1)
    base = lane & RUNS
    last = base + (RUNS - 1)
    start = 8 * place - SHIFT

    def fill(jumps, hops):
        for shard in range(shards):
            held = got_ref[shard, top:, :].astype(F32).astype(jnp.int32)
            below = base
            for jump in jumps:
                further = below + jump
                below = jnp.where(lane_pick(held, further - 1) < start, further, below)
            codes = jnp.zeros((tokens, LANES), jnp.int32)
            for hop in range(hops):
                spot = below if hop == 0 else jnp.minimum(below + hop, last)
                ahead = lane_pick(held, spot) - start
                code = jnp.where((ahead & -8) == 0, ahead + 1, 0)
                if hop > 0:
                    code = jnp.where(below + hop <= last, code, 0)
                codes = codes | jnp.left_shift(code, 4 * hop)
            spot_ref[shard, 0:tokens, :] = below
            spot_ref[shard, tokens:, :] = codes

    deep = jnp.zeros((tokens, LANES), jnp.int32)
    for shard in range(shards):
        held = got_ref[shard, top:, :].astype(F32).astype(jnp.int32)
        ahead = pltpu.roll(held, LANES - FEW[1], 1)
        crowd = ((held >> 3) == (ahead >> 3)) & (place < RUNS - FEW[1])
        many = place == sum(FEW[0])
        deep = jnp.where((held < EMPTY) & (crowd | many), 1, deep)
    deep = jnp.max(deep)

    @pl.when(deep == 0)
    def _():
        fill(*FEW)

    @pl.when(deep != 0)
    def _():
        fill(*ALL)


def slot_spots(got):
    parts, rows, tokens = got.shape
    shards = 2
    return pl.pallas_call(
        spots_kernel,
        grid=(parts // shards,),
        in_specs=[pl.BlockSpec((shards, rows, tokens), lambda i: (i, 0, 0))],
        out_specs=pl.BlockSpec((shards, 2 * tokens, LANES), lambda i: (i, 0, 0)),
        out_shape=jax.ShapeDtypeStruct((parts, 2 * tokens, LANES), jnp.int32),
        compiler_params=grant(56),
        cost_estimate=cost(SPOTS_FLOPS, 8 << 20),
    )(got)


def dense(table, below, codes, hops):
    lane = lax.broadcasted_iota(jnp.int32, below.shape, 1)
    near = lane < RUNS
    far_codes = pltpu.roll(codes, RUNS, 1)
    kept, which = ([], []), ([], [])
    for hop in range(hops):
        spot = below if hop == 0 else jnp.minimum(below + hop, LANES - 1)
        value = lane_pick(table, spot)
        far_value = pltpu.roll(value, RUNS, 1)
        code = (codes >> (4 * hop)) & 15
        far_code = (far_codes >> (4 * hop)) & 15
        kept[0].append(jnp.where(near, value, far_value))
        kept[1].append(jnp.where(near, far_value, value))
        which[0].append(jnp.where(near, code, far_code - 1))
        which[1].append(jnp.where(near, far_code, code - 1))
    for layer in range(2):
        for chunk in range(4):
            found = jnp.zeros(below.shape, F32)
            for hop in range(hops):
                found = jnp.where(which[layer][hop] == 2 * chunk + 1, kept[layer][hop], found)
            yield layer, chunk, found.astype(BF16)


def fill_dense(table_ref, top, spot_ref, out_ref, halves, product):
    shards, tokens = spot_ref.shape[0], spot_ref.shape[1] // 2
    crowd = jnp.zeros((tokens, LANES), jnp.int32)
    for shard in range(shards):
        crowd = jnp.where((spot_ref[shard, tokens:, :] >> (4 * FEW[1])) != 0, 1, crowd)
    crowd = jnp.max(crowd)

    def fill(hops, shard):
        table = table_ref[shard, top : top + tokens, :].astype(F32)
        low = shard * tokens
        if not isinstance(shard, int):
            low = pl.multiple_of(low, tokens)
        for layer, chunk, found in dense(table, spot_ref[shard, 0:tokens, :], spot_ref[shard, tokens:, :], hops):
            at = slice((4 * layer + chunk) * LANES, (4 * layer + chunk + 1) * LANES)
            if halves and layer == 1:
                half = tokens // 2
                found = jnp.concatenate([found[half:], found[:half]], axis=0)
            out_ref[pl.ds(low, tokens), at] = found

    @pl.when(crowd == 0)
    def _():
        for shard in range(shards):
            fill(FEW[1], shard)
            if shard % 2 == 1:
                product(shard - 1)

    @pl.when(crowd != 0)
    def _():
        def one(shard, carry):
            fill(ALL[1], shard)
            return carry

        lax.fori_loop(0, shards, one, 0)
        for shard in range(0, shards, 2):
            product(shard)


def codes_kernel(got_ref, spot_ref, first_ref, second_ref, code_ref, sum_ref):
    shards, tokens = spot_ref.shape[0], spot_ref.shape[1] // 2
    cols, lat_width = second_ref.shape
    step = pl.program_id(0)

    @pl.when(step == 0)
    def _():
        sum_ref[...] = jnp.zeros_like(sum_ref)

    def product(first):
        rows = slice(first * tokens, (first + 2) * tokens)
        cot = jnp.concatenate([got_ref[shard, 0 : 2 * cols, :] for shard in (first, first + 1)], axis=1)
        dot = functools.partial(jnp.dot, preferred_element_type=F32)
        sum_ref[0 : 2 * cols, :] += dot(cot, code_ref[rows, 0:lat_width])
        sum_ref[2 * cols : 3 * cols, :] += dot(cot[cols:], code_ref[rows, lat_width:])

    fill_dense(got_ref, 2 * cols, spot_ref, code_ref, False, product)

    @pl.when(step == pl.num_programs(0) - 1)
    def _():
        first_ref[0] = sum_ref[0:cols, :].astype(BF16)
        first_ref[1] = sum_ref[cols : 2 * cols, :].astype(BF16)
        second_ref[...] = sum_ref[2 * cols : 3 * cols, :].astype(BF16)


def decoder_grads(got, spots, cols, lat_width):
    parts, rows, tokens = got.shape
    shards = 4
    return pl.pallas_call(
        codes_kernel,
        grid=(parts // shards,),
        in_specs=[
            pl.BlockSpec((shards, rows, tokens), lambda i: (i, 0, 0)),
            pl.BlockSpec((shards, 2 * tokens, LANES), lambda i: (i, 0, 0)),
        ],
        out_specs=[
            pl.BlockSpec((2, cols, lat_width), lambda i: (0, 0, 0)),
            pl.BlockSpec((cols, lat_width), lambda i: (0, 0)),
        ],
        out_shape=[
            jax.ShapeDtypeStruct((2, cols, lat_width), BF16),
            jax.ShapeDtypeStruct((cols, lat_width), BF16),
        ],
        scratch_shapes=[
            pltpu.VMEM((shards * tokens, 2 * lat_width), BF16),
            pltpu.VMEM((3 * cols, lat_width), F32),
        ],
        compiler_params=grant(52),
        cost_estimate=cost(2 * parts * tokens * cols * 3 * lat_width, 8 << 20),
    )(got, spots)


def back_kernel(own_ref, mine_ref, other_ref, spot_ref, grad_ref, enc_ref, back_ref, sum_ref):
    shards, tokens = spot_ref.shape[0], spot_ref.shape[1] // 2
    cols, _, lat_width = enc_ref.shape
    step = pl.program_id(0)
    @pl.when(step == 0)
    def _():
        sum_ref[...] = jnp.zeros_like(sum_ref)

    lane = lax.broadcasted_iota(jnp.int32, (cols, tokens), 1)
    mine = (lane < RUNS) == (own_ref[1] == 0)

    def product(first):
        rows = slice(first * tokens, (first + 2) * tokens)
        sides = ([], [])
        for shard in (first, first + 1):
            one, two = mine_ref[shard].astype(F32), other_ref[shard].astype(F32)
            sides[0].append(jnp.where(mine, one, two).astype(BF16))
            sides[1].append(jnp.where(mine, two, one).astype(BF16))
        for layer in range(2):
            sum_ref[layer * cols : (layer + 1) * cols, :] += jnp.dot(
                jnp.concatenate(sides[layer], axis=1),
                back_ref[rows, layer * lat_width : (layer + 1) * lat_width],
                preferred_element_type=F32,
            )

    fill_dense(grad_ref, 0, spot_ref, back_ref, True, product)

    @pl.when(step == pl.num_programs(0) - 1)
    def _():
        enc_ref[:, 0, :] = sum_ref[0:cols, :].astype(BF16)
        enc_ref[:, 1, :] = sum_ref[cols:, :].astype(BF16)


def encoder_grads(own, mine, other, spots, grads, cols, lat_width):
    parts, tokens, _ = grads.shape
    shards = 4
    return pl.pallas_call(
        back_kernel,
        grid=(parts // shards,),
        in_specs=[
            pl.BlockSpec(memory_space=pltpu.SMEM),
            pl.BlockSpec((shards, cols, tokens), lambda i: (i, 0, 0)),
            pl.BlockSpec((shards, cols, tokens), lambda i: (i, 0, 0)),
            pl.BlockSpec((shards,) + spots.shape[1:], lambda i: (i, 0, 0)),
            pl.BlockSpec((shards, tokens, LANES), lambda i: (i, 0, 0)),
        ],
        out_specs=pl.BlockSpec((cols, 2, lat_width), lambda i: (0, 0, 0)),
        out_shape=jax.ShapeDtypeStruct((cols, 2, lat_width), BF16),
        scratch_shapes=[
            pltpu.VMEM((shards * tokens, 2 * lat_width), BF16),
            pltpu.VMEM((2 * cols, lat_width), F32),
        ],
        compiler_params=grant(50),
        cost_estimate=cost(2 * parts * tokens * cols * 2 * lat_width, 8 << 20),
    )(own, mine, other, spots, grads)


def exchange(array, axis):
    return lax.all_to_all(array, axis, 0, 0, tiled=True)


def from_hops(array, axis, size, hops):
    return [lax.ppermute(array, axis, [(at, at ^ hop) for at in range(size)]) for hop in hops]


def shards(layers, parts, residual, cotangent, decoder_first, decoder_second, latent_index, latent_value, active_count):
    lat_width = decoder_first.shape[0]
    cols = decoder_second.shape[1]
    tokens = residual.shape[1]
    members = 2
    place = lax.axis_index("layer")
    own = jnp.stack([place * lat_width, place // 2 % members]).astype(jnp.int32)
    index, value = latent_index.transpose(0, 2, 1), latent_value.transpose(0, 2, 1)
    packed, rank = pack(lat_width, parts, own, cotangent, index, value, active_count)
    got = exchange(packed, "dp")
    half = pack_half(parts, own, residual)
    terms = slot_terms(decoder_first.transpose(1, 2, 0), decoder_second.T, half, got)
    slots = exchange(terms, "dp")
    spots = slot_spots(got)
    first_grad, second_grad = decoder_grads(got, spots, cols, lat_width)
    slots, first_grad = lax.optimization_barrier((slots, first_grad))
    grads, part = slot_totals(slots, rank)
    share = slots[:, tokens:, :]
    (other,) = from_hops(share, "layer", layers, (2,))
    all_grads = exchange(grads, "dp")
    part = functools.reduce(jnp.add, from_hops(part, "layer", layers, (1, 2, 3)), part)
    far = from_hops(part, "layer", layers, (4, 8, 12))
    latent_grad = functools.reduce(jnp.add, far, part)
    all_grads, latent_grad = lax.optimization_barrier((all_grads, latent_grad))
    encoder_grad = encoder_grads(own, share, other, spots, all_grads, cols, lat_width)
    return (
        first_grad.transpose(2, 0, 1),
        second_grad.T,
        encoder_grad,
        latent_grad.astype(F32).transpose(0, 2, 1),
    )


def solution(mesh):
    return jax.shard_map(
        functools.partial(shards, mesh.shape["layer"], mesh.shape["dp"]),
        mesh=mesh,
        in_specs=(
            P(None, "dp", None),
            P(None, "dp", None),
            P("layer", None, "dp"),
            P("layer", "dp"),
            P(None, "dp", None),
            P(None, "dp", None),
            P(None, "dp"),
        ),
        out_specs=(
            P("layer", None, "dp"),
            P("layer", "dp"),
            P("dp", None, "layer"),
            P(None, "dp", None),
        ),
        check_vma=False,
    )
```

```python
import functools
import jax
import jax.numpy as jnp
from jax import lax
from jax.experimental import pallas as pl
from jax.experimental.pallas import tpu as pltpu
from jax.sharding import PartitionSpec as P

BF16 = jnp.bfloat16
F32 = jnp.float32
LANES = 128
RUNS = LANES // 2
SHIFT = 256
EMPTY = 512
STREAM_MIB = 60
KERNEL_MIB = 16
TERMS_MIB = 56
SPOTS_FLOPS = 1 << 32


def grant(mib=KERNEL_MIB):
    return pltpu.CompilerParams(vmem_limit_bytes=mib << 20)


def cost(flops, moved):
    return pl.CostEstimate(flops=flops, bytes_accessed=moved, transcendentals=0)


def lane_pick(table, where):
    return jnp.take_along_axis(table, where, axis=1, mode="promise_in_bounds")


def turn(source, out_ref, base):
    dests = out_ref.shape[0]
    cols = source.shape[1] // dests
    turned = source.T
    for dest in range(dests):
        out_ref[dest, base : base + cols, :] = turned[dest * cols : (dest + 1) * cols]


def kept_slots(own_ref, idx_ref, live_ref, layer, lat_width):
    slots, tokens = idx_ref.shape[1:]
    place = lax.broadcasted_iota(jnp.int32, (slots, tokens), 0)
    local = idx_ref[layer] - own_ref[0]
    inside = (place < live_ref[layer : layer + 1, :]) & (local >= 0) & (local < lat_width)
    return place, local, inside


def pack_kernel(lat_width, own_ref, cot_ref, idx_ref, val_ref, live_ref, out_ref, rank_ref, slot_ref):
    slots, tokens = idx_ref.shape[1:]
    dests = out_ref.shape[0]
    cols = cot_ref.shape[2] // dests

    @pl.when(pl.program_id(0) == 0)
    def _():
        found, codes = [], []
        for layer in range(2):
            place, local, inside = kept_slots(own_ref, idx_ref, live_ref, layer, lat_width)
            key = (local & (RUNS - 1)) * 8 + (local >> 6)
            held_key = key - SHIFT
            key = jnp.where(inside, key, 1 << 20)
            rank = jnp.zeros((slots, tokens), jnp.int32)
            for slot in range(slots):
                rank = rank + jnp.where(key[slot : slot + 1, :] < key, 1, 0)
            rank = jnp.where(inside, rank, slots)
            rank_ref[layer] = rank
            held = jnp.full((slots, tokens), EMPTY, jnp.int32)
            value = val_ref[layer].astype(F32)
            code = jnp.zeros((slots, tokens), F32)
            for slot in range(slots):
                here = rank[slot : slot + 1, :] == place
                held = jnp.where(here, held_key[slot : slot + 1, :], held)
                code = jnp.where(here, value[slot : slot + 1, :], code)
            found.append(held.astype(F32))
            codes.append(code)
        slot_ref[0:tokens, :] = jnp.concatenate(codes, axis=0).T.astype(BF16)
        slot_ref[tokens:, :] = jnp.concatenate(found, axis=0).T.astype(BF16)

    for layer in range(2):
        turn(cot_ref[layer], out_ref, layer * cols)
    for dest in range(dests):
        out_ref[dest, 2 * cols :, :] = slot_ref[...]


def pack(lat_width, parts, start, cotangent, index, value, live):
    _, tokens, width = cotangent.shape
    slots = index.shape[1]
    steps = 4
    rows = 2 * (width // parts) + 2 * tokens
    return pl.pallas_call(
        functools.partial(pack_kernel, lat_width),
        grid_spec=pltpu.PrefetchScalarGridSpec(
            num_scalar_prefetch=1,
            grid=(steps,),
            in_specs=[
                pl.BlockSpec((2, tokens, width // steps), lambda i, own: (0, 0, i)),
                pl.BlockSpec((2, slots, tokens), lambda i, own: (0, 0, 0)),
                pl.BlockSpec((2, slots, tokens), lambda i, own: (0, 0, 0)),
                pl.BlockSpec((2, tokens), lambda i, own: (0, 0)),
            ],
            out_specs=[
                pl.BlockSpec((parts // steps, rows, tokens), lambda i, own: (i, 0, 0)),
                pl.BlockSpec((2, slots, tokens), lambda i, own: (0, 0, 0)),
            ],
            scratch_shapes=[pltpu.VMEM((2 * tokens, LANES), BF16)],
        ),
        out_shape=[
            jax.ShapeDtypeStruct((parts, rows, tokens), BF16),
            jax.ShapeDtypeStruct((2, slots, tokens), jnp.int32),
        ],
        compiler_params=grant(STREAM_MIB),
        cost_estimate=cost(0, 5 << 20),
    )(start, cotangent, index, value, live)


def half_kernel(own_ref, res_ref, out_ref):
    turn(jnp.concatenate([res_ref[own_ref[1]], res_ref[1 - own_ref[1]]], axis=0), out_ref, 0)


def pack_half(parts, own, residual):
    _, tokens, width = residual.shape
    steps = 4
    share = tokens // 2
    return pl.pallas_call(
        half_kernel,
        grid_spec=pltpu.PrefetchScalarGridSpec(
            num_scalar_prefetch=1,
            grid=(steps,),
            in_specs=[pl.BlockSpec((2, share, width // steps), lambda i, own: (0, own[1], i))],
            out_specs=pl.BlockSpec((parts // steps, width // parts, tokens), lambda i, own: (i, 0, 0)),
        ),
        out_shape=jax.ShapeDtypeStruct((parts, width // parts, tokens), BF16),
        compiler_params=grant(62),
        cost_estimate=cost(0, 2 << 20),
    )(own, residual)


def terms_kernel(wf_ref, ws_ref, half_ref, got_ref, out_ref, weight_ref):
    shards, _, tokens = got_ref.shape
    cols, lat_width = ws_ref.shape

    @pl.when(pl.program_id(0) == 0)
    def _():
        weight_ref[0:cols, 0:lat_width] = wf_ref[0]
        weight_ref[cols : 2 * cols, 0:lat_width] = wf_ref[1]
        weight_ref[0:cols, lat_width:] = jnp.zeros((cols, lat_width), BF16)
        weight_ref[cols : 2 * cols, lat_width:] = ws_ref[...]

    out_ref[:, tokens:, :] = half_ref[...]
    pair = 2
    for first in range(0, shards, pair):
        some = range(first, first + pair)
        cot = jnp.concatenate([got_ref[shard, 0 : 2 * cols, :] for shard in some], axis=1)
        dense = jnp.dot(cot.T, weight_ref[...], preferred_element_type=F32)
        held = jnp.concatenate([got_ref[shard, 2 * cols + tokens :, :] for shard in some], axis=0)
        held = held.astype(F32).astype(jnp.int32) + SHIFT
        lane = lax.broadcasted_iota(jnp.int32, held.shape, 1)
        chunks = lat_width // LANES
        chunk = ((held & 7) >> 1) + jnp.where(lane >= RUNS, chunks, 0)
        chunk = jnp.where(held < lat_width, chunk, 2 * chunks)
        within = jnp.where((held & 1) == 1, RUNS, 0) + (held >> 3)
        picked = jnp.zeros(held.shape, F32)
        for part in range(2 * chunks):
            table = dense[:, part * LANES : (part + 1) * LANES]
            picked = jnp.where(chunk == part, lane_pick(table, within), picked)
        for shard in some:
            out_ref[shard, 0:tokens, :] = picked[(shard - first) * tokens : (shard - first + 1) * tokens].astype(BF16)


def slot_terms(first, second, half, got):
    parts, rows, tokens = got.shape
    cols, lat_width = second.shape
    shards = 4
    return pl.pallas_call(
        terms_kernel,
        grid=(parts // shards,),
        in_specs=[
            pl.BlockSpec((2, cols, lat_width), lambda i: (0, 0, 0)),
            pl.BlockSpec((cols, lat_width), lambda i: (0, 0)),
            pl.BlockSpec((shards, cols, tokens), lambda i: (i, 0, 0)),
            pl.BlockSpec((shards, rows, tokens), lambda i: (i, 0, 0)),
        ],
        out_specs=pl.BlockSpec((shards, tokens + cols, LANES), lambda i: (i, 0, 0)),
        out_shape=jax.ShapeDtypeStruct((parts, tokens + cols, LANES), BF16),
        scratch_shapes=[pltpu.VMEM((2 * cols, 2 * lat_width), BF16)],
        compiler_params=grant(TERMS_MIB),
        cost_estimate=cost(2 * parts * tokens * cols * 3 * lat_width, 6 << 20),
    )(first, second, half, got)


def total_kernel(got_ref, rank_ref, grad_ref, part_ref):
    total = jnp.sum(got_ref[...].astype(F32), axis=0)
    for dest in range(grad_ref.shape[0]):
        grad_ref[dest] = total.astype(BF16)
    turned = total.T
    slots = rank_ref.shape[1]
    for layer in range(2):
        rank = rank_ref[layer]
        part = jnp.zeros(rank.shape, F32)
        for slot in range(slots):
            row = layer * slots + slot
            part = jnp.where(rank == slot, turned[row : row + 1, :], part)
        part_ref[layer] = part.astype(BF16)


def slot_totals(got, rank):
    parts = got.shape[0]
    tokens = rank.shape[2]
    return pl.pallas_call(
        total_kernel,
        grid=(1,),
        in_specs=[
            pl.BlockSpec((parts, tokens, LANES), lambda i: (0, 0, 0)),
            pl.BlockSpec(rank.shape, lambda i: (0, 0, 0)),
        ],
        out_specs=[
            pl.BlockSpec((parts, tokens, LANES), lambda i: (0, 0, 0)),
            pl.BlockSpec(rank.shape, lambda i: (0, 0, 0)),
        ],
        out_shape=[
            jax.ShapeDtypeStruct((parts, tokens, LANES), BF16),
            jax.ShapeDtypeStruct(rank.shape, BF16),
        ],
        compiler_params=grant(),
        cost_estimate=cost(0, 1 << 20),
    )(got, rank)


FEW = ((8, 4, 2, 1), 3)
ALL = ((32, 16, 8, 4, 2, 1), 8)


def spots_kernel(got_ref, spot_ref):
    shards, _, tokens = got_ref.shape
    top = got_ref.shape[1] - tokens
    lane = lax.broadcasted_iota(jnp.int32, (tokens, LANES), 1)
    place = lane & (RUNS - 1)
    base = lane & RUNS
    last = base + (RUNS - 1)
    start = 8 * place - SHIFT

    def fill(jumps, hops):
        for shard in range(shards):
            held = got_ref[shard, top:, :].astype(F32).astype(jnp.int32)
            below = base
            for jump in jumps:
                further = below + jump
                below = jnp.where(lane_pick(held, further - 1) < start, further, below)
            codes = jnp.zeros((tokens, LANES), jnp.int32)
            for hop in range(hops):
                spot = below if hop == 0 else jnp.minimum(below + hop, last)
                ahead = lane_pick(held, spot) - start
                code = jnp.where((ahead & -8) == 0, ahead + 1, 0)
                if hop > 0:
                    code = jnp.where(below + hop <= last, code, 0)
                codes = codes | jnp.left_shift(code, 4 * hop)
            spot_ref[shard, 0:tokens, :] = below
            spot_ref[shard, tokens:, :] = codes

    deep = jnp.zeros((tokens, LANES), jnp.int32)
    for shard in range(shards):
        held = got_ref[shard, top:, :].astype(F32).astype(jnp.int32)
        ahead = pltpu.roll(held, LANES - FEW[1], 1)
        crowd = ((held >> 3) == (ahead >> 3)) & (place < RUNS - FEW[1])
        many = place == sum(FEW[0])
        deep = jnp.where((held < EMPTY) & (crowd | many), 1, deep)
    deep = jnp.max(deep)

    @pl.when(deep == 0)
    def _():
        fill(*FEW)

    @pl.when(deep != 0)
    def _():
        fill(*ALL)


def slot_spots(got):
    parts, rows, tokens = got.shape
    shards = 2
    return pl.pallas_call(
        spots_kernel,
        grid=(parts // shards,),
        in_specs=[pl.BlockSpec((shards, rows, tokens), lambda i: (i, 0, 0))],
        out_specs=pl.BlockSpec((shards, 2 * tokens, LANES), lambda i: (i, 0, 0)),
        out_shape=jax.ShapeDtypeStruct((parts, 2 * tokens, LANES), jnp.int32),
        compiler_params=grant(56),
        cost_estimate=cost(SPOTS_FLOPS, 8 << 20),
    )(got)


def dense(table, below, codes, hops):
    lane = lax.broadcasted_iota(jnp.int32, below.shape, 1)
    near = lane < RUNS
    far_codes = pltpu.roll(codes, RUNS, 1)
    kept, which = ([], []), ([], [])
    for hop in range(hops):
        spot = below if hop == 0 else jnp.minimum(below + hop, LANES - 1)
        value = lane_pick(table, spot)
        far_value = pltpu.roll(value, RUNS, 1)
        code = (codes >> (4 * hop)) & 15
        far_code = (far_codes >> (4 * hop)) & 15
        kept[0].append(jnp.where(near, value, far_value))
        kept[1].append(jnp.where(near, far_value, value))
        which[0].append(jnp.where(near, code, far_code - 1))
        which[1].append(jnp.where(near, far_code, code - 1))
    for layer in range(2):
        for chunk in range(4):
            found = jnp.zeros(below.shape, F32)
            for hop in range(hops):
                found = jnp.where(which[layer][hop] == 2 * chunk + 1, kept[layer][hop], found)
            yield layer, chunk, found.astype(BF16)


def fill_dense(table_ref, top, spot_ref, out_ref, halves, product):
    shards, tokens = spot_ref.shape[0], spot_ref.shape[1] // 2
    crowd = jnp.zeros((tokens, LANES), jnp.int32)
    for shard in range(shards):
        crowd = jnp.where((spot_ref[shard, tokens:, :] >> (4 * FEW[1])) != 0, 1, crowd)
    crowd = jnp.max(crowd)

    def fill(hops, shard):
        table = table_ref[shard, top : top + tokens, :].astype(F32)
        low = shard * tokens
        if not isinstance(shard, int):
            low = pl.multiple_of(low, tokens)
        for layer, chunk, found in dense(table, spot_ref[shard, 0:tokens, :], spot_ref[shard, tokens:, :], hops):
            at = slice((4 * layer + chunk) * LANES, (4 * layer + chunk + 1) * LANES)
            if halves and layer == 1:
                half = tokens // 2
                found = jnp.concatenate([found[half:], found[:half]], axis=0)
            out_ref[pl.ds(low, tokens), at] = found

    @pl.when(crowd == 0)
    def _():
        for shard in range(shards):
            fill(FEW[1], shard)
            if shard % 2 == 1:
                product(shard - 1)

    @pl.when(crowd != 0)
    def _():
        def one(shard, carry):
            fill(ALL[1], shard)
            return carry

        lax.fori_loop(0, shards, one, 0)
        for shard in range(0, shards, 2):
            product(shard)


def codes_kernel(got_ref, spot_ref, first_ref, second_ref, code_ref, sum_ref):
    shards, tokens = spot_ref.shape[0], spot_ref.shape[1] // 2
    cols, lat_width = second_ref.shape
    step = pl.program_id(0)

    @pl.when(step == 0)
    def _():
        sum_ref[...] = jnp.zeros_like(sum_ref)

    def product(first):
        rows = slice(first * tokens, (first + 2) * tokens)
        cot = jnp.concatenate([got_ref[shard, 0 : 2 * cols, :] for shard in (first, first + 1)], axis=1)
        dot = functools.partial(jnp.dot, preferred_element_type=F32)
        sum_ref[0 : 2 * cols, :] += dot(cot, code_ref[rows, 0:lat_width])
        sum_ref[2 * cols : 3 * cols, :] += dot(cot[cols:], code_ref[rows, lat_width:])

    fill_dense(got_ref, 2 * cols, spot_ref, code_ref, False, product)

    @pl.when(step == pl.num_programs(0) - 1)
    def _():
        first_ref[0] = sum_ref[0:cols, :].astype(BF16)
        first_ref[1] = sum_ref[cols : 2 * cols, :].astype(BF16)
        second_ref[...] = sum_ref[2 * cols : 3 * cols, :].astype(BF16)


def decoder_grads(got, spots, cols, lat_width):
    parts, rows, tokens = got.shape
    shards = 4
    return pl.pallas_call(
        codes_kernel,
        grid=(parts // shards,),
        in_specs=[
            pl.BlockSpec((shards, rows, tokens), lambda i: (i, 0, 0)),
            pl.BlockSpec((shards, 2 * tokens, LANES), lambda i: (i, 0, 0)),
        ],
        out_specs=[
            pl.BlockSpec((2, cols, lat_width), lambda i: (0, 0, 0)),
            pl.BlockSpec((cols, lat_width), lambda i: (0, 0)),
        ],
        out_shape=[
            jax.ShapeDtypeStruct((2, cols, lat_width), BF16),
            jax.ShapeDtypeStruct((cols, lat_width), BF16),
        ],
        scratch_shapes=[
            pltpu.VMEM((shards * tokens, 2 * lat_width), BF16),
            pltpu.VMEM((3 * cols, lat_width), F32),
        ],
        compiler_params=grant(52),
        cost_estimate=cost(2 * parts * tokens * cols * 3 * lat_width, 8 << 20),
    )(got, spots)


def back_kernel(own_ref, mine_ref, other_ref, spot_ref, grad_ref, enc_ref, back_ref, sum_ref):
    shards, tokens = spot_ref.shape[0], spot_ref.shape[1] // 2
    cols, _, lat_width = enc_ref.shape
    step = pl.program_id(0)
    @pl.when(step == 0)
    def _():
        sum_ref[...] = jnp.zeros_like(sum_ref)

    lane = lax.broadcasted_iota(jnp.int32, (cols, tokens), 1)
    mine = (lane < RUNS) == (own_ref[1] == 0)

    def product(first):
        rows = slice(first * tokens, (first + 2) * tokens)
        sides = ([], [])
        for shard in (first, first + 1):
            one, two = mine_ref[shard].astype(F32), other_ref[shard].astype(F32)
            sides[0].append(jnp.where(mine, one, two).astype(BF16))
            sides[1].append(jnp.where(mine, two, one).astype(BF16))
        for layer in range(2):
            sum_ref[layer * cols : (layer + 1) * cols, :] += jnp.dot(
                jnp.concatenate(sides[layer], axis=1),
                back_ref[rows, layer * lat_width : (layer + 1) * lat_width],
                preferred_element_type=F32,
            )

    fill_dense(grad_ref, 0, spot_ref, back_ref, True, product)

    @pl.when(step == pl.num_programs(0) - 1)
    def _():
        enc_ref[:, 0, :] = sum_ref[0:cols, :].astype(BF16)
        enc_ref[:, 1, :] = sum_ref[cols:, :].astype(BF16)


def encoder_grads(own, mine, other, spots, grads, cols, lat_width):
    parts, tokens, _ = grads.shape
    shards = 4
    return pl.pallas_call(
        back_kernel,
        grid=(parts // shards,),
        in_specs=[
            pl.BlockSpec(memory_space=pltpu.SMEM),
            pl.BlockSpec((shards, cols, tokens), lambda i: (i, 0, 0)),
            pl.BlockSpec((shards, cols, tokens), lambda i: (i, 0, 0)),
            pl.BlockSpec((shards,) + spots.shape[1:], lambda i: (i, 0, 0)),
            pl.BlockSpec((shards, tokens, LANES), lambda i: (i, 0, 0)),
        ],
        out_specs=pl.BlockSpec((cols, 2, lat_width), lambda i: (0, 0, 0)),
        out_shape=jax.ShapeDtypeStruct((cols, 2, lat_width), BF16),
        scratch_shapes=[
            pltpu.VMEM((shards * tokens, 2 * lat_width), BF16),
            pltpu.VMEM((2 * cols, lat_width), F32),
        ],
        compiler_params=grant(50),
        cost_estimate=cost(2 * parts * tokens * cols * 2 * lat_width, 8 << 20),
    )(own, mine, other, spots, grads)


def exchange(array, axis):
    return lax.all_to_all(array, axis, 0, 0, tiled=True)


def from_hops(array, axis, size, hops):
    return [lax.ppermute(array, axis, [(at, at ^ hop) for at in range(size)]) for hop in hops]


def shards(layers, parts, residual, cotangent, decoder_first, decoder_second, latent_index, latent_value, active_count):
    lat_width = decoder_first.shape[0]
    cols = decoder_second.shape[1]
    tokens = residual.shape[1]
    members = 2
    place = lax.axis_index("layer")
    own = jnp.stack([place * lat_width, place // 2 % members]).astype(jnp.int32)
    index, value = latent_index.transpose(0, 2, 1), latent_value.transpose(0, 2, 1)
    packed, rank = pack(lat_width, parts, own, cotangent, index, value, active_count)
    got = exchange(packed, "dp")
    half = pack_half(parts, own, residual)
    terms = slot_terms(decoder_first.transpose(1, 2, 0), decoder_second.T, half, got)
    slots = exchange(terms, "dp")
    spots = slot_spots(got)
    first_grad, second_grad = decoder_grads(got, spots, cols, lat_width)
    slots, first_grad = lax.optimization_barrier((slots, first_grad))
    grads, part = slot_totals(slots, rank)
    share = slots[:, tokens:, :]
    (other,) = from_hops(share, "layer", layers, (2,))
    all_grads = exchange(grads, "dp")
    part = functools.reduce(jnp.add, from_hops(part, "layer", layers, (1, 4, 5)), part)
    far = from_hops(part, "layer", layers, (2, 8, 10))
    latent_grad = functools.reduce(jnp.add, far, part)
    all_grads, latent_grad = lax.optimization_barrier((all_grads, latent_grad))
    encoder_grad = encoder_grads(own, share, other, spots, all_grads, cols, lat_width)
    return (
        first_grad.transpose(2, 0, 1),
        second_grad.T,
        encoder_grad,
        latent_grad.astype(F32).transpose(0, 2, 1),
    )


def solution(mesh):
    return jax.shard_map(
        functools.partial(shards, mesh.shape["layer"], mesh.shape["dp"]),
        mesh=mesh,
        in_specs=(
            P(None, "dp", None),
            P(None, "dp", None),
            P("layer", None, "dp"),
            P("layer", "dp"),
            P(None, "dp", None),
            P(None, "dp", None),
            P(None, "dp"),
        ),
        out_specs=(
            P("layer", None, "dp"),
            P("layer", "dp"),
            P("dp", None, "layer"),
            P(None, "dp", None),
        ),
        check_vma=False,
    )
```

```python
import functools
import jax
import jax.numpy as jnp
from jax import lax
from jax.experimental import pallas as pl
from jax.experimental.pallas import tpu as pltpu
from jax.sharding import PartitionSpec as P

BF16 = jnp.bfloat16
F32 = jnp.float32
LANES = 128
RUNS = LANES // 2
SHIFT = 256
EMPTY = 512
STREAM_MIB = 60
KERNEL_MIB = 16
TERMS_MIB = 56
SPOTS_FLOPS = 1 << 32


def grant(mib=KERNEL_MIB):
    return pltpu.CompilerParams(vmem_limit_bytes=mib << 20)


def cost(flops, moved):
    return pl.CostEstimate(flops=flops, bytes_accessed=moved, transcendentals=0)


def lane_pick(table, where):
    return jnp.take_along_axis(table, where, axis=1, mode="promise_in_bounds")


def turn(source, out_ref, base):
    dests = out_ref.shape[0]
    cols = source.shape[1] // dests
    turned = source.T
    for dest in range(dests):
        out_ref[dest, base : base + cols, :] = turned[dest * cols : (dest + 1) * cols]


def kept_slots(own_ref, idx_ref, live_ref, layer, lat_width):
    slots, tokens = idx_ref.shape[1:]
    place = lax.broadcasted_iota(jnp.int32, (slots, tokens), 0)
    local = idx_ref[layer] - own_ref[0]
    inside = (place < live_ref[layer : layer + 1, :]) & (local >= 0) & (local < lat_width)
    return place, local, inside


def pack_kernel(lat_width, own_ref, cot_ref, idx_ref, val_ref, live_ref, out_ref, rank_ref, slot_ref):
    slots, tokens = idx_ref.shape[1:]
    dests = out_ref.shape[0]
    cols = cot_ref.shape[2] // dests

    @pl.when(pl.program_id(0) == 0)
    def _():
        found, codes = [], []
        for layer in range(2):
            place, local, inside = kept_slots(own_ref, idx_ref, live_ref, layer, lat_width)
            key = (local & (RUNS - 1)) * 8 + (local >> 6)
            held_key = key - SHIFT
            key = jnp.where(inside, key, 1 << 20)
            rank = jnp.zeros((slots, tokens), jnp.int32)
            for slot in range(slots):
                rank = rank + jnp.where(key[slot : slot + 1, :] < key, 1, 0)
            rank = jnp.where(inside, rank, slots)
            rank_ref[layer] = rank
            held = jnp.full((slots, tokens), EMPTY, jnp.int32)
            value = val_ref[layer].astype(F32)
            code = jnp.zeros((slots, tokens), F32)
            for slot in range(slots):
                here = rank[slot : slot + 1, :] == place
                held = jnp.where(here, held_key[slot : slot + 1, :], held)
                code = jnp.where(here, value[slot : slot + 1, :], code)
            found.append(held.astype(F32))
            codes.append(code)
        slot_ref[0:tokens, :] = jnp.concatenate(codes, axis=0).T.astype(BF16)
        slot_ref[tokens:, :] = jnp.concatenate(found, axis=0).T.astype(BF16)

    for layer in range(2):
        turn(cot_ref[layer], out_ref, layer * cols)
    for dest in range(dests):
        out_ref[dest, 2 * cols :, :] = slot_ref[...]


def pack(lat_width, parts, start, cotangent, index, value, live):
    _, tokens, width = cotangent.shape
    slots = index.shape[1]
    steps = 4
    rows = 2 * (width // parts) + 2 * tokens
    return pl.pallas_call(
        functools.partial(pack_kernel, lat_width),
        grid_spec=pltpu.PrefetchScalarGridSpec(
            num_scalar_prefetch=1,
            grid=(steps,),
            in_specs=[
                pl.BlockSpec((2, tokens, width // steps), lambda i, own: (0, 0, i)),
                pl.BlockSpec((2, slots, tokens), lambda i, own: (0, 0, 0)),
                pl.BlockSpec((2, slots, tokens), lambda i, own: (0, 0, 0)),
                pl.BlockSpec((2, tokens), lambda i, own: (0, 0)),
            ],
            out_specs=[
                pl.BlockSpec((parts // steps, rows, tokens), lambda i, own: (i, 0, 0)),
                pl.BlockSpec((2, slots, tokens), lambda i, own: (0, 0, 0)),
            ],
            scratch_shapes=[pltpu.VMEM((2 * tokens, LANES), BF16)],
        ),
        out_shape=[
            jax.ShapeDtypeStruct((parts, rows, tokens), BF16),
            jax.ShapeDtypeStruct((2, slots, tokens), jnp.int32),
        ],
        compiler_params=grant(STREAM_MIB),
        cost_estimate=cost(0, 5 << 20),
    )(start, cotangent, index, value, live)


def residual_kernel(res_ref, out_ref):
    cols = out_ref.shape[1] // 2
    for layer in range(2):
        turn(res_ref[layer], out_ref, layer * cols)


def pack_residual(parts, residual):
    _, tokens, width = residual.shape
    steps = 4
    rows = 2 * (width // parts)
    return pl.pallas_call(
        residual_kernel,
        grid=(steps,),
        in_specs=[pl.BlockSpec((2, tokens, width // steps), lambda i: (0, 0, i))],
        out_specs=pl.BlockSpec((parts // steps, rows, tokens), lambda i: (i, 0, 0)),
        out_shape=jax.ShapeDtypeStruct((parts, rows, tokens), BF16),
        compiler_params=grant(62),
        cost_estimate=cost(0, 4 << 20),
    )(residual)


def terms_kernel(wf_ref, ws_ref, res_ref, got_ref, out_ref, weight_ref):
    shards, _, tokens = got_ref.shape
    cols, lat_width = ws_ref.shape

    @pl.when(pl.program_id(0) == 0)
    def _():
        weight_ref[0:cols, 0:lat_width] = wf_ref[0]
        weight_ref[cols : 2 * cols, 0:lat_width] = wf_ref[1]
        weight_ref[0:cols, lat_width:] = jnp.zeros((cols, lat_width), BF16)
        weight_ref[cols : 2 * cols, lat_width:] = ws_ref[...]

    out_ref[:, tokens:, :] = res_ref[...]
    pair = 2
    for first in range(0, shards, pair):
        some = range(first, first + pair)
        cot = jnp.concatenate([got_ref[shard, 0 : 2 * cols, :] for shard in some], axis=1)
        dense = jnp.dot(cot.T, weight_ref[...], preferred_element_type=F32)
        held = jnp.concatenate([got_ref[shard, 2 * cols + tokens :, :] for shard in some], axis=0)
        held = held.astype(F32).astype(jnp.int32) + SHIFT
        lane = lax.broadcasted_iota(jnp.int32, held.shape, 1)
        chunks = lat_width // LANES
        chunk = ((held & 7) >> 1) + jnp.where(lane >= RUNS, chunks, 0)
        chunk = jnp.where(held < lat_width, chunk, 2 * chunks)
        within = jnp.where((held & 1) == 1, RUNS, 0) + (held >> 3)
        picked = jnp.zeros(held.shape, F32)
        for part in range(2 * chunks):
            table = dense[:, part * LANES : (part + 1) * LANES]
            picked = jnp.where(chunk == part, lane_pick(table, within), picked)
        for shard in some:
            out_ref[shard, 0:tokens, :] = picked[(shard - first) * tokens : (shard - first + 1) * tokens].astype(BF16)


def slot_terms(first, second, res, got):
    parts, rows, tokens = got.shape
    cols, lat_width = second.shape
    shards = 4
    return pl.pallas_call(
        terms_kernel,
        grid=(parts // shards,),
        in_specs=[
            pl.BlockSpec((2, cols, lat_width), lambda i: (0, 0, 0)),
            pl.BlockSpec((cols, lat_width), lambda i: (0, 0)),
            pl.BlockSpec((shards, 2 * cols, tokens), lambda i: (i, 0, 0)),
            pl.BlockSpec((shards, rows, tokens), lambda i: (i, 0, 0)),
        ],
        out_specs=pl.BlockSpec((shards, tokens + 2 * cols, LANES), lambda i: (i, 0, 0)),
        out_shape=jax.ShapeDtypeStruct((parts, tokens + 2 * cols, LANES), BF16),
        scratch_shapes=[pltpu.VMEM((2 * cols, 2 * lat_width), BF16)],
        compiler_params=grant(TERMS_MIB),
        cost_estimate=cost(2 * parts * tokens * cols * 3 * lat_width, 6 << 20),
    )(first, second, res, got)


def total_kernel(got_ref, rank_ref, grad_ref, part_ref):
    total = jnp.sum(got_ref[...].astype(F32), axis=0)
    for dest in range(grad_ref.shape[0]):
        grad_ref[dest] = total.astype(BF16)
    turned = total.T
    slots = rank_ref.shape[1]
    for layer in range(2):
        rank = rank_ref[layer]
        part = jnp.zeros(rank.shape, F32)
        for slot in range(slots):
            row = layer * slots + slot
            part = jnp.where(rank == slot, turned[row : row + 1, :], part)
        part_ref[layer] = part.astype(BF16)


def slot_totals(got, rank):
    parts = got.shape[0]
    tokens = rank.shape[2]
    return pl.pallas_call(
        total_kernel,
        grid=(1,),
        in_specs=[
            pl.BlockSpec((parts, tokens, LANES), lambda i: (0, 0, 0)),
            pl.BlockSpec(rank.shape, lambda i: (0, 0, 0)),
        ],
        out_specs=[
            pl.BlockSpec((parts, tokens, LANES), lambda i: (0, 0, 0)),
            pl.BlockSpec(rank.shape, lambda i: (0, 0, 0)),
        ],
        out_shape=[
            jax.ShapeDtypeStruct((parts, tokens, LANES), BF16),
            jax.ShapeDtypeStruct(rank.shape, BF16),
        ],
        compiler_params=grant(),
        cost_estimate=cost(0, 1 << 20),
    )(got, rank)


FEW = ((8, 4, 2, 1), 3)
ALL = ((32, 16, 8, 4, 2, 1), 8)


def spots_kernel(got_ref, spot_ref):
    shards, _, tokens = got_ref.shape
    top = got_ref.shape[1] - tokens
    lane = lax.broadcasted_iota(jnp.int32, (tokens, LANES), 1)
    place = lane & (RUNS - 1)
    base = lane & RUNS
    last = base + (RUNS - 1)
    start = 8 * place - SHIFT

    def fill(jumps, hops):
        for shard in range(shards):
            held = got_ref[shard, top:, :].astype(F32).astype(jnp.int32)
            below = base
            for jump in jumps:
                further = below + jump
                below = jnp.where(lane_pick(held, further - 1) < start, further, below)
            codes = jnp.zeros((tokens, LANES), jnp.int32)
            for hop in range(hops):
                spot = below if hop == 0 else jnp.minimum(below + hop, last)
                ahead = lane_pick(held, spot) - start
                code = jnp.where((ahead & -8) == 0, ahead + 1, 0)
                if hop > 0:
                    code = jnp.where(below + hop <= last, code, 0)
                codes = codes | jnp.left_shift(code, 4 * hop)
            spot_ref[shard, 0:tokens, :] = below
            spot_ref[shard, tokens:, :] = codes

    deep = jnp.zeros((tokens, LANES), jnp.int32)
    for shard in range(shards):
        held = got_ref[shard, top:, :].astype(F32).astype(jnp.int32)
        ahead = pltpu.roll(held, LANES - FEW[1], 1)
        crowd = ((held >> 3) == (ahead >> 3)) & (place < RUNS - FEW[1])
        many = place == sum(FEW[0])
        deep = jnp.where((held < EMPTY) & (crowd | many), 1, deep)
    deep = jnp.max(deep)

    @pl.when(deep == 0)
    def _():
        fill(*FEW)

    @pl.when(deep != 0)
    def _():
        fill(*ALL)


def slot_spots(got):
    parts, rows, tokens = got.shape
    shards = 2
    return pl.pallas_call(
        spots_kernel,
        grid=(parts // shards,),
        in_specs=[pl.BlockSpec((shards, rows, tokens), lambda i: (i, 0, 0))],
        out_specs=pl.BlockSpec((shards, 2 * tokens, LANES), lambda i: (i, 0, 0)),
        out_shape=jax.ShapeDtypeStruct((parts, 2 * tokens, LANES), jnp.int32),
        compiler_params=grant(56),
        cost_estimate=cost(SPOTS_FLOPS, 8 << 20),
    )(got)


def dense(table, below, codes, hops):
    lane = lax.broadcasted_iota(jnp.int32, below.shape, 1)
    near = lane < RUNS
    far_codes = pltpu.roll(codes, RUNS, 1)
    kept, which = ([], []), ([], [])
    for hop in range(hops):
        spot = below if hop == 0 else jnp.minimum(below + hop, LANES - 1)
        value = lane_pick(table, spot)
        far_value = pltpu.roll(value, RUNS, 1)
        code = (codes >> (4 * hop)) & 15
        far_code = (far_codes >> (4 * hop)) & 15
        kept[0].append(jnp.where(near, value, far_value))
        kept[1].append(jnp.where(near, far_value, value))
        which[0].append(jnp.where(near, code, far_code - 1))
        which[1].append(jnp.where(near, far_code, code - 1))
    for layer in range(2):
        for chunk in range(4):
            found = jnp.zeros(below.shape, F32)
            for hop in range(hops):
                found = jnp.where(which[layer][hop] == 2 * chunk + 1, kept[layer][hop], found)
            yield layer, chunk, found.astype(BF16)


def fill_dense(table_ref, top, spot_ref, out_ref, product):
    shards, tokens = spot_ref.shape[0], spot_ref.shape[1] // 2
    crowd = jnp.zeros((tokens, LANES), jnp.int32)
    for shard in range(shards):
        crowd = jnp.where((spot_ref[shard, tokens:, :] >> (4 * FEW[1])) != 0, 1, crowd)
    crowd = jnp.max(crowd)

    def fill(hops, shard):
        table = table_ref[shard, top : top + tokens, :].astype(F32)
        low = shard * tokens
        if not isinstance(shard, int):
            low = pl.multiple_of(low, tokens)
        for layer, chunk, found in dense(table, spot_ref[shard, 0:tokens, :], spot_ref[shard, tokens:, :], hops):
            at = slice((4 * layer + chunk) * LANES, (4 * layer + chunk + 1) * LANES)
            out_ref[pl.ds(low, tokens), at] = found

    @pl.when(crowd == 0)
    def _():
        for shard in range(shards):
            fill(FEW[1], shard)
            if shard % 2 == 1:
                product(shard - 1)

    @pl.when(crowd != 0)
    def _():
        def one(shard, carry):
            fill(ALL[1], shard)
            return carry

        lax.fori_loop(0, shards, one, 0)
        for shard in range(0, shards, 2):
            product(shard)


def codes_kernel(got_ref, spot_ref, first_ref, second_ref, code_ref, sum_ref):
    shards, tokens = spot_ref.shape[0], spot_ref.shape[1] // 2
    cols, lat_width = second_ref.shape
    step = pl.program_id(0)

    @pl.when(step == 0)
    def _():
        sum_ref[...] = jnp.zeros_like(sum_ref)

    def product(first):
        rows = slice(first * tokens, (first + 2) * tokens)
        cot = jnp.concatenate([got_ref[shard, 0 : 2 * cols, :] for shard in (first, first + 1)], axis=1)
        dot = functools.partial(jnp.dot, preferred_element_type=F32)
        sum_ref[0 : 2 * cols, :] += dot(cot, code_ref[rows, 0:lat_width])
        sum_ref[2 * cols : 3 * cols, :] += dot(cot[cols:], code_ref[rows, lat_width:])

    fill_dense(got_ref, 2 * cols, spot_ref, code_ref, product)

    @pl.when(step == pl.num_programs(0) - 1)
    def _():
        first_ref[0] = sum_ref[0:cols, :].astype(BF16)
        first_ref[1] = sum_ref[cols : 2 * cols, :].astype(BF16)
        second_ref[...] = sum_ref[2 * cols : 3 * cols, :].astype(BF16)


def decoder_grads(got, spots, cols, lat_width):
    parts, rows, tokens = got.shape
    shards = 4
    return pl.pallas_call(
        codes_kernel,
        grid=(parts // shards,),
        in_specs=[
            pl.BlockSpec((shards, rows, tokens), lambda i: (i, 0, 0)),
            pl.BlockSpec((shards, 2 * tokens, LANES), lambda i: (i, 0, 0)),
        ],
        out_specs=[
            pl.BlockSpec((2, cols, lat_width), lambda i: (0, 0, 0)),
            pl.BlockSpec((cols, lat_width), lambda i: (0, 0)),
        ],
        out_shape=[
            jax.ShapeDtypeStruct((2, cols, lat_width), BF16),
            jax.ShapeDtypeStruct((cols, lat_width), BF16),
        ],
        scratch_shapes=[
            pltpu.VMEM((shards * tokens, 2 * lat_width), BF16),
            pltpu.VMEM((3 * cols, lat_width), F32),
        ],
        compiler_params=grant(52),
        cost_estimate=cost(2 * parts * tokens * cols * 3 * lat_width, 8 << 20),
    )(got, spots)


def back_kernel(res_ref, spot_ref, grad_ref, enc_ref, back_ref, sum_ref):
    shards, tokens = spot_ref.shape[0], spot_ref.shape[1] // 2
    cols, _, lat_width = enc_ref.shape
    step = pl.program_id(0)
    @pl.when(step == 0)
    def _():
        sum_ref[...] = jnp.zeros_like(sum_ref)

    def product(first):
        rows = slice(first * tokens, (first + 2) * tokens)
        for layer in range(2):
            low = tokens + layer * cols
            res = jnp.concatenate([res_ref[shard, low : low + cols, :] for shard in (first, first + 1)], axis=1)
            sum_ref[layer * cols : (layer + 1) * cols, :] += jnp.dot(
                res, back_ref[rows, layer * lat_width : (layer + 1) * lat_width], preferred_element_type=F32
            )

    fill_dense(grad_ref, 0, spot_ref, back_ref, product)

    @pl.when(step == pl.num_programs(0) - 1)
    def _():
        enc_ref[:, 0, :] = sum_ref[0:cols, :].astype(BF16)
        enc_ref[:, 1, :] = sum_ref[cols:, :].astype(BF16)


def encoder_grads(slots, spots, grads, cols, lat_width):
    parts, tokens, _ = grads.shape
    shards = 4
    return pl.pallas_call(
        back_kernel,
        grid=(parts // shards,),
        in_specs=[
            pl.BlockSpec((shards,) + slots.shape[1:], lambda i: (i, 0, 0)),
            pl.BlockSpec((shards,) + spots.shape[1:], lambda i: (i, 0, 0)),
            pl.BlockSpec((shards, tokens, LANES), lambda i: (i, 0, 0)),
        ],
        out_specs=pl.BlockSpec((cols, 2, lat_width), lambda i: (0, 0, 0)),
        out_shape=jax.ShapeDtypeStruct((cols, 2, lat_width), BF16),
        scratch_shapes=[
            pltpu.VMEM((shards * tokens, 2 * lat_width), BF16),
            pltpu.VMEM((2 * cols, lat_width), F32),
        ],
        compiler_params=grant(53),
        cost_estimate=cost(2 * parts * tokens * cols * 2 * lat_width, 8 << 20),
    )(slots, spots, grads)


def exchange(array, axis):
    return lax.all_to_all(array, axis, 0, 0, tiled=True)


def from_hops(array, axis, size, hops):
    return [lax.ppermute(array, axis, [(at, at ^ hop) for at in range(size)]) for hop in hops]


def shards(layers, parts, residual, cotangent, decoder_first, decoder_second, latent_index, latent_value, active_count):
    lat_width = decoder_first.shape[0]
    cols = decoder_second.shape[1]
    own = (lax.axis_index("layer") * lat_width).astype(jnp.int32).reshape(1)
    index, value = latent_index.transpose(0, 2, 1), latent_value.transpose(0, 2, 1)
    packed, rank = pack(lat_width, parts, own, cotangent, index, value, active_count)
    got = exchange(packed, "dp")
    res = pack_residual(parts, residual)
    terms = slot_terms(decoder_first.transpose(1, 2, 0), decoder_second.T, res, got)
    slots = exchange(terms, "dp")
    spots = slot_spots(got)
    first_grad, second_grad = decoder_grads(got, spots, cols, lat_width)
    slots, first_grad = lax.optimization_barrier((slots, first_grad))
    grads, part = slot_totals(slots, rank)
    all_grads = exchange(grads, "dp")
    part = functools.reduce(jnp.add, from_hops(part, "layer", layers, (1, 2, 3)), part)
    far = from_hops(part, "layer", layers, (4, 8, 12))
    latent_grad = functools.reduce(jnp.add, far, part)
    all_grads, latent_grad = lax.optimization_barrier((all_grads, latent_grad))
    encoder_grad = encoder_grads(slots, spots, all_grads, cols, lat_width)
    return (
        first_grad.transpose(2, 0, 1),
        second_grad.T,
        encoder_grad,
        latent_grad.astype(F32).transpose(0, 2, 1),
    )


def solution(mesh):
    return jax.shard_map(
        functools.partial(shards, mesh.shape["layer"], mesh.shape["dp"]),
        mesh=mesh,
        in_specs=(
            P(None, "dp", None),
            P(None, "dp", None),
            P("layer", None, "dp"),
            P("layer", "dp"),
            P(None, "dp", None),
            P(None, "dp", None),
            P(None, "dp"),
        ),
        out_specs=(
            P("layer", None, "dp"),
            P("layer", "dp"),
            P("dp", None, "layer"),
            P(None, "dp", None),
        ),
        check_vma=False,
    )
```

```python
import functools
import jax
import jax.numpy as jnp
from jax import lax
from jax.experimental import pallas as pl
from jax.experimental.pallas import tpu as pltpu
from jax.sharding import PartitionSpec as P

BF16 = jnp.bfloat16
F32 = jnp.float32
LANES = 128
RUNS = LANES // 2
SHIFT = 256
EMPTY = 512
STREAM_MIB = 60
KERNEL_MIB = 16
TERMS_MIB = 56
SPOTS_FLOPS = 1 << 32


def grant(mib=KERNEL_MIB):
    return pltpu.CompilerParams(vmem_limit_bytes=mib << 20)


def cost(flops, moved):
    return pl.CostEstimate(flops=flops, bytes_accessed=moved, transcendentals=0)


def lane_pick(table, where):
    return jnp.take_along_axis(table, where, axis=1, mode="promise_in_bounds")


def turn(source, out_ref, base):
    dests = out_ref.shape[0]
    cols = source.shape[1] // dests
    turned = source.T
    for dest in range(dests):
        out_ref[dest, base : base + cols, :] = turned[dest * cols : (dest + 1) * cols]


def kept_slots(own_ref, idx_ref, live_ref, layer, lat_width):
    slots, tokens = idx_ref.shape[1:]
    place = lax.broadcasted_iota(jnp.int32, (slots, tokens), 0)
    local = idx_ref[layer] - own_ref[0]
    inside = (place < live_ref[layer : layer + 1, :]) & (local >= 0) & (local < lat_width)
    return place, local, inside


def pack_kernel(lat_width, own_ref, cot_ref, idx_ref, val_ref, live_ref, out_ref, rank_ref, slot_ref):
    slots, tokens = idx_ref.shape[1:]
    dests = out_ref.shape[0]
    cols = cot_ref.shape[2] // dests

    @pl.when(pl.program_id(0) == 0)
    def _():
        found, codes = [], []
        for layer in range(2):
            place, local, inside = kept_slots(own_ref, idx_ref, live_ref, layer, lat_width)
            key = (local & (RUNS - 1)) * 8 + (local >> 6)
            held_key = key - SHIFT
            key = jnp.where(inside, key, 1 << 20)
            rank = jnp.zeros((slots, tokens), jnp.int32)
            for slot in range(slots):
                rank = rank + jnp.where(key[slot : slot + 1, :] < key, 1, 0)
            rank = jnp.where(inside, rank, slots)
            rank_ref[layer] = rank
            held = jnp.full((slots, tokens), EMPTY, jnp.int32)
            value = val_ref[layer].astype(F32)
            code = jnp.zeros((slots, tokens), F32)
            for slot in range(slots):
                here = rank[slot : slot + 1, :] == place
                held = jnp.where(here, held_key[slot : slot + 1, :], held)
                code = jnp.where(here, value[slot : slot + 1, :], code)
            found.append(held.astype(F32))
            codes.append(code)
        slot_ref[0:tokens, :] = jnp.concatenate(codes, axis=0).T.astype(BF16)
        slot_ref[tokens:, :] = jnp.concatenate(found, axis=0).T.astype(BF16)

    for layer in range(2):
        turn(cot_ref[layer], out_ref, layer * cols)
    for dest in range(dests):
        out_ref[dest, 2 * cols :, :] = slot_ref[...]


def pack(lat_width, parts, start, cotangent, index, value, live):
    _, tokens, width = cotangent.shape
    slots = index.shape[1]
    steps = 4
    rows = 2 * (width // parts) + 2 * tokens
    return pl.pallas_call(
        functools.partial(pack_kernel, lat_width),
        grid_spec=pltpu.PrefetchScalarGridSpec(
            num_scalar_prefetch=1,
            grid=(steps,),
            in_specs=[
                pl.BlockSpec((2, tokens, width // steps), lambda i, own: (0, 0, i)),
                pl.BlockSpec((2, slots, tokens), lambda i, own: (0, 0, 0)),
                pl.BlockSpec((2, slots, tokens), lambda i, own: (0, 0, 0)),
                pl.BlockSpec((2, tokens), lambda i, own: (0, 0)),
            ],
            out_specs=[
                pl.BlockSpec((parts // steps, rows, tokens), lambda i, own: (i, 0, 0)),
                pl.BlockSpec((2, slots, tokens), lambda i, own: (0, 0, 0)),
            ],
            scratch_shapes=[pltpu.VMEM((2 * tokens, LANES), BF16)],
        ),
        out_shape=[
            jax.ShapeDtypeStruct((parts, rows, tokens), BF16),
            jax.ShapeDtypeStruct((2, slots, tokens), jnp.int32),
        ],
        compiler_params=grant(STREAM_MIB),
        cost_estimate=cost(0, 5 << 20),
    )(start, cotangent, index, value, live)


def residual_kernel(res_ref, out_ref):
    cols = out_ref.shape[1] // 2
    for layer in range(2):
        turn(res_ref[layer], out_ref, layer * cols)


def pack_residual(parts, residual):
    _, tokens, width = residual.shape
    steps = 4
    rows = 2 * (width // parts)
    return pl.pallas_call(
        residual_kernel,
        grid=(steps,),
        in_specs=[pl.BlockSpec((2, tokens, width // steps), lambda i: (0, 0, i))],
        out_specs=pl.BlockSpec((parts // steps, rows, tokens), lambda i: (i, 0, 0)),
        out_shape=jax.ShapeDtypeStruct((parts, rows, tokens), BF16),
        compiler_params=grant(62),
        cost_estimate=cost(0, 4 << 20),
    )(residual)


def terms_kernel(wf_ref, ws_ref, res_ref, got_ref, out_ref, weight_ref):
    shards, _, tokens = got_ref.shape
    cols, lat_width = ws_ref.shape

    @pl.when(pl.program_id(0) == 0)
    def _():
        weight_ref[0:cols, 0:lat_width] = wf_ref[0]
        weight_ref[cols : 2 * cols, 0:lat_width] = wf_ref[1]
        weight_ref[0:cols, lat_width:] = jnp.zeros((cols, lat_width), BF16)
        weight_ref[cols : 2 * cols, lat_width:] = ws_ref[...]

    out_ref[:, tokens:, :] = res_ref[...]
    pair = 2
    for first in range(0, shards, pair):
        some = range(first, first + pair)
        cot = jnp.concatenate([got_ref[shard, 0 : 2 * cols, :] for shard in some], axis=1)
        dense = jnp.dot(cot.T, weight_ref[...], preferred_element_type=F32)
        held = jnp.concatenate([got_ref[shard, 2 * cols + tokens :, :] for shard in some], axis=0)
        held = held.astype(F32).astype(jnp.int32) + SHIFT
        lane = lax.broadcasted_iota(jnp.int32, held.shape, 1)
        chunks = lat_width // LANES
        chunk = ((held & 7) >> 1) + jnp.where(lane >= RUNS, chunks, 0)
        chunk = jnp.where(held < lat_width, chunk, 2 * chunks)
        within = jnp.where((held & 1) == 1, RUNS, 0) + (held >> 3)
        picked = jnp.zeros(held.shape, F32)
        for part in range(2 * chunks):
            table = dense[:, part * LANES : (part + 1) * LANES]
            picked = jnp.where(chunk == part, lane_pick(table, within), picked)
        for shard in some:
            out_ref[shard, 0:tokens, :] = picked[(shard - first) * tokens : (shard - first + 1) * tokens].astype(BF16)


def slot_terms(first, second, res, got):
    parts, rows, tokens = got.shape
    cols, lat_width = second.shape
    shards = 4
    return pl.pallas_call(
        terms_kernel,
        grid=(parts // shards,),
        in_specs=[
            pl.BlockSpec((2, cols, lat_width), lambda i: (0, 0, 0)),
            pl.BlockSpec((cols, lat_width), lambda i: (0, 0)),
            pl.BlockSpec((shards, 2 * cols, tokens), lambda i: (i, 0, 0)),
            pl.BlockSpec((shards, rows, tokens), lambda i: (i, 0, 0)),
        ],
        out_specs=pl.BlockSpec((shards, tokens + 2 * cols, LANES), lambda i: (i, 0, 0)),
        out_shape=jax.ShapeDtypeStruct((parts, tokens + 2 * cols, LANES), BF16),
        scratch_shapes=[pltpu.VMEM((2 * cols, 2 * lat_width), BF16)],
        compiler_params=grant(TERMS_MIB),
        cost_estimate=cost(2 * parts * tokens * cols * 3 * lat_width, 6 << 20),
    )(first, second, res, got)


def total_kernel(got_ref, grad_ref):
    total = jnp.sum(got_ref[...].astype(F32), axis=0).astype(BF16)
    for dest in range(grad_ref.shape[0]):
        grad_ref[dest] = total


def slot_totals(got, tokens):
    parts = got.shape[0]
    return pl.pallas_call(
        total_kernel,
        grid=(1,),
        in_specs=[pl.BlockSpec((parts, tokens, LANES), lambda i: (0, 0, 0))],
        out_specs=pl.BlockSpec((parts, tokens, LANES), lambda i: (0, 0, 0)),
        out_shape=jax.ShapeDtypeStruct((parts, tokens, LANES), BF16),
        compiler_params=grant(),
        cost_estimate=cost(0, 1 << 20),
    )(got)


def part_kernel(grad_ref, rank_ref, part_ref):
    turned = grad_ref[0].astype(F32).T
    slots = rank_ref.shape[1]
    for layer in range(2):
        rank = rank_ref[layer]
        part = jnp.zeros(rank.shape, F32)
        for slot in range(slots):
            row = layer * slots + slot
            part = jnp.where(rank == slot, turned[row : row + 1, :], part)
        part_ref[layer] = part.astype(BF16)


def slot_part(grads, rank):
    _, tokens, _ = grads.shape
    return pl.pallas_call(
        part_kernel,
        grid=(1,),
        in_specs=[
            pl.BlockSpec((1, tokens, LANES), lambda i: (0, 0, 0)),
            pl.BlockSpec(rank.shape, lambda i: (0, 0, 0)),
        ],
        out_specs=pl.BlockSpec(rank.shape, lambda i: (0, 0, 0)),
        out_shape=jax.ShapeDtypeStruct(rank.shape, BF16),
        compiler_params=grant(),
        cost_estimate=cost(0, 1 << 20),
    )(grads, rank)


FEW = ((8, 4, 2, 1), 3)
ALL = ((32, 16, 8, 4, 2, 1), 8)


def spots_kernel(got_ref, spot_ref):
    shards, _, tokens = got_ref.shape
    top = got_ref.shape[1] - tokens
    lane = lax.broadcasted_iota(jnp.int32, (tokens, LANES), 1)
    place = lane & (RUNS - 1)
    base = lane & RUNS
    last = base + (RUNS - 1)
    start = 8 * place - SHIFT

    def fill(jumps, hops):
        for shard in range(shards):
            held = got_ref[shard, top:, :].astype(F32).astype(jnp.int32)
            below = base
            for jump in jumps:
                further = below + jump
                below = jnp.where(lane_pick(held, further - 1) < start, further, below)
            codes = jnp.zeros((tokens, LANES), jnp.int32)
            for hop in range(hops):
                spot = below if hop == 0 else jnp.minimum(below + hop, last)
                ahead = lane_pick(held, spot) - start
                code = jnp.where((ahead & -8) == 0, ahead + 1, 0)
                if hop > 0:
                    code = jnp.where(below + hop <= last, code, 0)
                codes = codes | jnp.left_shift(code, 4 * hop)
            spot_ref[shard, 0:tokens, :] = below
            spot_ref[shard, tokens:, :] = codes

    deep = jnp.zeros((tokens, LANES), jnp.int32)
    for shard in range(shards):
        held = got_ref[shard, top:, :].astype(F32).astype(jnp.int32)
        ahead = pltpu.roll(held, LANES - FEW[1], 1)
        crowd = ((held >> 3) == (ahead >> 3)) & (place < RUNS - FEW[1])
        many = place == sum(FEW[0])
        deep = jnp.where((held < EMPTY) & (crowd | many), 1, deep)
    deep = jnp.max(deep)

    @pl.when(deep == 0)
    def _():
        fill(*FEW)

    @pl.when(deep != 0)
    def _():
        fill(*ALL)


def slot_spots(got):
    parts, rows, tokens = got.shape
    shards = 2
    return pl.pallas_call(
        spots_kernel,
        grid=(parts // shards,),
        in_specs=[pl.BlockSpec((shards, rows, tokens), lambda i: (i, 0, 0))],
        out_specs=pl.BlockSpec((shards, 2 * tokens, LANES), lambda i: (i, 0, 0)),
        out_shape=jax.ShapeDtypeStruct((parts, 2 * tokens, LANES), jnp.int32),
        compiler_params=grant(56),
        cost_estimate=cost(SPOTS_FLOPS, 8 << 20),
    )(got)


def dense(table, below, codes, hops):
    lane = lax.broadcasted_iota(jnp.int32, below.shape, 1)
    near = lane < RUNS
    far_codes = pltpu.roll(codes, RUNS, 1)
    kept, which = ([], []), ([], [])
    for hop in range(hops):
        spot = below if hop == 0 else jnp.minimum(below + hop, LANES - 1)
        value = lane_pick(table, spot)
        far_value = pltpu.roll(value, RUNS, 1)
        code = (codes >> (4 * hop)) & 15
        far_code = (far_codes >> (4 * hop)) & 15
        kept[0].append(jnp.where(near, value, far_value))
        kept[1].append(jnp.where(near, far_value, value))
        which[0].append(jnp.where(near, code, far_code - 1))
        which[1].append(jnp.where(near, far_code, code - 1))
    for layer in range(2):
        for chunk in range(4):
            found = jnp.zeros(below.shape, F32)
            for hop in range(hops):
                found = jnp.where(which[layer][hop] == 2 * chunk + 1, kept[layer][hop], found)
            yield layer, chunk, found.astype(BF16)


def fill_dense(table_ref, top, spot_ref, out_ref, product):
    shards, tokens = spot_ref.shape[0], spot_ref.shape[1] // 2
    crowd = jnp.zeros((tokens, LANES), jnp.int32)
    for shard in range(shards):
        crowd = jnp.where((spot_ref[shard, tokens:, :] >> (4 * FEW[1])) != 0, 1, crowd)
    crowd = jnp.max(crowd)

    def fill(hops, shard):
        table = table_ref[shard, top : top + tokens, :].astype(F32)
        low = shard * tokens
        if not isinstance(shard, int):
            low = pl.multiple_of(low, tokens)
        for layer, chunk, found in dense(table, spot_ref[shard, 0:tokens, :], spot_ref[shard, tokens:, :], hops):
            at = slice((4 * layer + chunk) * LANES, (4 * layer + chunk + 1) * LANES)
            out_ref[pl.ds(low, tokens), at] = found

    @pl.when(crowd == 0)
    def _():
        for shard in range(shards):
            fill(FEW[1], shard)
            if shard % 2 == 1:
                product(shard - 1)

    @pl.when(crowd != 0)
    def _():
        def one(shard, carry):
            fill(ALL[1], shard)
            return carry

        lax.fori_loop(0, shards, one, 0)
        for shard in range(0, shards, 2):
            product(shard)


def codes_kernel(got_ref, spot_ref, first_ref, second_ref, code_ref, sum_ref):
    shards, tokens = spot_ref.shape[0], spot_ref.shape[1] // 2
    cols, lat_width = second_ref.shape
    step = pl.program_id(0)

    @pl.when(step == 0)
    def _():
        sum_ref[...] = jnp.zeros_like(sum_ref)

    def product(first):
        rows = slice(first * tokens, (first + 2) * tokens)
        cot = jnp.concatenate([got_ref[shard, 0 : 2 * cols, :] for shard in (first, first + 1)], axis=1)
        dot = functools.partial(jnp.dot, preferred_element_type=F32)
        sum_ref[0 : 2 * cols, :] += dot(cot, code_ref[rows, 0:lat_width])
        sum_ref[2 * cols : 3 * cols, :] += dot(cot[cols:], code_ref[rows, lat_width:])

    fill_dense(got_ref, 2 * cols, spot_ref, code_ref, product)

    @pl.when(step == pl.num_programs(0) - 1)
    def _():
        first_ref[0] = sum_ref[0:cols, :].astype(BF16)
        first_ref[1] = sum_ref[cols : 2 * cols, :].astype(BF16)
        second_ref[...] = sum_ref[2 * cols : 3 * cols, :].astype(BF16)


def decoder_grads(got, spots, cols, lat_width):
    parts, rows, tokens = got.shape
    shards = 4
    return pl.pallas_call(
        codes_kernel,
        grid=(parts // shards,),
        in_specs=[
            pl.BlockSpec((shards, rows, tokens), lambda i: (i, 0, 0)),
            pl.BlockSpec((shards, 2 * tokens, LANES), lambda i: (i, 0, 0)),
        ],
        out_specs=[
            pl.BlockSpec((2, cols, lat_width), lambda i: (0, 0, 0)),
            pl.BlockSpec((cols, lat_width), lambda i: (0, 0)),
        ],
        out_shape=[
            jax.ShapeDtypeStruct((2, cols, lat_width), BF16),
            jax.ShapeDtypeStruct((cols, lat_width), BF16),
        ],
        scratch_shapes=[
            pltpu.VMEM((shards * tokens, 2 * lat_width), BF16),
            pltpu.VMEM((3 * cols, lat_width), F32),
        ],
        compiler_params=grant(52),
        cost_estimate=cost(2 * parts * tokens * cols * 3 * lat_width, 8 << 20),
    )(got, spots)


def back_kernel(res_ref, spot_ref, grad_ref, enc_ref, back_ref, sum_ref):
    shards, tokens = spot_ref.shape[0], spot_ref.shape[1] // 2
    cols, _, lat_width = enc_ref.shape
    step = pl.program_id(0)
    @pl.when(step == 0)
    def _():
        sum_ref[...] = jnp.zeros_like(sum_ref)

    def product(first):
        rows = slice(first * tokens, (first + 2) * tokens)
        for layer in range(2):
            low = tokens + layer * cols
            res = jnp.concatenate([res_ref[shard, low : low + cols, :] for shard in (first, first + 1)], axis=1)
            sum_ref[layer * cols : (layer + 1) * cols, :] += jnp.dot(
                res, back_ref[rows, layer * lat_width : (layer + 1) * lat_width], preferred_element_type=F32
            )

    fill_dense(grad_ref, 0, spot_ref, back_ref, product)

    @pl.when(step == pl.num_programs(0) - 1)
    def _():
        enc_ref[:, 0, :] = sum_ref[0:cols, :].astype(BF16)
        enc_ref[:, 1, :] = sum_ref[cols:, :].astype(BF16)


def encoder_grads(slots, spots, grads, cols, lat_width):
    parts, tokens, _ = grads.shape
    shards = 4
    return pl.pallas_call(
        back_kernel,
        grid=(parts // shards,),
        in_specs=[
            pl.BlockSpec((shards,) + slots.shape[1:], lambda i: (i, 0, 0)),
            pl.BlockSpec((shards,) + spots.shape[1:], lambda i: (i, 0, 0)),
            pl.BlockSpec((shards, tokens, LANES), lambda i: (i, 0, 0)),
        ],
        out_specs=pl.BlockSpec((cols, 2, lat_width), lambda i: (0, 0, 0)),
        out_shape=jax.ShapeDtypeStruct((cols, 2, lat_width), BF16),
        scratch_shapes=[
            pltpu.VMEM((shards * tokens, 2 * lat_width), BF16),
            pltpu.VMEM((2 * cols, lat_width), F32),
        ],
        compiler_params=grant(53),
        cost_estimate=cost(2 * parts * tokens * cols * 2 * lat_width, 8 << 20),
    )(slots, spots, grads)


def exchange(array, axis):
    return lax.all_to_all(array, axis, 0, 0, tiled=True)


def from_hops(array, axis, size, hops):
    return [lax.ppermute(array, axis, [(at, at ^ hop) for at in range(size)]) for hop in hops]


def shards(layers, parts, residual, cotangent, decoder_first, decoder_second, latent_index, latent_value, active_count):
    lat_width = decoder_first.shape[0]
    cols = decoder_second.shape[1]
    own = (lax.axis_index("layer") * lat_width).astype(jnp.int32).reshape(1)
    index, value = latent_index.transpose(0, 2, 1), latent_value.transpose(0, 2, 1)
    packed, rank = pack(lat_width, parts, own, cotangent, index, value, active_count)
    got = exchange(packed, "dp")
    res = pack_residual(parts, residual)
    terms = slot_terms(decoder_first.transpose(1, 2, 0), decoder_second.T, res, got)
    slots = exchange(terms, "dp")
    spots = slot_spots(got)
    first_grad, second_grad = decoder_grads(got, spots, cols, lat_width)
    slots, first_grad = lax.optimization_barrier((slots, first_grad))
    grads = slot_totals(slots, rank.shape[2])
    part = slot_part(grads, rank)
    all_grads = exchange(grads, "dp")
    part = functools.reduce(jnp.add, from_hops(part, "layer", layers, (1, 2, 3)), part)
    far = from_hops(part, "layer", layers, (4, 8, 12))
    encoder_grad = encoder_grads(slots, spots, all_grads, cols, lat_width)
    *far, encoder_grad = lax.optimization_barrier((*far, encoder_grad))
    latent_grad = functools.reduce(jnp.add, far, part)
    return (
        first_grad.transpose(2, 0, 1),
        second_grad.T,
        encoder_grad,
        latent_grad.astype(F32).transpose(0, 2, 1),
    )


def solution(mesh):
    return jax.shard_map(
        functools.partial(shards, mesh.shape["layer"], mesh.shape["dp"]),
        mesh=mesh,
        in_specs=(
            P(None, "dp", None),
            P(None, "dp", None),
            P("layer", None, "dp"),
            P("layer", "dp"),
            P(None, "dp", None),
            P(None, "dp", None),
            P(None, "dp"),
        ),
        out_specs=(
            P("layer", None, "dp"),
            P("layer", "dp"),
            P("dp", None, "layer"),
            P(None, "dp", None),
        ),
        check_vma=False,
    )
```

```python
import functools
import jax
import jax.numpy as jnp
from jax import lax
from jax.experimental import pallas as pl
from jax.experimental.pallas import tpu as pltpu
from jax.sharding import PartitionSpec as P

BF16 = jnp.bfloat16
F32 = jnp.float32
LANES = 128
RUNS = LANES // 2
SHIFT = 256
EMPTY = 512
STREAM_MIB = 60
KERNEL_MIB = 16
TERMS_MIB = 56
SPOTS_FLOPS = 1 << 32


def grant(mib=KERNEL_MIB):
    return pltpu.CompilerParams(vmem_limit_bytes=mib << 20)


def cost(flops, moved):
    return pl.CostEstimate(flops=flops, bytes_accessed=moved, transcendentals=0)


def lane_pick(table, where):
    return jnp.take_along_axis(table, where, axis=1, mode="promise_in_bounds")


def turn(source, out_ref, base):
    dests = out_ref.shape[0]
    cols = source.shape[1] // dests
    turned = source.T
    for dest in range(dests):
        out_ref[dest, base : base + cols, :] = turned[dest * cols : (dest + 1) * cols]


def kept_slots(own_ref, idx_ref, live_ref, layer, lat_width):
    slots, tokens = idx_ref.shape[1:]
    place = lax.broadcasted_iota(jnp.int32, (slots, tokens), 0)
    local = idx_ref[layer] - own_ref[0] * lat_width
    inside = (place < live_ref[layer : layer + 1, :]) & (local >= 0) & (local < lat_width)
    return place, local, inside


def pack_kernel(lat_width, own_ref, cot_ref, idx_ref, live_ref, out_ref, rank_ref, slot_ref):
    slots, tokens = idx_ref.shape[1:]
    dests = out_ref.shape[0]
    cols = cot_ref.shape[2] // dests

    @pl.when(pl.program_id(0) == 0)
    def _():
        found = []
        for layer in range(2):
            place, local, inside = kept_slots(own_ref, idx_ref, live_ref, layer, lat_width)
            key = (local & (RUNS - 1)) * 8 + (local >> 6)
            held_key = key - SHIFT
            key = jnp.where(inside, key, 1 << 20)
            rank = jnp.zeros((slots, tokens), jnp.int32)
            for slot in range(slots):
                rank = rank + jnp.where(key[slot : slot + 1, :] < key, 1, 0)
            rank = jnp.where(inside, rank, slots)
            rank_ref[layer] = rank
            held = jnp.full((slots, tokens), EMPTY, jnp.int32)
            for slot in range(slots):
                held = jnp.where(rank[slot : slot + 1, :] == place, held_key[slot : slot + 1, :], held)
            found.append(held.astype(F32))
        slot_ref[...] = jnp.concatenate(found, axis=0).T.astype(BF16)

    for layer in range(2):
        turn(cot_ref[layer], out_ref, layer * cols)
    for dest in range(dests):
        out_ref[dest, 2 * cols :, :] = slot_ref[...]


def pack(lat_width, parts, start, cotangent, index, live):
    _, tokens, width = cotangent.shape
    slots = index.shape[1]
    steps = 4
    rows = 2 * (width // parts) + tokens
    return pl.pallas_call(
        functools.partial(pack_kernel, lat_width),
        grid_spec=pltpu.PrefetchScalarGridSpec(
            num_scalar_prefetch=1,
            grid=(steps,),
            in_specs=[
                pl.BlockSpec((2, tokens, width // steps), lambda i, own: (0, 0, i)),
                pl.BlockSpec((2, slots, tokens), lambda i, own: (0, 0, 0)),
                pl.BlockSpec((2, tokens), lambda i, own: (0, 0)),
            ],
            out_specs=[
                pl.BlockSpec((parts // steps, rows, tokens), lambda i, own: (i, 0, 0)),
                pl.BlockSpec((2, slots, tokens), lambda i, own: (0, 0, 0)),
            ],
            scratch_shapes=[pltpu.VMEM((tokens, LANES), BF16)],
        ),
        out_shape=[
            jax.ShapeDtypeStruct((parts, rows, tokens), BF16),
            jax.ShapeDtypeStruct((2, slots, tokens), jnp.int32),
        ],
        compiler_params=grant(STREAM_MIB),
        cost_estimate=cost(0, 5 << 20),
    )(start, cotangent, index, live)


def half_of(own):
    return (own[0] >> 1) & 1


def half_kernel(own_ref, res_ref, out_ref):
    side = half_of(own_ref)
    turn(jnp.concatenate([res_ref[side], res_ref[1 - side]], axis=0), out_ref, 0)


def pack_half(parts, own, residual):
    _, tokens, width = residual.shape
    steps = 4
    share = tokens // 2
    return pl.pallas_call(
        half_kernel,
        grid_spec=pltpu.PrefetchScalarGridSpec(
            num_scalar_prefetch=1,
            grid=(steps,),
            in_specs=[pl.BlockSpec((2, share, width // steps), lambda i, own: (0, half_of(own), i))],
            out_specs=pl.BlockSpec((parts // steps, width // parts, tokens), lambda i, own: (i, 0, 0)),
        ),
        out_shape=jax.ShapeDtypeStruct((parts, width // parts, tokens), BF16),
        compiler_params=grant(62),
        cost_estimate=cost(0, 2 << 20),
    )(own, residual)


def values_kernel(rank_ref, val_ref, out_ref):
    slots, tokens = val_ref.shape[1:]
    place = lax.broadcasted_iota(jnp.int32, (slots, tokens), 0)
    codes = []
    for layer in range(2):
        rank = rank_ref[layer]
        value = val_ref[layer].astype(F32)
        code = jnp.zeros((slots, tokens), F32)
        for slot in range(slots):
            code = jnp.where(rank[slot : slot + 1, :] == place, value[slot : slot + 1, :], code)
        codes.append(code)
    out_ref[...] = jnp.concatenate(codes, axis=0).T.astype(BF16)


def slot_values(rank, value):
    return pl.pallas_call(
        values_kernel,
        out_shape=jax.ShapeDtypeStruct((value.shape[2], LANES), BF16),
        compiler_params=grant(62),
        cost_estimate=cost(0, 1 << 20),
    )(rank, value)


def terms_kernel(wf_ref, ws_ref, val_ref, half_ref, got_ref, out_ref, weight_ref):
    shards, _, tokens = got_ref.shape
    cols, lat_width = ws_ref.shape

    @pl.when(pl.program_id(0) == 0)
    def _():
        weight_ref[0:cols, 0:lat_width] = wf_ref[0]
        weight_ref[cols : 2 * cols, 0:lat_width] = wf_ref[1]
        weight_ref[0:cols, lat_width:] = jnp.zeros((cols, lat_width), BF16)
        weight_ref[cols : 2 * cols, lat_width:] = ws_ref[...]

    out_ref[:, 2 * tokens :, :] = half_ref[...]
    pair = 2
    for first in range(0, shards, pair):
        some = range(first, first + pair)
        cot = jnp.concatenate([got_ref[shard, 0 : 2 * cols, :] for shard in some], axis=1)
        dense = jnp.dot(cot.T, weight_ref[...], preferred_element_type=F32)
        held = jnp.concatenate([got_ref[shard, 2 * cols :, :] for shard in some], axis=0)
        held = held.astype(F32).astype(jnp.int32) + SHIFT
        lane = lax.broadcasted_iota(jnp.int32, held.shape, 1)
        chunks = lat_width // LANES
        chunk = ((held & 7) >> 1) + jnp.where(lane >= RUNS, chunks, 0)
        chunk = jnp.where(held < lat_width, chunk, 2 * chunks)
        within = jnp.where((held & 1) == 1, RUNS, 0) + (held >> 3)
        picked = jnp.zeros(held.shape, F32)
        for part in range(2 * chunks):
            table = dense[:, part * LANES : (part + 1) * LANES]
            picked = jnp.where(chunk == part, lane_pick(table, within), picked)
        for shard in some:
            out_ref[shard, 0:tokens, :] = picked[(shard - first) * tokens : (shard - first + 1) * tokens].astype(BF16)
            out_ref[shard, tokens : 2 * tokens, :] = val_ref[...]


def slot_terms(first, second, values, half, got):
    parts, rows, tokens = got.shape
    cols, lat_width = second.shape
    shards = 4
    return pl.pallas_call(
        terms_kernel,
        grid=(parts // shards,),
        in_specs=[
            pl.BlockSpec((2, cols, lat_width), lambda i: (0, 0, 0)),
            pl.BlockSpec((cols, lat_width), lambda i: (0, 0)),
            pl.BlockSpec((tokens, LANES), lambda i: (0, 0)),
            pl.BlockSpec((shards, cols, tokens), lambda i: (i, 0, 0)),
            pl.BlockSpec((shards, rows, tokens), lambda i: (i, 0, 0)),
        ],
        out_specs=pl.BlockSpec((shards, 2 * tokens + cols, LANES), lambda i: (i, 0, 0)),
        out_shape=jax.ShapeDtypeStruct((parts, 2 * tokens + cols, LANES), BF16),
        scratch_shapes=[pltpu.VMEM((2 * cols, 2 * lat_width), BF16)],
        compiler_params=grant(TERMS_MIB),
        cost_estimate=cost(2 * parts * tokens * cols * 3 * lat_width, 6 << 20),
    )(first, second, values, half, got)


def total_kernel(got_ref, rank_ref, grad_ref, part_ref):
    total = jnp.sum(got_ref[...].astype(F32), axis=0)
    for dest in range(grad_ref.shape[0]):
        grad_ref[dest] = total.astype(BF16)
    turned = total.T
    slots = rank_ref.shape[1]
    for layer in range(2):
        rank = rank_ref[layer]
        part = jnp.zeros(rank.shape, F32)
        for slot in range(slots):
            row = layer * slots + slot
            part = jnp.where(rank == slot, turned[row : row + 1, :], part)
        part_ref[layer] = part.astype(BF16)


def slot_totals(got, rank):
    parts = got.shape[0]
    tokens = rank.shape[2]
    return pl.pallas_call(
        total_kernel,
        grid=(1,),
        in_specs=[
            pl.BlockSpec((parts, tokens, LANES), lambda i: (0, 0, 0)),
            pl.BlockSpec(rank.shape, lambda i: (0, 0, 0)),
        ],
        out_specs=[
            pl.BlockSpec((parts, tokens, LANES), lambda i: (0, 0, 0)),
            pl.BlockSpec(rank.shape, lambda i: (0, 0, 0)),
        ],
        out_shape=[
            jax.ShapeDtypeStruct((parts, tokens, LANES), BF16),
            jax.ShapeDtypeStruct(rank.shape, BF16),
        ],
        compiler_params=grant(),
        cost_estimate=cost(0, 1 << 20),
    )(got, rank)


FEW = ((8, 4, 2, 1), 3)
ALL = ((32, 16, 8, 4, 2, 1), 8)


def spots_kernel(got_ref, spot_ref):
    shards, _, tokens = got_ref.shape
    top = got_ref.shape[1] - tokens
    lane = lax.broadcasted_iota(jnp.int32, (tokens, LANES), 1)
    place = lane & (RUNS - 1)
    base = lane & RUNS
    last = base + (RUNS - 1)
    start = 8 * place - SHIFT

    def fill(jumps, hops):
        for shard in range(shards):
            held = got_ref[shard, top:, :].astype(F32).astype(jnp.int32)
            below = base
            for jump in jumps:
                further = below + jump
                below = jnp.where(lane_pick(held, further - 1) < start, further, below)
            codes = jnp.zeros((tokens, LANES), jnp.int32)
            for hop in range(hops):
                spot = below if hop == 0 else jnp.minimum(below + hop, last)
                ahead = lane_pick(held, spot) - start
                code = jnp.where((ahead & -8) == 0, ahead + 1, 0)
                if hop > 0:
                    code = jnp.where(below + hop <= last, code, 0)
                codes = codes | jnp.left_shift(code, 4 * hop)
            spot_ref[shard, 0:tokens, :] = below
            spot_ref[shard, tokens:, :] = codes

    deep = jnp.zeros((tokens, LANES), jnp.int32)
    for shard in range(shards):
        held = got_ref[shard, top:, :].astype(F32).astype(jnp.int32)
        ahead = pltpu.roll(held, LANES - FEW[1], 1)
        crowd = ((held >> 3) == (ahead >> 3)) & (place < RUNS - FEW[1])
        many = place == sum(FEW[0])
        deep = jnp.where((held < EMPTY) & (crowd | many), 1, deep)
    deep = jnp.max(deep)

    @pl.when(deep == 0)
    def _():
        fill(*FEW)

    @pl.when(deep != 0)
    def _():
        fill(*ALL)


def slot_spots(got):
    parts, rows, tokens = got.shape
    shards = 2
    return pl.pallas_call(
        spots_kernel,
        grid=(parts // shards,),
        in_specs=[pl.BlockSpec((shards, rows, tokens), lambda i: (i, 0, 0))],
        out_specs=pl.BlockSpec((shards, 2 * tokens, LANES), lambda i: (i, 0, 0)),
        out_shape=jax.ShapeDtypeStruct((parts, 2 * tokens, LANES), jnp.int32),
        compiler_params=grant(56),
        cost_estimate=cost(SPOTS_FLOPS, 8 << 20),
    )(got)


def dense(table, below, codes, hops):
    lane = lax.broadcasted_iota(jnp.int32, below.shape, 1)
    near = lane < RUNS
    far_codes = pltpu.roll(codes, RUNS, 1)
    kept, which = ([], []), ([], [])
    for hop in range(hops):
        spot = below if hop == 0 else jnp.minimum(below + hop, LANES - 1)
        value = lane_pick(table, spot)
        far_value = pltpu.roll(value, RUNS, 1)
        code = (codes >> (4 * hop)) & 15
        far_code = (far_codes >> (4 * hop)) & 15
        kept[0].append(jnp.where(near, value, far_value))
        kept[1].append(jnp.where(near, far_value, value))
        which[0].append(jnp.where(near, code, far_code - 1))
        which[1].append(jnp.where(near, far_code, code - 1))
    for layer in range(2):
        for chunk in range(4):
            found = jnp.zeros(below.shape, F32)
            for hop in range(hops):
                found = jnp.where(which[layer][hop] == 2 * chunk + 1, kept[layer][hop], found)
            yield layer, chunk, found.astype(BF16)


def fill_dense(table_ref, spot_ref, out_ref, halves, product):
    shards, tokens = spot_ref.shape[0], spot_ref.shape[1] // 2
    crowd = jnp.zeros((tokens, LANES), jnp.int32)
    for shard in range(shards):
        crowd = jnp.where((spot_ref[shard, tokens:, :] >> (4 * FEW[1])) != 0, 1, crowd)
    crowd = jnp.max(crowd)

    def fill(hops, shard):
        table = table_ref[shard].astype(F32)
        low = shard * tokens
        if not isinstance(shard, int):
            low = pl.multiple_of(low, tokens)
        for layer, chunk, found in dense(table, spot_ref[shard, 0:tokens, :], spot_ref[shard, tokens:, :], hops):
            at = slice((4 * layer + chunk) * LANES, (4 * layer + chunk + 1) * LANES)
            if halves and layer == 1:
                half = tokens // 2
                found = jnp.concatenate([found[half:], found[:half]], axis=0)
            out_ref[pl.ds(low, tokens), at] = found

    @pl.when(crowd == 0)
    def _():
        for shard in range(shards):
            fill(FEW[1], shard)
            if shard % 2 == 1:
                product(shard - 1)

    @pl.when(crowd != 0)
    def _():
        def one(shard, carry):
            fill(ALL[1], shard)
            return carry

        lax.fori_loop(0, shards, one, 0)
        for shard in range(0, shards, 2):
            product(shard)


def codes_kernel(got_ref, val_ref, spot_ref, first_ref, second_ref, code_ref, sum_ref):
    shards, tokens = spot_ref.shape[0], spot_ref.shape[1] // 2
    cols, lat_width = second_ref.shape
    step = pl.program_id(0)

    @pl.when(step == 0)
    def _():
        sum_ref[...] = jnp.zeros_like(sum_ref)

    def product(first):
        rows = slice(first * tokens, (first + 2) * tokens)
        cot = jnp.concatenate([got_ref[shard, 0 : 2 * cols, :] for shard in (first, first + 1)], axis=1)
        dot = functools.partial(jnp.dot, preferred_element_type=F32)
        sum_ref[0 : 2 * cols, :] += dot(cot, code_ref[rows, 0:lat_width])
        sum_ref[2 * cols : 3 * cols, :] += dot(cot[cols:], code_ref[rows, lat_width:])

    fill_dense(val_ref, spot_ref, code_ref, False, product)

    @pl.when(step == pl.num_programs(0) - 1)
    def _():
        first_ref[0] = sum_ref[0:cols, :].astype(BF16)
        first_ref[1] = sum_ref[cols : 2 * cols, :].astype(BF16)
        second_ref[...] = sum_ref[2 * cols : 3 * cols, :].astype(BF16)


def decoder_grads(got, slots, spots, cols, lat_width):
    parts, rows, tokens = got.shape
    shards = 4
    return pl.pallas_call(
        codes_kernel,
        grid=(parts // shards,),
        in_specs=[
            pl.BlockSpec((shards, rows, tokens), lambda i: (i, 0, 0)),
            pl.BlockSpec((shards, tokens, LANES), lambda i: (i, 1, 0)),
            pl.BlockSpec((shards, 2 * tokens, LANES), lambda i: (i, 0, 0)),
        ],
        out_specs=[
            pl.BlockSpec((2, cols, lat_width), lambda i: (0, 0, 0)),
            pl.BlockSpec((cols, lat_width), lambda i: (0, 0)),
        ],
        out_shape=[
            jax.ShapeDtypeStruct((2, cols, lat_width), BF16),
            jax.ShapeDtypeStruct((cols, lat_width), BF16),
        ],
        scratch_shapes=[
            pltpu.VMEM((shards * tokens, 2 * lat_width), BF16),
            pltpu.VMEM((3 * cols, lat_width), F32),
        ],
        compiler_params=grant(52),
        cost_estimate=cost(2 * parts * tokens * cols * 3 * lat_width, 8 << 20),
    )(got, slots, spots)


def back_kernel(own_ref, mine_ref, other_ref, spot_ref, grad_ref, enc_ref, back_ref, sum_ref):
    shards, tokens = spot_ref.shape[0], spot_ref.shape[1] // 2
    cols, _, lat_width = enc_ref.shape
    step = pl.program_id(0)
    @pl.when(step == 0)
    def _():
        sum_ref[...] = jnp.zeros_like(sum_ref)

    lane = lax.broadcasted_iota(jnp.int32, (cols, tokens), 1)
    mine = (lane < RUNS) == (half_of(own_ref) == 0)

    def product(first):
        rows = slice(first * tokens, (first + 2) * tokens)
        sides = ([], [])
        for shard in (first, first + 1):
            one, two = mine_ref[shard].astype(F32), other_ref[shard].astype(F32)
            sides[0].append(jnp.where(mine, one, two).astype(BF16))
            sides[1].append(jnp.where(mine, two, one).astype(BF16))
        for layer in range(2):
            sum_ref[layer * cols : (layer + 1) * cols, :] += jnp.dot(
                jnp.concatenate(sides[layer], axis=1),
                back_ref[rows, layer * lat_width : (layer + 1) * lat_width],
                preferred_element_type=F32,
            )

    fill_dense(grad_ref, spot_ref, back_ref, True, product)

    @pl.when(step == pl.num_programs(0) - 1)
    def _():
        enc_ref[:, 0, :] = sum_ref[0:cols, :].astype(BF16)
        enc_ref[:, 1, :] = sum_ref[cols:, :].astype(BF16)


def encoder_grads(own, mine, other, spots, grads, cols, lat_width):
    parts, tokens, _ = grads.shape
    shards = 4
    return pl.pallas_call(
        back_kernel,
        grid=(parts // shards,),
        in_specs=[
            pl.BlockSpec(memory_space=pltpu.SMEM),
            pl.BlockSpec((shards, cols, tokens), lambda i: (i, 0, 0)),
            pl.BlockSpec((shards, cols, tokens), lambda i: (i, 0, 0)),
            pl.BlockSpec((shards,) + spots.shape[1:], lambda i: (i, 0, 0)),
            pl.BlockSpec((shards, tokens, LANES), lambda i: (i, 0, 0)),
        ],
        out_specs=pl.BlockSpec((cols, 2, lat_width), lambda i: (0, 0, 0)),
        out_shape=jax.ShapeDtypeStruct((cols, 2, lat_width), BF16),
        scratch_shapes=[
            pltpu.VMEM((shards * tokens, 2 * lat_width), BF16),
            pltpu.VMEM((2 * cols, lat_width), F32),
        ],
        compiler_params=grant(50),
        cost_estimate=cost(2 * parts * tokens * cols * 2 * lat_width, 8 << 20),
    )(own, mine, other, spots, grads)


def exchange(array, axis):
    return lax.all_to_all(array, axis, 0, 0, tiled=True)


def from_hops(array, axis, size, hops):
    return [lax.ppermute(array, axis, [(at, at ^ hop) for at in range(size)]) for hop in hops]


def shards(layers, parts, residual, cotangent, decoder_first, decoder_second, latent_index, latent_value, active_count):
    lat_width = decoder_first.shape[0]
    cols = decoder_second.shape[1]
    tokens = residual.shape[1]
    place = lax.axis_index("layer")
    own = place.astype(jnp.int32).reshape(1)
    index, value = latent_index.transpose(0, 2, 1), latent_value.transpose(0, 2, 1)
    packed, rank = pack(lat_width, parts, own, cotangent, index, active_count)
    got = exchange(packed, "dp")
    values = slot_values(rank, value)
    half = pack_half(parts, own, residual)
    terms = slot_terms(decoder_first.transpose(1, 2, 0), decoder_second.T, values, half, got)
    slots = exchange(terms, "dp")
    spots = slot_spots(got)
    slots, spots = lax.optimization_barrier((slots, spots))
    grads, part = slot_totals(slots, rank)
    share = slots[:, 2 * tokens :, :]
    (other,) = from_hops(share, "layer", layers, (2,))
    all_grads = exchange(grads, "dp")
    first_grad, second_grad = decoder_grads(got, slots, spots, cols, lat_width)
    part = functools.reduce(jnp.add, from_hops(part, "layer", layers, (4, 8, 12)), part)
    all_grads, first_grad, part = lax.optimization_barrier((all_grads, first_grad, part))
    encoder_grad = encoder_grads(own, share, other, spots, all_grads, cols, lat_width)
    far = from_hops(part, "layer", layers, (1, 2, 3))
    *far, encoder_grad = lax.optimization_barrier((*far, encoder_grad))
    latent_grad = functools.reduce(jnp.add, far, part)
    return (
        first_grad.transpose(2, 0, 1),
        second_grad.T,
        encoder_grad,
        latent_grad.astype(F32).transpose(0, 2, 1),
    )


def solution(mesh):
    return jax.shard_map(
        functools.partial(shards, mesh.shape["layer"], mesh.shape["dp"]),
        mesh=mesh,
        in_specs=(
            P(None, "dp", None),
            P(None, "dp", None),
            P("layer", None, "dp"),
            P("layer", "dp"),
            P(None, "dp", None),
            P(None, "dp", None),
            P(None, "dp"),
        ),
        out_specs=(
            P("layer", None, "dp"),
            P("layer", "dp"),
            P("dp", None, "layer"),
            P(None, "dp", None),
        ),
        check_vma=False,
    )
```

```python
import functools
import jax
import jax.numpy as jnp
from jax import lax
from jax.experimental import pallas as pl
from jax.experimental.pallas import tpu as pltpu
from jax.sharding import PartitionSpec as P

BF16 = jnp.bfloat16
F32 = jnp.float32
LANES = 128
RUNS = LANES // 2
SHIFT = 256
EMPTY = 512
STREAM_MIB = 60
KERNEL_MIB = 16
TERMS_MIB = 56
SPOTS_FLOPS = 1 << 32


def grant(mib=KERNEL_MIB):
    return pltpu.CompilerParams(vmem_limit_bytes=mib << 20)


def cost(flops, moved):
    return pl.CostEstimate(flops=flops, bytes_accessed=moved, transcendentals=0)


def lane_pick(table, where):
    return jnp.take_along_axis(table, where, axis=1, mode="promise_in_bounds")


def turn(source, out_ref, base):
    dests = out_ref.shape[0]
    cols = source.shape[1] // dests
    turned = source.T
    for dest in range(dests):
        out_ref[dest, base : base + cols, :] = turned[dest * cols : (dest + 1) * cols]


def kept_slots(own_ref, idx_ref, live_ref, layer, lat_width):
    slots, tokens = idx_ref.shape[1:]
    place = lax.broadcasted_iota(jnp.int32, (slots, tokens), 0)
    local = idx_ref[layer] - own_ref[0] * lat_width
    inside = (place < live_ref[layer : layer + 1, :]) & (local >= 0) & (local < lat_width)
    return place, local, inside


def pack_kernel(lat_width, own_ref, cot_ref, idx_ref, live_ref, out_ref, rank_ref, slot_ref):
    slots, tokens = idx_ref.shape[1:]
    dests = out_ref.shape[0]
    cols = cot_ref.shape[2] // dests

    @pl.when(pl.program_id(0) == 0)
    def _():
        found = []
        for layer in range(2):
            place, local, inside = kept_slots(own_ref, idx_ref, live_ref, layer, lat_width)
            key = (local & (RUNS - 1)) * 8 + (local >> 6)
            held_key = key - SHIFT
            key = jnp.where(inside, key, 1 << 20)
            rank = jnp.zeros((slots, tokens), jnp.int32)
            for slot in range(slots):
                rank = rank + jnp.where(key[slot : slot + 1, :] < key, 1, 0)
            rank = jnp.where(inside, rank, slots)
            rank_ref[layer] = rank
            held = jnp.full((slots, tokens), EMPTY, jnp.int32)
            for slot in range(slots):
                held = jnp.where(rank[slot : slot + 1, :] == place, held_key[slot : slot + 1, :], held)
            found.append(held.astype(F32))
        slot_ref[...] = jnp.concatenate(found, axis=0).T.astype(BF16)

    for layer in range(2):
        turn(cot_ref[layer], out_ref, layer * cols)
    for dest in range(dests):
        out_ref[dest, 2 * cols :, :] = slot_ref[...]


def pack(lat_width, parts, start, cotangent, index, live):
    _, tokens, width = cotangent.shape
    slots = index.shape[1]
    steps = 4
    rows = 2 * (width // parts) + tokens
    return pl.pallas_call(
        functools.partial(pack_kernel, lat_width),
        grid_spec=pltpu.PrefetchScalarGridSpec(
            num_scalar_prefetch=1,
            grid=(steps,),
            in_specs=[
                pl.BlockSpec((2, tokens, width // steps), lambda i, own: (0, 0, i)),
                pl.BlockSpec((2, slots, tokens), lambda i, own: (0, 0, 0)),
                pl.BlockSpec((2, tokens), lambda i, own: (0, 0)),
            ],
            out_specs=[
                pl.BlockSpec((parts // steps, rows, tokens), lambda i, own: (i, 0, 0)),
                pl.BlockSpec((2, slots, tokens), lambda i, own: (0, 0, 0)),
            ],
            scratch_shapes=[pltpu.VMEM((tokens, LANES), BF16)],
        ),
        out_shape=[
            jax.ShapeDtypeStruct((parts, rows, tokens), BF16),
            jax.ShapeDtypeStruct((2, slots, tokens), jnp.int32),
        ],
        compiler_params=grant(STREAM_MIB),
        cost_estimate=cost(0, 5 << 20),
    )(start, cotangent, index, live)


def half_of(own):
    return (own[0] >> 1) & 1


def half_kernel(own_ref, res_ref, out_ref):
    side = half_of(own_ref)
    turn(jnp.concatenate([res_ref[side], res_ref[1 - side]], axis=0), out_ref, 0)


def pack_half(parts, own, residual):
    _, tokens, width = residual.shape
    steps = 4
    share = tokens // 2
    return pl.pallas_call(
        half_kernel,
        grid_spec=pltpu.PrefetchScalarGridSpec(
            num_scalar_prefetch=1,
            grid=(steps,),
            in_specs=[pl.BlockSpec((2, share, width // steps), lambda i, own: (0, half_of(own), i))],
            out_specs=pl.BlockSpec((parts // steps, width // parts, tokens), lambda i, own: (i, 0, 0)),
        ),
        out_shape=jax.ShapeDtypeStruct((parts, width // parts, tokens), BF16),
        compiler_params=grant(62),
        cost_estimate=cost(0, 2 << 20),
    )(own, residual)


def values_kernel(rank_ref, val_ref, out_ref):
    slots, tokens = val_ref.shape[1:]
    place = lax.broadcasted_iota(jnp.int32, (slots, tokens), 0)
    codes = []
    for layer in range(2):
        rank = rank_ref[layer]
        value = val_ref[layer].astype(F32)
        code = jnp.zeros((slots, tokens), F32)
        for slot in range(slots):
            code = jnp.where(rank[slot : slot + 1, :] == place, value[slot : slot + 1, :], code)
        codes.append(code)
    out_ref[...] = jnp.concatenate(codes, axis=0).T.astype(BF16)


def slot_values(rank, value):
    return pl.pallas_call(
        values_kernel,
        out_shape=jax.ShapeDtypeStruct((value.shape[2], LANES), BF16),
        compiler_params=grant(62),
        cost_estimate=cost(0, 1 << 20),
    )(rank, value)


def terms_kernel(wf_ref, ws_ref, val_ref, half_ref, got_ref, out_ref, weight_ref):
    shards, _, tokens = got_ref.shape
    cols, lat_width = ws_ref.shape

    @pl.when(pl.program_id(0) == 0)
    def _():
        weight_ref[0:cols, :] = wf_ref[0]
        weight_ref[cols : 2 * cols, :] = wf_ref[1]

    out_ref[:, 2 * tokens :, :] = half_ref[...]
    pair = 2
    for first in range(0, shards, pair):
        some = range(first, first + pair)
        cot = jnp.concatenate([got_ref[shard, 0 : 2 * cols, :] for shard in some], axis=1)
        dot = functools.partial(jnp.dot, preferred_element_type=F32)
        dense = (dot(cot.T, weight_ref[...]), dot(cot[cols:].T, ws_ref[...]))
        held = jnp.concatenate([got_ref[shard, 2 * cols :, :] for shard in some], axis=0)
        held = held.astype(F32).astype(jnp.int32) + SHIFT
        lane = lax.broadcasted_iota(jnp.int32, held.shape, 1)
        chunks = lat_width // LANES
        chunk = ((held & 7) >> 1) + jnp.where(lane >= RUNS, chunks, 0)
        chunk = jnp.where(held < lat_width, chunk, 2 * chunks)
        within = jnp.where((held & 1) == 1, RUNS, 0) + (held >> 3)
        picked = jnp.zeros(held.shape, F32)
        for part in range(2 * chunks):
            table = dense[part // chunks][:, part % chunks * LANES : (part % chunks + 1) * LANES]
            picked = jnp.where(chunk == part, lane_pick(table, within), picked)
        for shard in some:
            out_ref[shard, 0:tokens, :] = picked[(shard - first) * tokens : (shard - first + 1) * tokens].astype(BF16)
            out_ref[shard, tokens : 2 * tokens, :] = val_ref[...]


def slot_terms(first, second, values, half, got):
    parts, rows, tokens = got.shape
    cols, lat_width = second.shape
    shards = 4
    return pl.pallas_call(
        terms_kernel,
        grid=(parts // shards,),
        in_specs=[
            pl.BlockSpec((2, cols, lat_width), lambda i: (0, 0, 0)),
            pl.BlockSpec((cols, lat_width), lambda i: (0, 0)),
            pl.BlockSpec((tokens, LANES), lambda i: (0, 0)),
            pl.BlockSpec((shards, cols, tokens), lambda i: (i, 0, 0)),
            pl.BlockSpec((shards, rows, tokens), lambda i: (i, 0, 0)),
        ],
        out_specs=pl.BlockSpec((shards, 2 * tokens + cols, LANES), lambda i: (i, 0, 0)),
        out_shape=jax.ShapeDtypeStruct((parts, 2 * tokens + cols, LANES), BF16),
        scratch_shapes=[pltpu.VMEM((2 * cols, lat_width), BF16)],
        compiler_params=grant(TERMS_MIB),
        cost_estimate=cost(2 * parts * tokens * cols * 3 * lat_width, 6 << 20),
    )(first, second, values, half, got)


def total_kernel(got_ref, rank_ref, grad_ref, part_ref):
    total = jnp.sum(got_ref[...].astype(F32), axis=0)
    for dest in range(grad_ref.shape[0]):
        grad_ref[dest] = total.astype(BF16)
    turned = total.T
    slots = rank_ref.shape[1]
    for layer in range(2):
        rank = rank_ref[layer]
        part = jnp.zeros(rank.shape, F32)
        for slot in range(slots):
            row = layer * slots + slot
            part = jnp.where(rank == slot, turned[row : row + 1, :], part)
        part_ref[layer] = part.astype(BF16)


def slot_totals(got, rank):
    parts = got.shape[0]
    tokens = rank.shape[2]
    return pl.pallas_call(
        total_kernel,
        grid=(1,),
        in_specs=[
            pl.BlockSpec((parts, tokens, LANES), lambda i: (0, 0, 0)),
            pl.BlockSpec(rank.shape, lambda i: (0, 0, 0)),
        ],
        out_specs=[
            pl.BlockSpec((parts, tokens, LANES), lambda i: (0, 0, 0)),
            pl.BlockSpec(rank.shape, lambda i: (0, 0, 0)),
        ],
        out_shape=[
            jax.ShapeDtypeStruct((parts, tokens, LANES), BF16),
            jax.ShapeDtypeStruct(rank.shape, BF16),
        ],
        compiler_params=grant(),
        cost_estimate=cost(0, 1 << 20),
    )(got, rank)


FEW = ((8, 4, 2, 1), 3)
ALL = ((32, 16, 8, 4, 2, 1), 8)


def spots_kernel(got_ref, spot_ref):
    shards, _, tokens = got_ref.shape
    top = got_ref.shape[1] - tokens
    lane = lax.broadcasted_iota(jnp.int32, (tokens, LANES), 1)
    place = lane & (RUNS - 1)
    base = lane & RUNS
    last = base + (RUNS - 1)
    start = 8 * place - SHIFT

    def fill(jumps, hops):
        for shard in range(shards):
            held = got_ref[shard, top:, :].astype(F32).astype(jnp.int32)
            below = base
            for jump in jumps:
                further = below + jump
                below = jnp.where(lane_pick(held, further - 1) < start, further, below)
            codes = jnp.zeros((tokens, LANES), jnp.int32)
            for hop in range(hops):
                spot = below if hop == 0 else jnp.minimum(below + hop, last)
                ahead = lane_pick(held, spot) - start
                code = jnp.where((ahead & -8) == 0, ahead + 1, 0)
                if hop > 0:
                    code = jnp.where(below + hop <= last, code, 0)
                codes = codes | jnp.left_shift(code, 4 * hop)
            spot_ref[shard, 0:tokens, :] = below
            spot_ref[shard, tokens:, :] = codes

    deep = jnp.zeros((tokens, LANES), jnp.int32)
    for shard in range(shards):
        held = got_ref[shard, top:, :].astype(F32).astype(jnp.int32)
        ahead = pltpu.roll(held, LANES - FEW[1], 1)
        crowd = ((held >> 3) == (ahead >> 3)) & (place < RUNS - FEW[1])
        many = place == sum(FEW[0])
        deep = jnp.where((held < EMPTY) & (crowd | many), 1, deep)
    deep = jnp.max(deep)

    @pl.when(deep == 0)
    def _():
        fill(*FEW)

    @pl.when(deep != 0)
    def _():
        fill(*ALL)


def slot_spots(got):
    parts, rows, tokens = got.shape
    shards = 2
    return pl.pallas_call(
        spots_kernel,
        grid=(parts // shards,),
        in_specs=[pl.BlockSpec((shards, rows, tokens), lambda i: (i, 0, 0))],
        out_specs=pl.BlockSpec((shards, 2 * tokens, LANES), lambda i: (i, 0, 0)),
        out_shape=jax.ShapeDtypeStruct((parts, 2 * tokens, LANES), jnp.int32),
        compiler_params=grant(56),
        cost_estimate=cost(SPOTS_FLOPS, 8 << 20),
    )(got)


def dense(table, below, codes, hops):
    lane = lax.broadcasted_iota(jnp.int32, below.shape, 1)
    near = lane < RUNS
    far_codes = pltpu.roll(codes, RUNS, 1)
    kept, which = ([], []), ([], [])
    for hop in range(hops):
        spot = below if hop == 0 else jnp.minimum(below + hop, LANES - 1)
        value = lane_pick(table, spot)
        far_value = pltpu.roll(value, RUNS, 1)
        code = (codes >> (4 * hop)) & 15
        far_code = (far_codes >> (4 * hop)) & 15
        kept[0].append(jnp.where(near, value, far_value))
        kept[1].append(jnp.where(near, far_value, value))
        which[0].append(jnp.where(near, code, far_code - 1))
        which[1].append(jnp.where(near, far_code, code - 1))
    for layer in range(2):
        for chunk in range(4):
            found = jnp.zeros(below.shape, F32)
            for hop in range(hops):
                found = jnp.where(which[layer][hop] == 2 * chunk + 1, kept[layer][hop], found)
            yield layer, chunk, found.astype(BF16)


def fill_dense(table_ref, spot_ref, out_ref, halves, product):
    shards, tokens = spot_ref.shape[0], spot_ref.shape[1] // 2
    crowd = jnp.zeros((tokens, LANES), jnp.int32)
    for shard in range(shards):
        crowd = jnp.where((spot_ref[shard, tokens:, :] >> (4 * FEW[1])) != 0, 1, crowd)
    crowd = jnp.max(crowd)

    def fill(hops, shard):
        table = table_ref[shard].astype(F32)
        low = shard * tokens
        if not isinstance(shard, int):
            low = pl.multiple_of(low, tokens)
        for layer, chunk, found in dense(table, spot_ref[shard, 0:tokens, :], spot_ref[shard, tokens:, :], hops):
            at = slice((4 * layer + chunk) * LANES, (4 * layer + chunk + 1) * LANES)
            if halves and layer == 1:
                half = tokens // 2
                found = jnp.concatenate([found[half:], found[:half]], axis=0)
            out_ref[pl.ds(low, tokens), at] = found

    @pl.when(crowd == 0)
    def _():
        for shard in range(shards):
            fill(FEW[1], shard)
            if shard % 2 == 1:
                product(shard - 1)

    @pl.when(crowd != 0)
    def _():
        def one(shard, carry):
            fill(ALL[1], shard)
            return carry

        lax.fori_loop(0, shards, one, 0)
        for shard in range(0, shards, 2):
            product(shard)


def codes_kernel(got_ref, val_ref, spot_ref, first_ref, second_ref, code_ref, sum_ref):
    shards, tokens = spot_ref.shape[0], spot_ref.shape[1] // 2
    cols, lat_width = second_ref.shape
    step = pl.program_id(0)

    @pl.when(step == 0)
    def _():
        sum_ref[...] = jnp.zeros_like(sum_ref)

    def product(first):
        rows = slice(first * tokens, (first + 2) * tokens)
        cot = jnp.concatenate([got_ref[shard, 0 : 2 * cols, :] for shard in (first, first + 1)], axis=1)
        dot = functools.partial(jnp.dot, preferred_element_type=F32)
        sum_ref[0 : 2 * cols, :] += dot(cot, code_ref[rows, 0:lat_width])
        sum_ref[2 * cols : 3 * cols, :] += dot(cot[cols:], code_ref[rows, lat_width:])

    fill_dense(val_ref, spot_ref, code_ref, False, product)

    @pl.when(step == pl.num_programs(0) - 1)
    def _():
        first_ref[0] = sum_ref[0:cols, :].astype(BF16)
        first_ref[1] = sum_ref[cols : 2 * cols, :].astype(BF16)
        second_ref[...] = sum_ref[2 * cols : 3 * cols, :].astype(BF16)


def decoder_grads(got, slots, spots, cols, lat_width):
    parts, rows, tokens = got.shape
    shards = 4
    return pl.pallas_call(
        codes_kernel,
        grid=(parts // shards,),
        in_specs=[
            pl.BlockSpec((shards, rows, tokens), lambda i: (i, 0, 0)),
            pl.BlockSpec((shards, tokens, LANES), lambda i: (i, 1, 0)),
            pl.BlockSpec((shards, 2 * tokens, LANES), lambda i: (i, 0, 0)),
        ],
        out_specs=[
            pl.BlockSpec((2, cols, lat_width), lambda i: (0, 0, 0)),
            pl.BlockSpec((cols, lat_width), lambda i: (0, 0)),
        ],
        out_shape=[
            jax.ShapeDtypeStruct((2, cols, lat_width), BF16),
            jax.ShapeDtypeStruct((cols, lat_width), BF16),
        ],
        scratch_shapes=[
            pltpu.VMEM((shards * tokens, 2 * lat_width), BF16),
            pltpu.VMEM((3 * cols, lat_width), F32),
        ],
        compiler_params=grant(52),
        cost_estimate=cost(2 * parts * tokens * cols * 3 * lat_width, 8 << 20),
    )(got, slots, spots)


def back_kernel(own_ref, mine_ref, other_ref, spot_ref, grad_ref, enc_ref, back_ref, sum_ref):
    shards, tokens = spot_ref.shape[0], spot_ref.shape[1] // 2
    cols, _, lat_width = enc_ref.shape
    step = pl.program_id(0)
    @pl.when(step == 0)
    def _():
        sum_ref[...] = jnp.zeros_like(sum_ref)

    lane = lax.broadcasted_iota(jnp.int32, (cols, tokens), 1)
    mine = (lane < RUNS) == (half_of(own_ref) == 0)

    def product(first):
        rows = slice(first * tokens, (first + 2) * tokens)
        sides = ([], [])
        for shard in (first, first + 1):
            one, two = mine_ref[shard].astype(F32), other_ref[shard].astype(F32)
            sides[0].append(jnp.where(mine, one, two).astype(BF16))
            sides[1].append(jnp.where(mine, two, one).astype(BF16))
        for layer in range(2):
            sum_ref[layer * cols : (layer + 1) * cols, :] += jnp.dot(
                jnp.concatenate(sides[layer], axis=1),
                back_ref[rows, layer * lat_width : (layer + 1) * lat_width],
                preferred_element_type=F32,
            )

    fill_dense(grad_ref, spot_ref, back_ref, True, product)

    @pl.when(step == pl.num_programs(0) - 1)
    def _():
        enc_ref[:, 0, :] = sum_ref[0:cols, :].astype(BF16)
        enc_ref[:, 1, :] = sum_ref[cols:, :].astype(BF16)


def encoder_grads(own, mine, other, spots, grads, cols, lat_width):
    parts, tokens, _ = grads.shape
    shards = 4
    return pl.pallas_call(
        back_kernel,
        grid=(parts // shards,),
        in_specs=[
            pl.BlockSpec(memory_space=pltpu.SMEM),
            pl.BlockSpec((shards, cols, tokens), lambda i: (i, 0, 0)),
            pl.BlockSpec((shards, cols, tokens), lambda i: (i, 0, 0)),
            pl.BlockSpec((shards,) + spots.shape[1:], lambda i: (i, 0, 0)),
            pl.BlockSpec((shards, tokens, LANES), lambda i: (i, 0, 0)),
        ],
        out_specs=pl.BlockSpec((cols, 2, lat_width), lambda i: (0, 0, 0)),
        out_shape=jax.ShapeDtypeStruct((cols, 2, lat_width), BF16),
        scratch_shapes=[
            pltpu.VMEM((shards * tokens, 2 * lat_width), BF16),
            pltpu.VMEM((2 * cols, lat_width), F32),
        ],
        compiler_params=grant(50),
        cost_estimate=cost(2 * parts * tokens * cols * 2 * lat_width, 8 << 20),
    )(own, mine, other, spots, grads)


def exchange(array, axis):
    return lax.all_to_all(array, axis, 0, 0, tiled=True)


def from_hops(array, axis, size, hops):
    return [lax.ppermute(array, axis, [(at, at ^ hop) for at in range(size)]) for hop in hops]


def shards(layers, parts, residual, cotangent, decoder_first, decoder_second, latent_index, latent_value, active_count):
    lat_width = decoder_first.shape[0]
    cols = decoder_second.shape[1]
    tokens = residual.shape[1]
    place = lax.axis_index("layer")
    own = place.astype(jnp.int32).reshape(1)
    index, value = latent_index.transpose(0, 2, 1), latent_value.transpose(0, 2, 1)
    packed, rank = pack(lat_width, parts, own, cotangent, index, active_count)
    got = exchange(packed, "dp")
    values = slot_values(rank, value)
    half = pack_half(parts, own, residual)
    terms = slot_terms(decoder_first.transpose(1, 2, 0), decoder_second.T, values, half, got)
    slots = exchange(terms, "dp")
    spots = slot_spots(got)
    slots, spots = lax.optimization_barrier((slots, spots))
    grads, part = slot_totals(slots, rank)
    share = slots[:, 2 * tokens :, :]
    (other,) = from_hops(share, "layer", layers, (2,))
    all_grads = exchange(grads, "dp")
    first_grad, second_grad = decoder_grads(got, slots, spots, cols, lat_width)
    part = functools.reduce(jnp.add, from_hops(part, "layer", layers, (1, 2, 3)), part)
    all_grads, first_grad, part = lax.optimization_barrier((all_grads, first_grad, part))
    encoder_grad = encoder_grads(own, share, other, spots, all_grads, cols, lat_width)
    far = from_hops(part, "layer", layers, (4, 8, 12))
    *far, encoder_grad = lax.optimization_barrier((*far, encoder_grad))
    latent_grad = functools.reduce(jnp.add, far, part)
    return (
        first_grad.transpose(2, 0, 1),
        second_grad.T,
        encoder_grad,
        latent_grad.astype(F32).transpose(0, 2, 1),
    )


def solution(mesh):
    return jax.shard_map(
        functools.partial(shards, mesh.shape["layer"], mesh.shape["dp"]),
        mesh=mesh,
        in_specs=(
            P(None, "dp", None),
            P(None, "dp", None),
            P("layer", None, "dp"),
            P("layer", "dp"),
            P(None, "dp", None),
            P(None, "dp", None),
            P(None, "dp"),
        ),
        out_specs=(
            P("layer", None, "dp"),
            P("layer", "dp"),
            P("dp", None, "layer"),
            P(None, "dp", None),
        ),
        check_vma=False,
    )
```
